32 devices in a mesh: tiles: 16 (over z, x, core), vec: 2 (over y).
Axes of the slice: x: 2, y: 2, z: 4, core: 2. Of those that a mesh axis runs over, the one named last changes fastest.
Arguments:
- omega: float32 [128, 4, 128, 128], P('vec', None, 'tiles'), may hold values from -24 to 24
- conductance: float32 [3, 4, 128, 128], P(None, None, 'tiles'), may hold values from 0.02 to 0.16
- wet: int32 [128, 128], P('tiles'), may hold values 0 or 1
- volume: float32 [128, 128], P('tiles'), may hold values from 0.3 to 27, as said below
- face_runs: int32 [16, 4], P('tiles'), may hold values from 0 to 128, as said below
Outputs:
- diffused: float32 [128, 4, 128, 128], P('vec', None, 'tiles')
- r_factor: float32 [128, 128], replicated
The draws below stay inside these ranges and needn't reach their ends.
Inputs may be any that keep to these rules, and one draw needn't show every extreme that they name: `face_runs`: tiles in tile row 0 have a closed lower row face and tiles in tile column 0 a closed lower column face (length 0); every other run lies within its face, covers at least half of it, and some tiles have fully open faces. Positive cell volume weights.
All inputs are finite; a program needn't handle non-finite values. No bound on the sum of `wet` on one device may be relied on, other than what follows from the above.
Results may differ from the reference program's by a relative error of at most 0.00005.
Values sent between devices are 32-bit elements; how exact they have to be, the bound alone decides.
No kernel may reach another device: no remote copies, remote signals or barrier semaphores. Data moves between devices by JAX's collectives and lax.ppermute only.
A program may use at most 64 MiB of HBM per device.

```python
import math
import jax
import jax.numpy as jnp
from jax import lax

VECS = 128
TGY = 8
ITERS = 4
LEV = 4
TX = 8
TY = 128
TILES = 16
TGX = 2


def draw_omega(key, part):
    first, second = jax.random.split(jax.random.fold_in(key, 11), 2)
    shape = (VECS, LEV, TILES * TX, TY)
    common_shape = (1, LEV, TILES * TX, TY)
    own = jax.random.normal(first, shape, jnp.float32)
    common = jax.random.normal(second, common_shape, jnp.float32)
    values = jnp.clip((own + 0.5 * common) / math.sqrt(1.25), -8.0, 8.0)
    return values.astype(jnp.float32)


def draw_volume(key, part):
    tile_of_row = (jnp.arange(TILES * TX) // TX).astype(jnp.float32)
    ramp = 1.0 + 2.0 * tile_of_row / (TILES - 1)
    rough = jnp.exp(jax.random.uniform(jax.random.fold_in(key, 22), (TILES * TX, TY), jnp.float32, math.log(0.5), math.log(2.0)))
    values = ramp[:, None] * rough
    return values.astype(jnp.float32)


def draw_face_runs(key, part):
    first, second, third, fourth = jax.random.split(jax.random.fold_in(key, 31), 4)
    tile_ids = jnp.arange(TILES, dtype=jnp.int32)
    tile_row = tile_ids // TGY
    tile_col = tile_ids % TGY
    length_x = jax.random.randint(first, (TILES,), TY // 2, TY + 1, dtype=jnp.int32)
    length_x = jnp.where(tile_ids % 3 == 0, TY, length_x)
    length_x = jnp.where(tile_row == 0, 0, length_x)
    start_x = jax.random.randint(second, (TILES,), 0, 1 << 20, dtype=jnp.int32) % (TY - length_x + 1)
    length_y = jax.random.randint(third, (TILES,), TX // 2, TX + 1, dtype=jnp.int32)
    length_y = jnp.where(tile_ids % 3 == 1, TX, length_y)
    length_y = jnp.where(tile_col == 0, 0, length_y)
    start_y = jax.random.randint(fourth, (TILES,), 0, 1 << 20, dtype=jnp.int32) % (TX - length_y + 1)
    return jnp.stack([start_x, length_x, start_y, length_y], axis=1).astype(jnp.int32)


def place_ends(entries, own_key, low, high):
    index_at = [jax.random.randint(jax.random.fold_in(own_key, axis), (), 0, length) for axis, length in enumerate(entries.shape)]
    longest = entries.shape.index(max(entries.shape))
    neighbour = index_at[:longest] + [(index_at[longest] + 1) % entries.shape[longest]] + index_at[longest + 1:]
    return entries.at[tuple(index_at)].set(low).at[tuple(neighbour)].set(high)


def block_levels(key, shape, cuts, low, top_value):
    gain = 1.0
    for axis_at, parts in cuts:
        draws = jax.random.uniform(jax.random.fold_in(jax.random.fold_in(key, 6), axis_at), (parts,), jnp.float32, low / len(cuts), top_value / len(cuts))
        gain = gain * jnp.repeat(jnp.exp(draws), shape[axis_at] // parts).reshape((-1,) + (1,) * (len(shape) - 1 - axis_at))
    return gain


def setup_inputs(seed: int = 0) -> dict:
    splits = jax.random.split(jax.random.key(seed), 6)
    omega = draw_omega(jax.random.fold_in(splits[5], 71), 0)
    conductance = jnp.clip(jnp.exp(math.log(0.16) - 2.0794415 * jax.random.uniform(splits[1], (3, LEV, TILES * TX, TY), jnp.float32) ** block_levels(splits[1], (3, LEV, TILES * TX, TY), ((2, 16),), -0.2, 0.2)), 0.02, 0.16)
    wet = place_ends((jax.random.randint(splits[2], (TILES * TX, TY), 0, 8) < 7).astype(jnp.int32), jax.random.fold_in(splits[2], 1), 0, 1)
    volume = draw_volume(jax.random.fold_in(splits[5], 71), 0)
    face_runs = draw_face_runs(jax.random.fold_in(splits[5], 71), 0)
    return dict(omega=omega, conductance=conductance, wet=wet, volume=volume, face_runs=face_runs)


def diffuse(field, statics):
    cond_x = statics[0]
    cond_y = statics[1]
    cond_z = statics[2]
    wet_cells = statics[3]
    flux_x = cond_x[:, 1:, :] * (field[:, :, 1:, :] - field[:, :, :-1, :])
    flux_y = cond_y[:, :, 1:] * (field[:, :, :, 1:] - field[:, :, :, :-1])
    flux_z = cond_z[1:] * (field[:, 1:] - field[:, :-1])
    zero_level = jnp.zeros_like(field[:, :1])
    flux_z = jnp.concatenate([zero_level, flux_z, zero_level], axis=1)
    change = flux_x[:, :, 1:, 1:-1] - flux_x[:, :, :-1, 1:-1]
    change = change + flux_y[:, :, 1:-1, 1:] - flux_y[:, :, 1:-1, :-1]
    change = change + (flux_z[:, 1:] - flux_z[:, :-1])[:, :, 1:-1, 1:-1]
    return wet_cells[:, 1:-1, 1:-1] * (field[:, :, 1:-1, 1:-1] + change)

def to_grid(array):
    leading = array.shape[:-2]
    shaped = array.reshape(leading + (TGX, TGY, TX, TY))
    shaped = jnp.moveaxis(shaped, -2, -3)
    return shaped.reshape(leading + (TGX * TX, TGY * TY))

def to_tiles(array):
    leading = array.shape[:-2]
    shaped = array.reshape(leading + (TGX, TX, TGY, TY))
    shaped = jnp.moveaxis(shaped, -3, -2)
    return shaped.reshape(leading + (TGX * TGY * TX, TY))

def reference(omega, conductance, wet, volume, face_runs):
    row_ids = jnp.arange(TILES * TX, dtype=jnp.int32)
    rows_in = row_ids % TX
    runs = jnp.repeat(face_runs, TX, axis=0)
    col_ids = jnp.arange(TY, dtype=jnp.int32)
    open_x = (col_ids[None, :] >= runs[:, 0:1]) & (col_ids[None, :] < runs[:, 0:1] + runs[:, 1:2])
    factor_x = jnp.where(rows_in[:, None] == 0, open_x.astype(jnp.float32), jnp.float32(1.0))
    open_y = (rows_in >= runs[:, 2]) & (rows_in < runs[:, 2] + runs[:, 3])
    factor_y = jnp.where(col_ids[None, :] == 0, open_y[:, None].astype(jnp.float32), jnp.float32(1.0))
    level_ids = jnp.arange(LEV, dtype=jnp.int32)
    cond_z = conductance[2] * (level_ids > 0).astype(jnp.float32)[:, None, None]
    wet_float = wet.astype(jnp.float32)
    statics = jnp.stack([conductance[0] * factor_x[None], conductance[1] * factor_y[None], cond_z, jnp.broadcast_to(wet_float[None], (LEV, TILES * TX, TY))])
    statics_grid = jnp.pad(to_grid(statics), ((0, 0), (0, 0), (1, 1), (1, 1)))
    start = wet_float[None, None] * omega

    def run_block(block):
        field = to_grid(block)
        for sweep_index in range(ITERS):
            padded = jnp.pad(field, ((0, 0), (0, 0), (1, 1), (1, 1)))
            field = diffuse(padded, statics_grid)
        return to_tiles(field)
    blocks = start.reshape(VECS // 16, 16, LEV, TILES * TX, TY)
    diffused = lax.map(run_block, blocks).reshape(VECS, LEV, TILES * TX, TY)
    total_cells = LEV * TILES * TX * TY
    flat_values = diffused.reshape(VECS, -1)
    weighted = (diffused * volume[None, None]).reshape(VECS, -1)
    gram = lax.dot_general(weighted.astype(jnp.float32), flat_values.astype(jnp.float32), (((1,), (1,)), ((), ())), precision=lax.Precision.HIGHEST, preferred_element_type=jnp.float32) / total_cells
    r_factor = jnp.linalg.cholesky(gram).T
    return (diffused, r_factor)
```

```python
import functools
import jax
import jax.numpy as jnp
from jax import lax
from jax.experimental import pallas as pl
from jax.experimental.pallas import tpu as pltpu
from jax.sharding import PartitionSpec as P

TGY = 8
ITERS = 4


def shifted(value, axis, steps):
    count = lax.axis_size(axis)
    first, last = (max(0, -steps), min(count, count - steps))
    return lax.ppermute(value, axis, [(source, source + steps) for source in range(first, last)])


def diffuse(field, statics):
    cond_x = statics[0]
    cond_y = statics[1]
    cond_z = statics[2]
    wet_cells = statics[3]
    flux_x = cond_x[:, 1:, :] * (field[:, :, 1:, :] - field[:, :, :-1, :])
    flux_y = cond_y[:, :, 1:] * (field[:, :, :, 1:] - field[:, :, :, :-1])
    flux_z = cond_z[1:] * (field[:, 1:] - field[:, :-1])
    zero_level = jnp.zeros_like(field[:, :1])
    flux_z = jnp.concatenate([zero_level, flux_z, zero_level], axis=1)
    change = flux_x[:, :, 1:, 1:-1] - flux_x[:, :, :-1, 1:-1]
    change = change + flux_y[:, :, 1:-1, 1:] - flux_y[:, :, 1:-1, :-1]
    change = change + (flux_z[:, 1:] - flux_z[:, :-1])[:, :, 1:-1, 1:-1]
    return wet_cells[:, 1:-1, 1:-1] * (field[:, :, 1:-1, 1:-1] + change)


def moving(values, offset):
    return shifted(values, "tiles", offset)


def fixed_rim(values, offset):
    return shifted(values, "tiles", offset)


def extend(values, margin, neighbour):
    lower_rim = neighbour(values[:, :, -margin:, :], TGY)
    upper_rim = neighbour(values[:, :, :margin, :], -TGY)
    stacked = jnp.concatenate([lower_rim, values, upper_rim], axis=2)
    left_rim = neighbour(stacked[:, :, :, -margin:], 1)
    right_rim = neighbour(stacked[:, :, :, :margin], -1)
    return jnp.concatenate([left_rim, stacked, right_rim], axis=3)


def swapped(value, axis, bit):
    count = lax.axis_size(axis)
    return lax.ppermute(value, axis, [(source, source ^ bit) for source in range(count)])


def total_over_mesh(value):
    for axis in ("tiles", "vec"):
        bit = 1
        while bit < lax.axis_size(axis):
            value = value + swapped(value, axis, bit)
            bit *= 2
    return value


def factor_kernel(scale, gram_ref, out_ref):
    order = gram_ref.shape[0]
    height = 8
    count = order // height
    blocks = [gram_ref[height * b : height * (b + 1), :] * scale for b in range(count)]
    row_ids = lax.broadcasted_iota(jnp.int32, (height, order), 0)
    col_ids = lax.broadcasted_iota(jnp.int32, (height, order), 1)
    for p in range(count):
        rows = jnp.zeros((height, order), jnp.float32)
        for j in range(height):
            k = height * p + j
            current = blocks[p]
            inverse = jnp.broadcast_to(lax.rsqrt(current[j : j + 1, k : k + 1]), (height, order))
            pivot_row = jnp.broadcast_to(current[j : j + 1, :], (height, order)) * inverse
            rows = jnp.where((row_ids == j) & (col_ids >= k), pivot_row, rows)
            for q in range(p, count):
                pivot_col = jnp.broadcast_to(blocks[q][:, k : k + 1], (height, order)) * inverse
                blocks[q] = blocks[q] - pivot_col * pivot_row
        out_ref[height * p : height * (p + 1), :] = rows


def factor(gram, scale):
    return pl.pallas_call(
        functools.partial(factor_kernel, scale),
        out_shape=jax.ShapeDtypeStruct(gram.shape, jnp.float32),
        in_specs=[pl.BlockSpec(memory_space=pltpu.VMEM)],
        out_specs=pl.BlockSpec(memory_space=pltpu.VMEM),
    )(gram)


def shards(omega, conductance, wet, volume, face_runs):
    levels = omega.shape[1]
    tile_rows = omega.shape[2]
    tile_cols = omega.shape[3]
    row_ids = lax.broadcasted_iota(jnp.int32, (tile_rows, tile_cols), 0)
    col_ids = lax.broadcasted_iota(jnp.int32, (tile_rows, tile_cols), 1)
    runs = face_runs[0]
    open_x = (col_ids >= runs[0]) & (col_ids < runs[0] + runs[1])
    factor_x = jnp.where(row_ids == 0, open_x.astype(jnp.float32), jnp.float32(1.0))
    open_y = (row_ids >= runs[2]) & (row_ids < runs[2] + runs[3])
    factor_y = jnp.where(col_ids == 0, open_y.astype(jnp.float32), jnp.float32(1.0))
    level_ids = lax.broadcasted_iota(jnp.int32, (levels, 1, 1), 0)
    cond_z = conductance[2] * (level_ids > 0).astype(jnp.float32)
    wet_float = wet.astype(jnp.float32)
    statics = jnp.stack(
        [
            conductance[0] * factor_x[None],
            conductance[1] * factor_y[None],
            cond_z,
            jnp.broadcast_to(wet_float[None], (levels, tile_rows, tile_cols)),
        ]
    )
    margin = 2
    statics_wide = extend(statics, margin, fixed_rim)
    field = wet_float[None, None] * omega
    for block_index in range(ITERS // margin):
        grown = extend(field, margin, moving)
        current = statics_wide
        for inner_index in range(margin):
            grown = diffuse(grown, current)
            current = current[:, :, 1:-1, 1:-1]
        field = grown
    regrouped = lax.all_to_all(field, "vec", split_axis=1, concat_axis=0, tiled=True)
    all_vectors = regrouped.shape[0]
    total_cells = levels * lax.axis_size("tiles") * tile_rows * tile_cols
    flat_values = regrouped.reshape(all_vectors, -1)
    weighted = (regrouped * volume[None, None]).reshape(all_vectors, -1)
    gram_local = lax.dot_general(
        weighted,
        flat_values,
        (((1,), (1,)), ((), ())),
        precision=lax.Precision.HIGHEST,
        preferred_element_type=jnp.float32,
    )
    r_factor = factor(total_over_mesh(gram_local), 1.0 / total_cells)
    return (field, r_factor)


def solution(mesh):
    in_specs = (
        P("vec", None, "tiles", None),
        P(None, None, "tiles", None),
        P("tiles", None),
        P("tiles", None),
        P("tiles", None),
    )
    out_specs = (P("vec", None, "tiles", None), P())
    return jax.shard_map(shards, mesh=mesh, in_specs=in_specs, out_specs=out_specs, check_vma=False)
```

```python
import functools
import jax
import jax.numpy as jnp
from jax import lax
from jax.experimental import pallas as pl
from jax.experimental.pallas import tpu as pltpu
from jax.sharding import PartitionSpec as P

TGY = 8
ITERS = 4
EDGE = 2 * ITERS
VMEM_LIMIT = 32 * 1024 * 1024
MAIN, SLOT = (0, 1)


def ids(shape, axis):
    return lax.broadcasted_iota(jnp.int32, shape, axis)


def turn(value, steps, axis):
    size = value.shape[axis]
    steps = steps % size
    return value if steps == 0 else pltpu.roll(value, steps, axis)


def low_half(shape):
    return ids(shape, 0) < ITERS


def left_lanes(shape):
    return ids(shape, 1) % EDGE < ITERS


def first_pair(a, b):
    return jnp.where(low_half(a.shape), a, turn(b, ITERS, 0))


def last_pair(a, b):
    return jnp.where(low_half(a.shape), turn(a, ITERS, 0), b)


def slots(below, above):
    low = low_half(below.shape)
    return (
        jnp.where(low, below, turn(above, ITERS, 0)),
        jnp.where(low, turn(below, ITERS, 0), above),
    )


def store_pair(outs, index, a, b, is_first_row):
    if len(outs) == 1:
        outs[0][index] = jnp.where(is_first_row, last_pair(a, b), first_pair(a, b))
    else:
        outs[0][index] = first_pair(a, b)
        outs[1][index] = last_pair(a, b)


def add_edge(acc, value, place):
    lanes = ids(value.shape, 1) // EDGE
    moved = turn(value, EDGE * place + ITERS, 1)
    return moved if acc is None else jnp.where(lanes == place, moved, acc)


def prev_row(part, other):
    return jnp.where(ids(part.shape, 0) == 0, turn(other, 1, 0), turn(part, 1, 0))


def next_row(part, other):
    last = part.shape[0] - 1
    return jnp.where(ids(part.shape, 0) == last, turn(other, -1, 0), turn(part, -1, 0))


def prev_col(part, rim):
    return jnp.where(ids(part.shape, 1) == 0, rim, turn(part, 1, 1))


def next_col(part, rim):
    last = part.shape[1] - 1
    return jnp.where(ids(part.shape, 1) == last, rim, turn(part, -1, 1))


def strips(edges, rims):
    left = left_lanes(edges.shape)
    return (jnp.where(left, rims, edges), jnp.where(left, edges, rims))


def crossing(left_strip, right_strip):
    lanes = ids(left_strip.shape, 1) % EDGE
    return jnp.where(lanes == ITERS - 1, turn(right_strip, -1, 1), turn(left_strip, 1, 1))


def rim_of(cross, place):
    return turn(cross, -(EDGE * place + ITERS), 1)


def pack_kernel(chunks, meta, runs, omega, conductance, wet, static_out, edge_out, *row_outs):
    directions = len(row_outs) // chunks
    levels, rows, cols = omega.shape[1:]
    shape = (rows, cols)
    is_first_row = meta[0] == 0
    row_ids, col_ids = (ids(shape, 0), ids(shape, 1))
    wet_cells = wet[...].astype(jnp.float32)
    open_x = (col_ids >= runs[0, 0]) & (col_ids < runs[0, 0] + runs[0, 1])
    open_y = (row_ids >= runs[0, 2]) & (row_ids < runs[0, 2] + runs[0, 3])
    keep_x = (row_ids > 0) | open_x
    keep_y = (col_ids > 0) | open_y
    statics = []
    for level in range(levels):
        statics.append(
            [
                jnp.where(keep_x, conductance[0, level], 0.0),
                jnp.where(keep_y, conductance[1, level], 0.0),
                conductance[2, level] if level else jnp.zeros(shape, jnp.float32),
                wet_cells,
            ]
        )
    kinds = len(statics[0])
    group = cols // EDGE
    for level in range(levels):
        edge = None
        for kind in range(kinds):
            static_out[kind, level] = statics[level][kind]
            edge = add_edge(edge, statics[level][kind], kind)
        edge_out[chunks, level] = edge
        for kind in range(0, kinds, 2):
            outs = row_outs[:directions]
            store_pair(outs, (group // 2 + kind // 2, level), statics[level][kind], statics[level][kind + 1], is_first_row)
        for chunk in range(chunks):
            outs = row_outs[directions * chunk : directions * (chunk + 1)]
            edge = None
            for pair in range(group // 2):
                start = [omega[chunk * group + 2 * pair + i, level] * wet_cells for i in range(2)]
                edge = add_edge(edge, start[0], 2 * pair)
                edge = add_edge(edge, start[1], 2 * pair + 1)
                store_pair(outs, (pair, level), start[0], start[1], is_first_row)
            edge_out[chunk, level] = edge


def corner_kernel(meta, left, right, *outs):
    is_first_row = meta[0] == 0
    groups, levels, rows, cols = left.shape
    take = left_lanes((rows, cols))
    for g in range(groups):
        for level in range(0, levels, 2):
            pair = [jnp.where(take, left[g, level + i], right[g, level + i]) for i in range(2)]
            store_pair(outs, (g, level // 2), pair[0], pair[1], is_first_row)


def rims_of_group(left, right, corner_below, corner_above):
    levels, rows, cols = left.shape[1:]
    take = left_lanes((rows, cols))
    rims = [[jnp.where(take, left[0, level], right[0, level]), None] for level in range(levels)]
    for level in range(0, levels, 2):
        pair = slots(corner_below[0, level // 2], corner_above[0, level // 2])
        rims[level][SLOT], rims[level + 1][SLOT] = pair
    return rims


def weight_kernel(meta, statics, below, above, edges, left, right, corner_below, corner_above, main_out, strip_out):
    kinds, levels, rows, cols = statics.shape
    shape = (rows, cols)
    low = low_half(shape)
    valid = (low & (meta[1] > 0)) | (jnp.logical_not(low) & (meta[0] > 0))
    first = below.shape[0] - kinds // 2
    rims = rims_of_group(left, right, corner_below, corner_above)
    field = [[[statics[kind, level], None] for level in range(levels)] for kind in range(kinds)]
    for level in range(levels):
        for kind in range(0, kinds, 2):
            pair = slots(below[first + kind // 2, level], above[first + kind // 2, level])
            for i in range(2):
                field[kind + i][level][SLOT] = jnp.where(valid, pair[i], 0.0)
    width = cols // EDGE
    lanes = ids(shape, 1) // EDGE

    def spread(strip, kind):
        value = jnp.where(lanes == 0, turn(strip, -EDGE * kind, 1), 0.0)
        span = 1
        while span < width:
            value = value + turn(value, EDGE * span, 1)
            span *= 2
        return value

    side = [[[[None, None] for _ in range(levels)] for _ in range(kinds)] for _ in range(2)]
    cross = [[None, None] for _ in range(levels)]
    for level in range(levels):
        for part in range(2):
            edge = edges[0, level] if part == MAIN else None
            if part == SLOT:
                for kind in range(kinds):
                    edge = add_edge(edge, field[kind][level][SLOT], kind)
            rim = rims[level][part]
            if part == SLOT:
                rim = jnp.where(valid, rim, 0.0)
            pair = strips(edge, rim)
            cross[level][part] = crossing(pair[0], pair[1])
            for s in range(2):
                for kind in range(kinds):
                    side[s][kind][level][part] = spread(pair[s], kind)

    def emit(out, values, after_of):
        for level in range(levels):
            for part in range(2):
                cond_x, cond_y, cond_z, wet = (values[kind][level][part] for kind in range(kinds))
                faces = [
                    cond_x,
                    next_row(cond_x, values[0][level][1 - part]),
                    cond_y,
                    after_of(cond_y, level, part),
                    cond_z,
                    values[2][level + 1][part] if level + 1 < levels else jnp.zeros(shape, jnp.float32),
                ]
                total = faces[0]
                for face in faces[1:]:
                    total = total + face
                out[0, level, part] = wet * (1.0 - total)
                for index, face in enumerate(faces):
                    out[index + 1, level, part] = wet * face

    emit(main_out, field, lambda cond, level, part: next_col(cond, rim_of(cross[level][part], 1)))
    for s in range(2):
        emit(strip_out.at[s], side[s], lambda cond, level, part: turn(cond, -1, 1))


def one_pass(state, weight, parts, rim_at):
    levels = len(state)
    result = [[None, None] for _ in range(levels)]
    for level in range(levels):
        for part in parts:
            value, other = (state[level][part], state[level][1 - part])
            rim = rim_at(level, part)
            before = turn(value, 1, 1) if rim is None else prev_col(value, rim)
            after = turn(value, -1, 1) if rim is None else next_col(value, rim)
            total = weight(0, level, part) * value
            total = total + weight(1, level, part) * prev_row(value, other)
            total = total + weight(2, level, part) * next_row(value, other)
            total = total + weight(3, level, part) * before
            total = total + weight(4, level, part) * after
            if level > 0:
                total = total + weight(5, level, part) * state[level - 1][part]
            if level < levels - 1:
                total = total + weight(6, level, part) * state[level + 1][part]
            result[level][part] = total
    return result


def diffuse_kernel(
    batch, meta, omega, wet, volume, below, above, edges, left, right, corner_below, corner_above,
    main_weights, strip_weights, *rest
):
    field_out, keep_out, send_out, cross_scratch, slot_scratch = rest[-5:]
    group, levels, rows, cols = omega.shape
    shape = (rows, cols)
    wet_cells = wet[...].astype(jnp.float32)
    root = jnp.sqrt(volume[...])
    half = levels // 2
    keeps_low = meta[2] == 0
    rims = rims_of_group(left, right, corner_below, corner_above)
    slot_edges = [None] * levels
    for level in range(levels):
        for pair in range(group // 2):
            two = slots(below[pair, level], above[pair, level])
            for i in range(2):
                slot_scratch[2 * pair + i, level] = two[i]
                slot_edges[level] = add_edge(slot_edges[level], two[i], 2 * pair + i)
    state = [[[None, None] for _ in range(levels)] for _ in range(2)]
    for level in range(levels):
        for part in range(2):
            edge = edges[0, level] if part == MAIN else slot_edges[level]
            pair = strips(edge, rims[level][part])
            for s in range(2):
                state[s][level][part] = pair[s]
    for sweep in range(ITERS):
        for level in range(levels):
            for part in range(2):
                cross_scratch[sweep, level, part] = crossing(state[0][level][part], state[1][level][part])
        if sweep < ITERS - 1:
            for s in range(2):
                state[s] = one_pass(
                    state[s], lambda n, level, part: strip_weights[s, n, level, part], (MAIN, SLOT), lambda level, part: None
                )

    for first in range(0, group, batch):
        fields = []
        for place in range(first, first + batch):
            fields.append([[omega[place, level] * wet_cells, slot_scratch[place, level]] for level in range(levels)])
        for sweep in range(ITERS):
            parts = (MAIN, SLOT) if sweep < ITERS - 1 else (MAIN,)
            for i in range(batch):
                fields[i] = one_pass(
                    fields[i],
                    lambda n, level, part: main_weights[n, level, part],
                    parts,
                    lambda level, part: rim_of(cross_scratch[sweep, level, part], first + i),
                )
        for i in range(batch):
            scaled = []
            for level in range(levels):
                value = fields[i][level][MAIN]
                field_out[first + i, level] = value
                scaled.append(value * root)
            for level in range(half):
                at = ((first + i) * half + level) * rows
                keep_out[at : at + rows, :] = jnp.where(keeps_low, scaled[level], scaled[half + level])
                send_out[at : at + rows, :] = jnp.where(keeps_low, scaled[half + level], scaled[level])


def gram_kernel(chunks, slices, meta, *refs):
    out = refs[-1]
    sources = refs[:-1]
    stride = slices
    group = sources[0].shape[0] // stride
    order = group * len(sources)
    cols = sources[0].shape[1]
    exact = jnp.zeros((order, order), jnp.float32)
    cross = jnp.zeros((order, order), jnp.float32)
    for at in range(0, slices, 2):
        columns = []
        for i in range(2):
            columns.append(jnp.concatenate([ref[pl.ds(at + i, group, stride), :] for ref in sources], axis=0))
        values = jnp.concatenate(columns, axis=1)
        high = values.astype(jnp.bfloat16)
        rest = (values - high.astype(jnp.float32)).astype(jnp.bfloat16)
        dims = (((1,), (1,)), ((), ()))
        exact = exact + lax.dot_general(high, high, dims, preferred_element_type=jnp.float32)
        cross = cross + lax.dot_general(high, rest, dims, preferred_element_type=jnp.float32)
    gram = exact + (cross + cross.T)
    moved = turn(turn(gram, order // 2, 0), order // 2, 1)
    out[...] = jnp.where(meta[2] == 0, gram, moved)


def swapped(value, axis, bit):
    count = lax.axis_size(axis)
    return lax.ppermute(value, axis, [(source, source ^ bit) for source in range(count)])


def total_over_mesh(value):
    for axis in ("tiles", "vec"):
        bit = 1
        while bit < lax.axis_size(axis):
            value = value + swapped(value, axis, bit)
            bit *= 2
    return value


def factor_kernel(scale, gram_ref, out_ref):
    order = gram_ref.shape[0]
    height = 8
    count = order // height
    blocks = [gram_ref[height * b : height * (b + 1), :] * scale for b in range(count)]
    row_ids = lax.broadcasted_iota(jnp.int32, (height, order), 0)
    col_ids = lax.broadcasted_iota(jnp.int32, (height, order), 1)
    for p in range(count):
        rows = jnp.zeros((height, order), jnp.float32)
        for j in range(height):
            k = height * p + j
            current = blocks[p]
            inverse = jnp.broadcast_to(lax.rsqrt(current[j : j + 1, k : k + 1]), (height, order))
            pivot_row = jnp.broadcast_to(current[j : j + 1, :], (height, order)) * inverse
            rows = jnp.where((row_ids == j) & (col_ids >= k), pivot_row, rows)
            for q in range(p, count):
                pivot_col = jnp.broadcast_to(blocks[q][:, k : k + 1], (height, order)) * inverse
                blocks[q] = blocks[q] - pivot_col * pivot_row
        out_ref[height * p : height * (p + 1), :] = rows


def shifted(value, axis, steps):
    count = lax.axis_size(axis)
    first, last = (max(0, -steps), min(count, count - steps))
    return lax.ppermute(value, axis, [(source, source + steps) for source in range(first, last)])


def exchange_rows(messages, grid_rows):
    if len(messages) == 1:
        received = swapped(messages[0], "tiles", TGY)
        return (received, received)
    return (shifted(messages[0], "tiles", -TGY), shifted(messages[1], "tiles", TGY))


def f32(*shape):
    return jax.ShapeDtypeStruct(shape, jnp.float32)


def block(shape, *at):
    return pl.BlockSpec(shape, lambda i: at)


def call(kernel, in_specs, out_specs, out_shape, flops=0, scratch=(), aliases=None):
    return pl.pallas_call(
        kernel,
        grid=(1,),
        in_specs=in_specs,
        out_specs=out_specs,
        out_shape=out_shape,
        scratch_shapes=scratch,
        input_output_aliases=aliases or {},
        compiler_params=pltpu.CompilerParams(vmem_limit_bytes=VMEM_LIMIT),
        cost_estimate=pl.CostEstimate(flops=flops, bytes_accessed=1 << 20, transcendentals=0),
    )


def whole(array):
    zeros = (0,) * array.ndim
    return pl.BlockSpec(array.shape, lambda i: zeros)


def shards(omega, conductance, wet, volume, face_runs):
    vectors, levels, rows, cols = omega.shape
    tiles = lax.axis_size("tiles")
    grid_rows = tiles // TGY
    tile_row = lax.axis_index("tiles") // TGY
    meta = jnp.stack([tile_row, grid_rows - 1 - tile_row, lax.axis_index("vec")]).astype(jnp.int32)
    smem = pl.BlockSpec(memory_space=pltpu.SMEM)
    group = cols // EDGE
    chunks = vectors // group
    directions = 1 if grid_rows == 2 else 2
    kinds = 4
    half = levels // 2

    row_shapes = [f32(group // 2 + (kinds // 2 if c == 0 else 0), levels, rows, cols) for c in range(chunks)]
    row_shapes = [shape for shape in row_shapes for _ in range(directions)]
    packed_shapes = [f32(kinds, levels, rows, cols), f32(chunks + 1, levels, rows, cols)] + row_shapes
    statics, edges, *messages = call(
        functools.partial(pack_kernel, chunks),
        [smem, smem, whole(omega), whole(conductance), whole(wet)],
        [whole(s) for s in packed_shapes],
        packed_shapes,
    )(meta, face_runs, omega, conductance, wet)
    messages = [messages[directions * c : directions * (c + 1)] for c in range(chunks)]
    received = [exchange_rows(messages[0], grid_rows)]
    left = shifted(edges, "tiles", 1)
    right = shifted(edges, "tiles", -1)
    corner_shapes = [f32(chunks + 1, levels // 2, rows, cols)] * directions
    corners = call(
        corner_kernel, [smem, whole(left), whole(right)], [whole(s) for s in corner_shapes], corner_shapes
    )(meta, left, right)
    corners = exchange_rows(corners, grid_rows)
    for c in range(1, chunks):
        received.append(exchange_rows(messages[c], grid_rows))

    def group_specs(c):
        edge = block((1, levels, rows, cols), c, 0, 0, 0)
        corner = block((1, levels // 2, rows, cols), c, 0, 0, 0)
        return [edge, edge, edge, corner, corner]

    around = (edges, left, right, *corners)
    weight_shapes = [f32(7, levels, 2, rows, cols), f32(2, 7, levels, 2, rows, cols)]
    main_weights, strip_weights = call(
        weight_kernel,
        [smem, whole(statics), whole(received[0][0]), whole(received[0][1])] + group_specs(chunks),
        [whole(s) for s in weight_shapes],
        weight_shapes,
    )(meta, statics, *received[0], *around)

    field = None
    kept, sent = ([], [])
    half_shape = f32(group * half * rows, cols)
    for c in range(chunks):
        operands = [meta, omega, wet, volume, *received[c], *around, main_weights, strip_weights]
        row_block = block((group // 2, levels, rows, cols), 0, 0, 0, 0)
        chunk_block = block((group, levels, rows, cols), c, 0, 0, 0)
        specs = [smem, chunk_block, whole(wet), whole(volume), row_block, row_block] + group_specs(c)
        specs += [whole(main_weights), whole(strip_weights)]
        aliases = {}
        if field is not None:
            aliases = {len(operands): 0}
            operands.append(field)
            specs.append(pl.BlockSpec(memory_space=pl.ANY))
        field, keep, send = call(
            functools.partial(diffuse_kernel, 4),
            specs,
            [chunk_block, whole(half_shape), whole(half_shape)],
            [f32(*omega.shape), half_shape, half_shape],
            scratch=[pltpu.VMEM((ITERS, levels, 2, rows, cols), jnp.float32), pltpu.VMEM((group, levels, rows, cols), jnp.float32)],
            aliases=aliases,
        )(*operands)
        kept.append(keep)
        sent.append(swapped(send, "vec", 1))

    order = 2 * vectors
    gram = call(
        functools.partial(gram_kernel, chunks, half * rows),
        [smem] + [whole(half_shape)] * (2 * chunks),
        whole(f32(order, order)),
        f32(order, order),
    )(meta, *kept, *sent)
    total_cells = levels * tiles * rows * cols
    r_factor = call(
        functools.partial(factor_kernel, 1.0 / total_cells),
        [whole(gram)],
        whole(gram),
        f32(order, order),
    )(total_over_mesh(gram))
    return (field, r_factor)


def solution(mesh):
    in_specs = (
        P("vec", None, "tiles", None),
        P(None, None, "tiles", None),
        P("tiles", None),
        P("tiles", None),
        P("tiles", None),
    )
    out_specs = (P("vec", None, "tiles", None), P())
    return jax.shard_map(shards, mesh=mesh, in_specs=in_specs, out_specs=out_specs, check_vma=False)
```

```python
import functools
import jax
import jax.numpy as jnp
from jax import lax
from jax.experimental import pallas as pl
from jax.experimental.pallas import tpu as pltpu
from jax.sharding import PartitionSpec as P

TGY = 8
ITERS = 4
EDGE = 2 * ITERS
VMEM_LIMIT = 32 * 1024 * 1024
MAIN, SLOT = (0, 1)


def ids(shape, axis):
    return lax.broadcasted_iota(jnp.int32, shape, axis)


def turn(value, steps, axis):
    size = value.shape[axis]
    steps = steps % size
    return value if steps == 0 else pltpu.roll(value, steps, axis)


def low_half(shape):
    return ids(shape, 0) < ITERS


def left_lanes(shape):
    return ids(shape, 1) % EDGE < ITERS


def first_pair(a, b):
    return jnp.where(low_half(a.shape), a, turn(b, ITERS, 0))


def last_pair(a, b):
    return jnp.where(low_half(a.shape), turn(a, ITERS, 0), b)


def slots(below, above):
    low = low_half(below.shape)
    return (
        jnp.where(low, below, turn(above, ITERS, 0)),
        jnp.where(low, turn(below, ITERS, 0), above),
    )


def store_pair(outs, index, a, b, is_first_row):
    if len(outs) == 1:
        outs[0][index] = jnp.where(is_first_row, last_pair(a, b), first_pair(a, b))
    else:
        outs[0][index] = first_pair(a, b)
        outs[1][index] = last_pair(a, b)


def add_edge(acc, value, place):
    lanes = ids(value.shape, 1) // EDGE
    moved = turn(value, EDGE * place + ITERS, 1)
    return moved if acc is None else jnp.where(lanes == place, moved, acc)


def prev_row(part, other):
    return jnp.where(ids(part.shape, 0) == 0, turn(other, 1, 0), turn(part, 1, 0))


def next_row(part, other):
    last = part.shape[0] - 1
    return jnp.where(ids(part.shape, 0) == last, turn(other, -1, 0), turn(part, -1, 0))


def prev_col(part, rim):
    return jnp.where(ids(part.shape, 1) == 0, rim, turn(part, 1, 1))


def next_col(part, rim):
    last = part.shape[1] - 1
    return jnp.where(ids(part.shape, 1) == last, rim, turn(part, -1, 1))


def strips(edges, rims):
    left = left_lanes(edges.shape)
    return (jnp.where(left, rims, edges), jnp.where(left, edges, rims))


def crossing(left_strip, right_strip):
    lanes = ids(left_strip.shape, 1) % EDGE
    return jnp.where(lanes == ITERS - 1, turn(right_strip, -1, 1), turn(left_strip, 1, 1))


def rim_of(cross, place):
    return turn(cross, -(EDGE * place + ITERS), 1)


def pack_kernel(chunks, meta, runs, omega, conductance, wet, static_out, edge_out, *row_outs):
    directions = len(row_outs) // chunks
    levels, rows, cols = omega.shape[1:]
    shape = (rows, cols)
    is_first_row = meta[0] == 0
    row_ids, col_ids = (ids(shape, 0), ids(shape, 1))
    wet_cells = wet[...].astype(jnp.float32)
    open_x = (col_ids >= runs[0, 0]) & (col_ids < runs[0, 0] + runs[0, 1])
    open_y = (row_ids >= runs[0, 2]) & (row_ids < runs[0, 2] + runs[0, 3])
    keep_x = (row_ids > 0) | open_x
    keep_y = (col_ids > 0) | open_y
    statics = []
    for level in range(levels):
        statics.append(
            [
                jnp.where(keep_x, conductance[0, level], 0.0),
                jnp.where(keep_y, conductance[1, level], 0.0),
                conductance[2, level] if level else jnp.zeros(shape, jnp.float32),
                wet_cells,
            ]
        )
    kinds = len(statics[0])
    group = cols // EDGE
    for level in range(levels):
        edge = None
        for kind in range(kinds):
            static_out[kind, level] = statics[level][kind]
            edge = add_edge(edge, statics[level][kind], kind)
        edge_out[chunks, level] = edge
        for kind in range(0, kinds, 2):
            outs = row_outs[:directions]
            store_pair(outs, (group // 2 + kind // 2, level), statics[level][kind], statics[level][kind + 1], is_first_row)
        for chunk in range(chunks):
            outs = row_outs[directions * chunk : directions * (chunk + 1)]
            edge = None
            for pair in range(group // 2):
                start = [omega[chunk * group + 2 * pair + i, level] * wet_cells for i in range(2)]
                edge = add_edge(edge, start[0], 2 * pair)
                edge = add_edge(edge, start[1], 2 * pair + 1)
                store_pair(outs, (pair, level), start[0], start[1], is_first_row)
            edge_out[chunk, level] = edge


def corner_kernel(meta, left, right, *outs):
    is_first_row = meta[0] == 0
    groups, levels, rows, cols = left.shape
    take = left_lanes((rows, cols))
    for g in range(groups):
        for level in range(0, levels, 2):
            pair = [jnp.where(take, left[g, level + i], right[g, level + i]) for i in range(2)]
            store_pair(outs, (g, level // 2), pair[0], pair[1], is_first_row)


def rims_of_group(left, right, corner_below, corner_above):
    levels, rows, cols = left.shape[1:]
    take = left_lanes((rows, cols))
    rims = [[jnp.where(take, left[0, level], right[0, level]), None] for level in range(levels)]
    for level in range(0, levels, 2):
        pair = slots(corner_below[0, level // 2], corner_above[0, level // 2])
        rims[level][SLOT], rims[level + 1][SLOT] = pair
    return rims


def weight_kernel(meta, statics, below, above, edges, left, right, corner_below, corner_above, main_out, strip_out):
    kinds, levels, rows, cols = statics.shape
    shape = (rows, cols)
    low = low_half(shape)
    valid = (low & (meta[1] > 0)) | (jnp.logical_not(low) & (meta[0] > 0))
    first = below.shape[0] - kinds // 2
    rims = rims_of_group(left, right, corner_below, corner_above)
    field = [[[statics[kind, level], None] for level in range(levels)] for kind in range(kinds)]
    for level in range(levels):
        for kind in range(0, kinds, 2):
            pair = slots(below[first + kind // 2, level], above[first + kind // 2, level])
            for i in range(2):
                field[kind + i][level][SLOT] = jnp.where(valid, pair[i], 0.0)
    width = cols // EDGE
    lanes = ids(shape, 1) // EDGE

    def spread(strip, kind):
        value = jnp.where(lanes == 0, turn(strip, -EDGE * kind, 1), 0.0)
        span = 1
        while span < width:
            value = value + turn(value, EDGE * span, 1)
            span *= 2
        return value

    side = [[[[None, None] for _ in range(levels)] for _ in range(kinds)] for _ in range(2)]
    cross = [[None, None] for _ in range(levels)]
    for level in range(levels):
        for part in range(2):
            edge = edges[0, level] if part == MAIN else None
            if part == SLOT:
                for kind in range(kinds):
                    edge = add_edge(edge, field[kind][level][SLOT], kind)
            rim = rims[level][part]
            if part == SLOT:
                rim = jnp.where(valid, rim, 0.0)
            pair = strips(edge, rim)
            cross[level][part] = crossing(pair[0], pair[1])
            for s in range(2):
                for kind in range(kinds):
                    side[s][kind][level][part] = spread(pair[s], kind)

    def emit(out, values, after_of):
        for level in range(levels):
            for part in range(2):
                cond_x, cond_y, cond_z, wet = (values[kind][level][part] for kind in range(kinds))
                faces = [
                    cond_x,
                    next_row(cond_x, values[0][level][1 - part]),
                    cond_y,
                    after_of(cond_y, level, part),
                    cond_z,
                    values[2][level + 1][part] if level + 1 < levels else jnp.zeros(shape, jnp.float32),
                ]
                total = faces[0]
                for face in faces[1:]:
                    total = total + face
                out[0, level, part] = wet * (1.0 - total)
                for index, face in enumerate(faces):
                    out[index + 1, level, part] = wet * face

    emit(main_out, field, lambda cond, level, part: next_col(cond, rim_of(cross[level][part], 1)))
    for s in range(2):
        emit(strip_out.at[s], side[s], lambda cond, level, part: turn(cond, -1, 1))


def one_pass(state, weight, parts, rim_at):
    levels = len(state)
    result = [[None, None] for _ in range(levels)]
    for level in range(levels):
        for part in parts:
            value, other = (state[level][part], state[level][1 - part])
            rim = rim_at(level, part)
            before = turn(value, 1, 1) if rim is None else prev_col(value, rim)
            after = turn(value, -1, 1) if rim is None else next_col(value, rim)
            total = weight(0, level, part) * value
            total = total + weight(1, level, part) * prev_row(value, other)
            total = total + weight(2, level, part) * next_row(value, other)
            total = total + weight(3, level, part) * before
            total = total + weight(4, level, part) * after
            if level > 0:
                total = total + weight(5, level, part) * state[level - 1][part]
            if level < levels - 1:
                total = total + weight(6, level, part) * state[level + 1][part]
            result[level][part] = total
    return result


def diffuse_kernel(
    batch, meta, omega, wet, volume, below, above, edges, left, right, corner_below, corner_above,
    main_weights, strip_weights, *rest
):
    field_out, keep_out, send_out, cross_scratch, slot_scratch = rest[-5:]
    group, levels, rows, cols = omega.shape
    shape = (rows, cols)
    wet_cells = wet[...].astype(jnp.float32)
    root = jnp.sqrt(volume[...])
    half = levels // 2
    keeps_low = meta[2] == 0
    rims = rims_of_group(left, right, corner_below, corner_above)
    slot_edges = [None] * levels
    for level in range(levels):
        for pair in range(group // 2):
            two = slots(below[pair, level], above[pair, level])
            for i in range(2):
                slot_scratch[2 * pair + i, level] = two[i]
                slot_edges[level] = add_edge(slot_edges[level], two[i], 2 * pair + i)
    state = [[[None, None] for _ in range(levels)] for _ in range(2)]
    for level in range(levels):
        for part in range(2):
            edge = edges[0, level] if part == MAIN else slot_edges[level]
            pair = strips(edge, rims[level][part])
            for s in range(2):
                state[s][level][part] = pair[s]
    for sweep in range(ITERS):
        for level in range(levels):
            for part in range(2):
                cross_scratch[sweep, level, part] = crossing(state[0][level][part], state[1][level][part])
        if sweep < ITERS - 1:
            for s in range(2):
                state[s] = one_pass(
                    state[s], lambda n, level, part: strip_weights[s, n, level, part], (MAIN, SLOT), lambda level, part: None
                )

    for first in range(0, group, batch):
        fields = []
        for place in range(first, first + batch):
            fields.append([[omega[place, level] * wet_cells, slot_scratch[place, level]] for level in range(levels)])
        for sweep in range(ITERS):
            parts = (MAIN, SLOT) if sweep < ITERS - 1 else (MAIN,)
            for i in range(batch):
                fields[i] = one_pass(
                    fields[i],
                    lambda n, level, part: main_weights[n, level, part],
                    parts,
                    lambda level, part: rim_of(cross_scratch[sweep, level, part], first + i),
                )
        for i in range(batch):
            scaled = []
            for level in range(levels):
                value = fields[i][level][MAIN]
                field_out[first + i, level] = value
                scaled.append(value * root)
            for level in range(half):
                at = ((first + i) * half + level) * rows
                keep_out[at : at + rows, :] = jnp.where(keeps_low, scaled[level], scaled[half + level])
                send_out[at : at + rows, :] = jnp.where(keeps_low, scaled[half + level], scaled[level])


def gram_kernel(chunks, slices, meta, *refs):
    out = refs[-1]
    sources = refs[:-1]
    stride = slices
    group = sources[0].shape[0] // stride
    order = group * len(sources)
    cols = sources[0].shape[1]
    exact = jnp.zeros((order, order), jnp.float32)
    cross = jnp.zeros((order, order), jnp.float32)
    for at in range(0, slices, 2):
        columns = []
        for i in range(2):
            columns.append(jnp.concatenate([ref[pl.ds(at + i, group, stride), :] for ref in sources], axis=0))
        values = jnp.concatenate(columns, axis=1)
        high = values.astype(jnp.bfloat16)
        rest = (values - high.astype(jnp.float32)).astype(jnp.bfloat16)
        dims = (((1,), (1,)), ((), ()))
        exact = exact + lax.dot_general(high, high, dims, preferred_element_type=jnp.float32)
        cross = cross + lax.dot_general(high, rest, dims, preferred_element_type=jnp.float32)
    gram = exact + (cross + cross.T)
    moved = turn(turn(gram, order // 2, 0), order // 2, 1)
    out[...] = jnp.where(meta[2] == 0, gram, moved)


def swapped(value, axis, bit):
    count = lax.axis_size(axis)
    return lax.ppermute(value, axis, [(source, source ^ bit) for source in range(count)])


def total_over_mesh(value):
    for axis in ("tiles", "vec"):
        bit = 1
        while bit < lax.axis_size(axis):
            value = value + swapped(value, axis, bit)
            bit *= 2
    return value


def factor_kernel(scale, gram_ref, out_ref):
    order = gram_ref.shape[0]
    height = 8
    count = order // height
    blocks = [gram_ref[height * b : height * (b + 1), :] * scale for b in range(count)]
    row_ids = lax.broadcasted_iota(jnp.int32, (height, order), 0)
    col_ids = lax.broadcasted_iota(jnp.int32, (height, order), 1)
    for p in range(count):
        rows = jnp.zeros((height, order), jnp.float32)
        for j in range(height):
            k = height * p + j
            current = blocks[p]
            inverse = jnp.broadcast_to(lax.rsqrt(current[j : j + 1, k : k + 1]), (height, order))
            pivot_row = jnp.broadcast_to(current[j : j + 1, :], (height, order)) * inverse
            rows = jnp.where((row_ids == j) & (col_ids >= k), pivot_row, rows)
            for q in range(p, count):
                pivot_col = jnp.broadcast_to(blocks[q][:, k : k + 1], (height, order)) * inverse
                blocks[q] = blocks[q] - pivot_col * pivot_row
        out_ref[height * p : height * (p + 1), :] = rows


def shifted(value, axis, steps):
    count = lax.axis_size(axis)
    first, last = (max(0, -steps), min(count, count - steps))
    return lax.ppermute(value, axis, [(source, source + steps) for source in range(first, last)])


def beside(value, steps):
    count = lax.axis_size("tiles")
    pairs = [(source, source + steps) for source in range(count)]
    return lax.ppermute(value, "tiles", [(a, b) for a, b in pairs if 0 <= b < count and a // TGY == b // TGY])


def after(values, *done):
    return lax.optimization_barrier((values, done))[0]


def exchange_rows(messages, grid_rows):
    if len(messages) == 1:
        received = swapped(messages[0], "tiles", TGY)
        return (received, received)
    return (shifted(messages[0], "tiles", -TGY), shifted(messages[1], "tiles", TGY))


def f32(*shape):
    return jax.ShapeDtypeStruct(shape, jnp.float32)


def block(shape, *at):
    return pl.BlockSpec(shape, lambda i: at)


def call(kernel, in_specs, out_specs, out_shape, flops=0, scratch=(), aliases=None):
    return pl.pallas_call(
        kernel,
        grid=(1,),
        in_specs=in_specs,
        out_specs=out_specs,
        out_shape=out_shape,
        scratch_shapes=scratch,
        input_output_aliases=aliases or {},
        compiler_params=pltpu.CompilerParams(vmem_limit_bytes=VMEM_LIMIT),
        cost_estimate=pl.CostEstimate(flops=flops, bytes_accessed=1 << 20, transcendentals=0),
    )


def whole(array):
    zeros = (0,) * array.ndim
    return pl.BlockSpec(array.shape, lambda i: zeros)


def shards(omega, conductance, wet, volume, face_runs):
    vectors, levels, rows, cols = omega.shape
    tiles = lax.axis_size("tiles")
    grid_rows = tiles // TGY
    tile_row = lax.axis_index("tiles") // TGY
    meta = jnp.stack([tile_row, grid_rows - 1 - tile_row, lax.axis_index("vec")]).astype(jnp.int32)
    smem = pl.BlockSpec(memory_space=pltpu.SMEM)
    group = cols // EDGE
    chunks = vectors // group
    directions = 1 if grid_rows == 2 else 2
    kinds = 4
    half = levels // 2

    row_shapes = [f32(group // 2 + (kinds // 2 if c == 0 else 0), levels, rows, cols) for c in range(chunks)]
    row_shapes = [shape for shape in row_shapes for _ in range(directions)]
    packed_shapes = [f32(kinds, levels, rows, cols), f32(chunks + 1, levels, rows, cols)] + row_shapes
    statics, edges, *messages = call(
        functools.partial(pack_kernel, chunks),
        [smem, smem, whole(omega), whole(conductance), whole(wet)],
        [whole(s) for s in packed_shapes],
        packed_shapes,
    )(meta, face_runs, omega, conductance, wet)
    messages = [messages[directions * c : directions * (c + 1)] for c in range(chunks)]
    received = [exchange_rows(messages[0], grid_rows)]
    left = beside(edges, 1)
    right = beside(edges, -1)
    corner_shapes = [f32(chunks + 1, levels // 2, rows, cols)] * directions
    corners = call(
        corner_kernel, [smem, whole(left), whole(right)], [whole(s) for s in corner_shapes], corner_shapes
    )(meta, left, right)
    corners = exchange_rows(corners, grid_rows)
    gates = [(left, right), corners]
    for c in range(1, chunks):
        gate = gates[c - 1] if c <= 2 else received[c - 2]
        received.append(exchange_rows(after(messages[c], *gate), grid_rows))

    def group_specs(c):
        edge = block((1, levels, rows, cols), c, 0, 0, 0)
        corner = block((1, levels // 2, rows, cols), c, 0, 0, 0)
        return [edge, edge, edge, corner, corner]

    around = (edges, left, right, *corners)
    weight_shapes = [f32(7, levels, 2, rows, cols), f32(2, 7, levels, 2, rows, cols)]
    main_weights, strip_weights = call(
        weight_kernel,
        [smem, whole(statics), whole(received[0][0]), whole(received[0][1])] + group_specs(chunks),
        [whole(s) for s in weight_shapes],
        weight_shapes,
    )(meta, statics, *received[0], *around)

    field = None
    kept, sent = ([], [])
    half_shape = f32(group * half * rows, cols)
    for c in range(chunks):
        rims = after(received[c], sent[c - 2]) if c >= 2 else received[c]
        operands = [meta, omega, wet, volume, *rims, *around, main_weights, strip_weights]
        row_block = block((group // 2, levels, rows, cols), 0, 0, 0, 0)
        chunk_block = block((group, levels, rows, cols), c, 0, 0, 0)
        specs = [smem, chunk_block, whole(wet), whole(volume), row_block, row_block] + group_specs(c)
        specs += [whole(main_weights), whole(strip_weights)]
        aliases = {}
        if field is not None:
            aliases = {len(operands): 0}
            operands.append(field)
            specs.append(pl.BlockSpec(memory_space=pl.ANY))
        field, keep, send = call(
            functools.partial(diffuse_kernel, 4),
            specs,
            [chunk_block, whole(half_shape), whole(half_shape)],
            [f32(*omega.shape), half_shape, half_shape],
            flops=4 * 10**9,
            scratch=[pltpu.VMEM((ITERS, levels, 2, rows, cols), jnp.float32), pltpu.VMEM((group, levels, rows, cols), jnp.float32)],
            aliases=aliases,
        )(*operands)
        kept.append(keep)
        sent.append(swapped(send, "vec", 1))

    order = 2 * vectors
    gram = call(
        functools.partial(gram_kernel, chunks, half * rows),
        [smem] + [whole(half_shape)] * (2 * chunks),
        whole(f32(order, order)),
        f32(order, order),
    )(meta, *kept, *sent)
    total_cells = levels * tiles * rows * cols
    r_factor = call(
        functools.partial(factor_kernel, 1.0 / total_cells),
        [whole(gram)],
        whole(gram),
        f32(order, order),
    )(total_over_mesh(gram))
    return (field, r_factor)


def solution(mesh):
    in_specs = (
        P("vec", None, "tiles", None),
        P(None, None, "tiles", None),
        P("tiles", None),
        P("tiles", None),
        P("tiles", None),
    )
    out_specs = (P("vec", None, "tiles", None), P())
    return jax.shard_map(shards, mesh=mesh, in_specs=in_specs, out_specs=out_specs, check_vma=False)
```

```python
import functools
import jax
import jax.numpy as jnp
from jax import lax
from jax.experimental import pallas as pl
from jax.experimental.pallas import tpu as pltpu
from jax.sharding import PartitionSpec as P

TGY = 8
ITERS = 4
EDGE = 2 * ITERS
VMEM_LIMIT = 32 * 1024 * 1024
MAIN, SLOT = (0, 1)


def ids(shape, axis):
    return lax.broadcasted_iota(jnp.int32, shape, axis)


def turn(value, steps, axis):
    size = value.shape[axis]
    steps = steps % size
    return value if steps == 0 else pltpu.roll(value, steps, axis)


def low_half(shape):
    return ids(shape, 0) < ITERS


def left_lanes(shape):
    return ids(shape, 1) % EDGE < ITERS


def first_pair(a, b):
    return jnp.where(low_half(a.shape), a, turn(b, ITERS, 0))


def last_pair(a, b):
    return jnp.where(low_half(a.shape), turn(a, ITERS, 0), b)


def slots(below, above):
    low = low_half(below.shape)
    return (
        jnp.where(low, below, turn(above, ITERS, 0)),
        jnp.where(low, turn(below, ITERS, 0), above),
    )


def store_pair(outs, index, a, b, is_first_row):
    if len(outs) == 1:
        outs[0][index] = jnp.where(is_first_row, last_pair(a, b), first_pair(a, b))
    else:
        outs[0][index] = first_pair(a, b)
        outs[1][index] = last_pair(a, b)


def add_edge(acc, value, place):
    lanes = ids(value.shape, 1) // EDGE
    moved = turn(value, EDGE * place + ITERS, 1)
    return moved if acc is None else jnp.where(lanes == place, moved, acc)


def prev_row(part, other):
    return jnp.where(ids(part.shape, 0) == 0, turn(other, 1, 0), turn(part, 1, 0))


def next_row(part, other):
    last = part.shape[0] - 1
    return jnp.where(ids(part.shape, 0) == last, turn(other, -1, 0), turn(part, -1, 0))


def prev_col(part, rim):
    return jnp.where(ids(part.shape, 1) == 0, rim, turn(part, 1, 1))


def next_col(part, rim):
    last = part.shape[1] - 1
    return jnp.where(ids(part.shape, 1) == last, rim, turn(part, -1, 1))


def strips(edges, rims):
    left = left_lanes(edges.shape)
    return (jnp.where(left, rims, edges), jnp.where(left, edges, rims))


def crossing(left_strip, right_strip):
    lanes = ids(left_strip.shape, 1) % EDGE
    return jnp.where(lanes == ITERS - 1, turn(right_strip, -1, 1), turn(left_strip, 1, 1))


def rim_of(cross, place):
    return turn(cross, -(EDGE * place + ITERS), 1)


def pack_kernel(chunks, meta, runs, omega, conductance, wet, static_out, edge_out, *row_outs):
    directions = len(row_outs) // chunks
    levels, rows, cols = omega.shape[1:]
    shape = (rows, cols)
    is_first_row = meta[0] == 0
    row_ids, col_ids = (ids(shape, 0), ids(shape, 1))
    wet_cells = wet[...].astype(jnp.float32)
    open_x = (col_ids >= runs[0, 0]) & (col_ids < runs[0, 0] + runs[0, 1])
    open_y = (row_ids >= runs[0, 2]) & (row_ids < runs[0, 2] + runs[0, 3])
    keep_x = (row_ids > 0) | open_x
    keep_y = (col_ids > 0) | open_y
    statics = []
    for level in range(levels):
        statics.append(
            [
                jnp.where(keep_x, conductance[0, level], 0.0),
                jnp.where(keep_y, conductance[1, level], 0.0),
                conductance[2, level] if level else jnp.zeros(shape, jnp.float32),
                wet_cells,
            ]
        )
    kinds = len(statics[0])
    group = cols // EDGE
    for level in range(levels):
        edge = None
        for kind in range(kinds):
            static_out[kind, level] = statics[level][kind]
            edge = add_edge(edge, statics[level][kind], kind)
        edge_out[chunks, level] = edge
        for kind in range(0, kinds, 2):
            outs = row_outs[:directions]
            store_pair(outs, (group // 2 + kind // 2, level), statics[level][kind], statics[level][kind + 1], is_first_row)
        for chunk in range(chunks):
            outs = row_outs[directions * chunk : directions * (chunk + 1)]
            edge = None
            for pair in range(group // 2):
                start = [omega[chunk * group + 2 * pair + i, level] * wet_cells for i in range(2)]
                edge = add_edge(edge, start[0], 2 * pair)
                edge = add_edge(edge, start[1], 2 * pair + 1)
                store_pair(outs, (pair, level), start[0], start[1], is_first_row)
            edge_out[chunk, level] = edge


def corner_kernel(meta, left, right, *outs):
    is_first_row = meta[0] == 0
    groups, levels, rows, cols = left.shape
    take = left_lanes((rows, cols))
    for g in range(groups):
        for level in range(0, levels, 2):
            pair = [jnp.where(take, left[g, level + i], right[g, level + i]) for i in range(2)]
            store_pair(outs, (g, level // 2), pair[0], pair[1], is_first_row)


def rims_of_group(left, right, corner_below, corner_above):
    levels, rows, cols = left.shape[1:]
    take = left_lanes((rows, cols))
    rims = [[jnp.where(take, left[0, level], right[0, level]), None] for level in range(levels)]
    for level in range(0, levels, 2):
        pair = slots(corner_below[0, level // 2], corner_above[0, level // 2])
        rims[level][SLOT], rims[level + 1][SLOT] = pair
    return rims


def weight_kernel(meta, statics, below, above, edges, left, right, corner_below, corner_above, main_out, strip_out):
    kinds, levels, rows, cols = statics.shape
    shape = (rows, cols)
    low = low_half(shape)
    valid = (low & (meta[1] > 0)) | (jnp.logical_not(low) & (meta[0] > 0))
    first = below.shape[0] - kinds // 2
    rims = rims_of_group(left, right, corner_below, corner_above)
    field = [[[statics[kind, level], None] for level in range(levels)] for kind in range(kinds)]
    for level in range(levels):
        for kind in range(0, kinds, 2):
            pair = slots(below[first + kind // 2, level], above[first + kind // 2, level])
            for i in range(2):
                field[kind + i][level][SLOT] = jnp.where(valid, pair[i], 0.0)
    width = cols // EDGE
    lanes = ids(shape, 1) // EDGE

    def spread(strip, kind):
        value = jnp.where(lanes == 0, turn(strip, -EDGE * kind, 1), 0.0)
        span = 1
        while span < width:
            value = value + turn(value, EDGE * span, 1)
            span *= 2
        return value

    side = [[[[None, None] for _ in range(levels)] for _ in range(kinds)] for _ in range(2)]
    cross = [[None, None] for _ in range(levels)]
    for level in range(levels):
        for part in range(2):
            edge = edges[0, level] if part == MAIN else None
            if part == SLOT:
                for kind in range(kinds):
                    edge = add_edge(edge, field[kind][level][SLOT], kind)
            rim = rims[level][part]
            if part == SLOT:
                rim = jnp.where(valid, rim, 0.0)
            pair = strips(edge, rim)
            cross[level][part] = crossing(pair[0], pair[1])
            for s in range(2):
                for kind in range(kinds):
                    side[s][kind][level][part] = spread(pair[s], kind)

    def emit(out, values, after_of):
        for level in range(levels):
            for part in range(2):
                cond_x, cond_y, cond_z, wet = (values[kind][level][part] for kind in range(kinds))
                faces = [
                    cond_x,
                    next_row(cond_x, values[0][level][1 - part]),
                    cond_y,
                    after_of(cond_y, level, part),
                    cond_z,
                    values[2][level + 1][part] if level + 1 < levels else jnp.zeros(shape, jnp.float32),
                ]
                total = faces[0]
                for face in faces[1:]:
                    total = total + face
                out[0, level, part] = wet * (1.0 - total)
                for index, face in enumerate(faces):
                    out[index + 1, level, part] = wet * face

    emit(main_out, field, lambda cond, level, part: next_col(cond, rim_of(cross[level][part], 1)))
    for s in range(2):
        emit(strip_out.at[s], side[s], lambda cond, level, part: turn(cond, -1, 1))


def one_pass(state, weight, parts, rim_at):
    levels = len(state)
    result = [[None, None] for _ in range(levels)]
    for level in range(levels):
        for part in parts:
            value, other = (state[level][part], state[level][1 - part])
            rim = rim_at(level, part)
            before = turn(value, 1, 1) if rim is None else prev_col(value, rim)
            after = turn(value, -1, 1) if rim is None else next_col(value, rim)
            total = weight(0, level, part) * value
            total = total + weight(1, level, part) * prev_row(value, other)
            total = total + weight(2, level, part) * next_row(value, other)
            total = total + weight(3, level, part) * before
            total = total + weight(4, level, part) * after
            if level > 0:
                total = total + weight(5, level, part) * state[level - 1][part]
            if level < levels - 1:
                total = total + weight(6, level, part) * state[level + 1][part]
            result[level][part] = total
    return result


def diffuse_kernel(
    batch, meta, omega, wet, volume, below, above, edges, left, right, corner_below, corner_above,
    main_weights, strip_weights, *rest
):
    field_out, keep_out, send_out, cross_scratch, slot_scratch = rest[-5:]
    group, levels, rows, cols = omega.shape
    shape = (rows, cols)
    wet_cells = wet[...].astype(jnp.float32)
    root = jnp.sqrt(volume[...])
    half = levels // 2
    keeps_low = meta[2] == 0
    rims = rims_of_group(left, right, corner_below, corner_above)
    slot_edges = [None] * levels
    for level in range(levels):
        for pair in range(group // 2):
            two = slots(below[pair, level], above[pair, level])
            for i in range(2):
                slot_scratch[2 * pair + i, level] = two[i]
                slot_edges[level] = add_edge(slot_edges[level], two[i], 2 * pair + i)
    state = [[[None, None] for _ in range(levels)] for _ in range(2)]
    for level in range(levels):
        for part in range(2):
            edge = edges[0, level] if part == MAIN else slot_edges[level]
            pair = strips(edge, rims[level][part])
            for s in range(2):
                state[s][level][part] = pair[s]
    for sweep in range(ITERS):
        for level in range(levels):
            for part in range(2):
                cross_scratch[sweep, level, part] = crossing(state[0][level][part], state[1][level][part])
        if sweep < ITERS - 1:
            for s in range(2):
                state[s] = one_pass(
                    state[s], lambda n, level, part: strip_weights[s, n, level, part], (MAIN, SLOT), lambda level, part: None
                )

    for first in range(0, group, batch):
        fields = []
        for place in range(first, first + batch):
            fields.append([[omega[place, level] * wet_cells, slot_scratch[place, level]] for level in range(levels)])
        for sweep in range(ITERS):
            parts = (MAIN, SLOT) if sweep < ITERS - 1 else (MAIN,)
            for i in range(batch):
                fields[i] = one_pass(
                    fields[i],
                    lambda n, level, part: main_weights[n, level, part],
                    parts,
                    lambda level, part: rim_of(cross_scratch[sweep, level, part], first + i),
                )
        for i in range(batch):
            scaled = []
            for level in range(levels):
                value = fields[i][level][MAIN]
                field_out[first + i, level] = value
                scaled.append(value * root)
            for level in range(half):
                at = ((first + i) * half + level) * rows
                keep_out[at : at + rows, :] = jnp.where(keeps_low, scaled[level], scaled[half + level])
                send_out[at : at + rows, :] = jnp.where(keeps_low, scaled[half + level], scaled[level])


def gram_kernel(chunks, slices, meta, *refs):
    mine, theirs = refs[-2:]
    sources = refs[:-2]
    stride = slices
    group = sources[0].shape[0] // stride
    order = group * len(sources)
    cols = sources[0].shape[1]
    exact = jnp.zeros((order, order), jnp.float32)
    cross = jnp.zeros((order, order), jnp.float32)
    for at in range(0, slices, 2):
        columns = []
        for i in range(2):
            columns.append(jnp.concatenate([ref[pl.ds(at + i, group, stride), :] for ref in sources], axis=0))
        values = jnp.concatenate(columns, axis=1)
        high = values.astype(jnp.bfloat16)
        rest = (values - high.astype(jnp.float32)).astype(jnp.bfloat16)
        dims = (((1,), (1,)), ((), ()))
        exact = exact + lax.dot_general(high, high, dims, preferred_element_type=jnp.float32)
        cross = cross + lax.dot_general(high, rest, dims, preferred_element_type=jnp.float32)
    gram = exact + (cross + cross.T)
    moved = turn(turn(gram, order // 2, 0), order // 2, 1)
    first, second = halves_of_gram(jnp.where(meta[2] == 0, gram, moved))
    is_first = meta[3] == 0
    mine[...] = jnp.where(is_first, first, second)
    theirs[...] = jnp.where(is_first, second, first)


def swapped(value, axis, bit):
    count = lax.axis_size(axis)
    return lax.ppermute(value, axis, [(source, source ^ bit) for source in range(count)])


def mesh_permute(value, mask):
    axes = ("tiles", "vec")
    count = lax.axis_size("tiles") * lax.axis_size("vec")
    return lax.ppermute(value, axes, [(source, source ^ mask) for source in range(count)])


def total_over_chips(value):
    vec = lax.axis_size("vec")
    masks = []
    bit = 1
    while bit < vec:
        masks.append(bit)
        bit *= 2
    bit = 2
    while bit < lax.axis_size("tiles"):
        masks.append(bit * vec)
        bit *= 2
    while masks:
        near, masks = (masks[:2], masks[2:])
        if len(near) == 1:
            value = value + mesh_permute(value, near[0])
        else:
            one, two, both = (mesh_permute(value, mask) for mask in (near[0], near[1], near[0] ^ near[1]))
            value = (value + one) + (two + both)
    return value


def fold(a, b):
    half = a.shape[1] // 2
    return jnp.where(ids(a.shape, 1) < half, a, b)


def flip(value):
    return turn(value, value.shape[1] // 2, 1)


def halves_of_gram(gram):
    q = gram.shape[0] // 8
    first = [fold(gram[: 2 * q], flip(gram[2 * q : 4 * q])), fold(flip(gram[:q]), gram[q : 2 * q])]
    second = [fold(flip(gram[4 * q : 6 * q]), gram[6 * q :]), fold(flip(gram[2 * q : 3 * q]), gram[3 * q : 4 * q])]
    return (jnp.concatenate(first, axis=0), jnp.concatenate(second, axis=0))


def gram_of_halves(first, second):
    q = first.shape[0] // 3
    return jnp.concatenate(
        [
            fold(first[:q], flip(first[2 * q :])),
            fold(first[q : 2 * q], first[2 * q :]),
            fold(flip(first[:q]), flip(second[2 * q :])),
            fold(flip(first[q : 2 * q]), second[2 * q :]),
            flip(second[: 2 * q]),
            second[: 2 * q],
        ],
        axis=0,
    )


def spread_lane(value, lane):
    return jnp.broadcast_to(value[:, lane : lane + 1], value.shape)


def squares(rows):
    high = rows.astype(jnp.bfloat16).astype(jnp.float32)
    rest = rows - high
    middle = rest.astype(jnp.bfloat16).astype(jnp.float32)
    low = rest - middle
    one = jnp.concatenate([high, high, middle, high, low, middle], axis=0).astype(jnp.bfloat16)
    two = jnp.concatenate([high, middle, high, low, high, middle], axis=0).astype(jnp.bfloat16)
    return lax.dot_general(one, two, (((0,), (0,)), ((), ())), preferred_element_type=jnp.float32)


def factor_kernel(scale, meta, own, other, out_ref):
    order = out_ref.shape[0]
    height = 8
    count = order // height
    shape = (height, order)
    is_first = meta[3] == 0
    mine, theirs = (own[...], other[...])
    gram = gram_of_halves(jnp.where(is_first, mine, theirs), jnp.where(is_first, theirs, mine)) * scale
    blocks = [gram[height * b : height * (b + 1), :] for b in range(count)]
    row_ids, col_ids = (ids(shape, 0), ids(shape, 1))
    previous = None
    for p in range(count):
        base = height * p
        rows = [jnp.broadcast_to(blocks[p][j : j + 1, :], shape) for j in range(height)]
        corner = {(i, j): spread_lane(rows[j], base + i) for j in range(height) for i in range(j, height)}
        if previous is not None:
            for done in previous:
                lanes = [spread_lane(done, base + j) for j in range(height)]
                for j in range(height):
                    rows[j] = rows[j] - lanes[j] * done
                    for i in range(j, height):
                        corner[i, j] = corner[i, j] - lanes[i] * lanes[j]
        panel = jnp.zeros(shape, jnp.float32)
        for s in range(height):
            inverse = lax.rsqrt(corner[s, s])
            rows[s] = rows[s] * inverse
            lanes = {j: corner[j, s] * inverse for j in range(s + 1, height)}
            for j in range(s + 1, height):
                for i in range(j, height):
                    corner[i, j] = corner[i, j] - lanes[i] * lanes[j]
                rows[j] = rows[j] - lanes[j] * rows[s]
            panel = jnp.where(row_ids == s, rows[s], panel)
        panel = jnp.where(col_ids >= base + row_ids, panel, 0.0)
        out_ref[base : base + height, :] = panel
        if p + 2 < count:
            update = squares(panel)
            for q in range(p + 2, count):
                blocks[q] = blocks[q] - update[height * q : height * (q + 1), :]
        previous = rows


def shifted(value, axis, steps):
    count = lax.axis_size(axis)
    first, last = (max(0, -steps), min(count, count - steps))
    return lax.ppermute(value, axis, [(source, source + steps) for source in range(first, last)])


def beside(value, steps):
    count = lax.axis_size("tiles")
    pairs = [(source, source + steps) for source in range(count)]
    return lax.ppermute(value, "tiles", [(a, b) for a, b in pairs if 0 <= b < count and a // TGY == b // TGY])


def after(values, *done):
    return lax.optimization_barrier((values, done))[0]


def exchange_rows(messages, grid_rows):
    if len(messages) == 1:
        received = swapped(messages[0], "tiles", TGY)
        return (received, received)
    return (shifted(messages[0], "tiles", -TGY), shifted(messages[1], "tiles", TGY))


def f32(*shape):
    return jax.ShapeDtypeStruct(shape, jnp.float32)


def block(shape, *at):
    return pl.BlockSpec(shape, lambda i: at)


def call(kernel, in_specs, out_specs, out_shape, flops=0, scratch=(), aliases=None):
    return pl.pallas_call(
        kernel,
        grid=(1,),
        in_specs=in_specs,
        out_specs=out_specs,
        out_shape=out_shape,
        scratch_shapes=scratch,
        input_output_aliases=aliases or {},
        compiler_params=pltpu.CompilerParams(vmem_limit_bytes=VMEM_LIMIT),
        cost_estimate=pl.CostEstimate(flops=flops, bytes_accessed=1 << 20, transcendentals=0),
    )


def whole(array):
    zeros = (0,) * array.ndim
    return pl.BlockSpec(array.shape, lambda i: zeros)


def shards(omega, conductance, wet, volume, face_runs):
    vectors, levels, rows, cols = omega.shape
    tiles = lax.axis_size("tiles")
    grid_rows = tiles // TGY
    tile_row = lax.axis_index("tiles") // TGY
    core = lax.axis_index("tiles") % 2
    meta = jnp.stack([tile_row, grid_rows - 1 - tile_row, lax.axis_index("vec"), core]).astype(jnp.int32)
    smem = pl.BlockSpec(memory_space=pltpu.SMEM)
    group = cols // EDGE
    chunks = vectors // group
    directions = 1 if grid_rows == 2 else 2
    kinds = 4
    half = levels // 2

    row_shapes = [f32(group // 2 + (kinds // 2 if c == 0 else 0), levels, rows, cols) for c in range(chunks)]
    row_shapes = [shape for shape in row_shapes for _ in range(directions)]
    packed_shapes = [f32(kinds, levels, rows, cols), f32(chunks + 1, levels, rows, cols)] + row_shapes
    statics, edges, *messages = call(
        functools.partial(pack_kernel, chunks),
        [smem, smem, whole(omega), whole(conductance), whole(wet)],
        [whole(s) for s in packed_shapes],
        packed_shapes,
    )(meta, face_runs, omega, conductance, wet)
    messages = [messages[directions * c : directions * (c + 1)] for c in range(chunks)]
    received = [exchange_rows(messages[0], grid_rows)]
    left = beside(edges, 1)
    right = beside(edges, -1)
    corner_shapes = [f32(chunks + 1, levels // 2, rows, cols)] * directions
    corners = call(
        corner_kernel, [smem, whole(left), whole(right)], [whole(s) for s in corner_shapes], corner_shapes
    )(meta, left, right)
    corners = exchange_rows(corners, grid_rows)
    gates = [(left, right), corners]
    for c in range(1, chunks):
        gate = gates[c - 1] if c <= 2 else received[c - 2]
        received.append(exchange_rows(after(messages[c], *gate), grid_rows))

    def group_specs(c):
        edge = block((1, levels, rows, cols), c, 0, 0, 0)
        corner = block((1, levels // 2, rows, cols), c, 0, 0, 0)
        return [edge, edge, edge, corner, corner]

    around = (edges, left, right, *corners)
    weight_shapes = [f32(7, levels, 2, rows, cols), f32(2, 7, levels, 2, rows, cols)]
    main_weights, strip_weights = call(
        weight_kernel,
        [smem, whole(statics), whole(received[0][0]), whole(received[0][1])] + group_specs(chunks),
        [whole(s) for s in weight_shapes],
        weight_shapes,
    )(meta, statics, *received[0], *around)

    field = None
    kept, sent = ([], [])
    half_shape = f32(group * half * rows, cols)
    for c in range(chunks):
        rims = after(received[c], sent[c - 2]) if c >= 2 else received[c]
        operands = [meta, omega, wet, volume, *rims, *around, main_weights, strip_weights]
        row_block = block((group // 2, levels, rows, cols), 0, 0, 0, 0)
        chunk_block = block((group, levels, rows, cols), c, 0, 0, 0)
        specs = [smem, chunk_block, whole(wet), whole(volume), row_block, row_block] + group_specs(c)
        specs += [whole(main_weights), whole(strip_weights)]
        aliases = {}
        if field is not None:
            aliases = {len(operands): 0}
            operands.append(field)
            specs.append(pl.BlockSpec(memory_space=pl.ANY))
        field, keep, send = call(
            functools.partial(diffuse_kernel, 4),
            specs,
            [chunk_block, whole(half_shape), whole(half_shape)],
            [f32(*omega.shape), half_shape, half_shape],
            flops=4 * 10**9,
            scratch=[pltpu.VMEM((ITERS, levels, 2, rows, cols), jnp.float32), pltpu.VMEM((group, levels, rows, cols), jnp.float32)],
            aliases=aliases,
        )(*operands)
        kept.append(keep)
        sent.append(swapped(send, "vec", 1))

    order = 2 * vectors
    half_gram = f32(3 * order // 8, order)
    mine, theirs = call(
        functools.partial(gram_kernel, chunks, half * rows),
        [smem] + [whole(half_shape)] * (2 * chunks),
        [whole(half_gram)] * 2,
        [half_gram] * 2,
    )(meta, *kept, *sent)
    mine = total_over_chips(mine + swapped(theirs, "tiles", 1))
    total_cells = levels * tiles * rows * cols
    r_factor = call(
        functools.partial(factor_kernel, 1.0 / total_cells),
        [smem, whole(half_gram), whole(half_gram)],
        whole(f32(order, order)),
        f32(order, order),
    )(meta, mine, swapped(mine, "tiles", 1))
    return (field, r_factor)


def solution(mesh):
    in_specs = (
        P("vec", None, "tiles", None),
        P(None, None, "tiles", None),
        P("tiles", None),
        P("tiles", None),
        P("tiles", None),
    )
    out_specs = (P("vec", None, "tiles", None), P())
    return jax.shard_map(shards, mesh=mesh, in_specs=in_specs, out_specs=out_specs, check_vma=False)
```

```python
import functools
import jax
import jax.numpy as jnp
from jax import lax
from jax.experimental import pallas as pl
from jax.experimental.pallas import tpu as pltpu
from jax.sharding import PartitionSpec as P

TGY = 8
ITERS = 4
EDGE = 2 * ITERS
VMEM_LIMIT = 32 * 1024 * 1024
EDGE_LIMIT = 63 * 1024 * 1024 + 256 * 1024
MAIN, SLOT = (0, 1)


def ids(shape, axis):
    return lax.broadcasted_iota(jnp.int32, shape, axis)


def turn(value, steps, axis):
    size = value.shape[axis]
    steps = steps % size
    return value if steps == 0 else pltpu.roll(value, steps, axis)


def low_half(shape):
    return ids(shape, 0) < ITERS


def left_lanes(shape):
    return ids(shape, 1) % EDGE < ITERS


def first_pair(a, b):
    return jnp.where(low_half(a.shape), a, turn(b, ITERS, 0))


def last_pair(a, b):
    return jnp.where(low_half(a.shape), turn(a, ITERS, 0), b)


def slots(below, above):
    low = low_half(below.shape)
    return (
        jnp.where(low, below, turn(above, ITERS, 0)),
        jnp.where(low, turn(below, ITERS, 0), above),
    )


def store_pair(outs, index, a, b, is_first_row):
    if len(outs) == 1:
        outs[0][index] = jnp.where(is_first_row, last_pair(a, b), first_pair(a, b))
    else:
        outs[0][index] = first_pair(a, b)
        outs[1][index] = last_pair(a, b)


def add_edge(acc, value, place):
    lanes = ids(value.shape, 1) // EDGE
    moved = turn(value, EDGE * place + ITERS, 1)
    return moved if acc is None else jnp.where(lanes == place, moved, acc)


def prev_row(part, other):
    return jnp.where(ids(part.shape, 0) == 0, turn(other, 1, 0), turn(part, 1, 0))


def next_row(part, other):
    last = part.shape[0] - 1
    return jnp.where(ids(part.shape, 0) == last, turn(other, -1, 0), turn(part, -1, 0))


def prev_col(part, rim):
    return jnp.where(ids(part.shape, 1) == 0, rim, turn(part, 1, 1))


def next_col(part, rim):
    last = part.shape[1] - 1
    return jnp.where(ids(part.shape, 1) == last, rim, turn(part, -1, 1))


def strips(edges, rims):
    left = left_lanes(edges.shape)
    return (jnp.where(left, rims, edges), jnp.where(left, edges, rims))


def crossing(left_strip, right_strip):
    lanes = ids(left_strip.shape, 1) % EDGE
    return jnp.where(lanes == ITERS - 1, turn(right_strip, -1, 1), turn(left_strip, 1, 1))


def rim_of(cross, place):
    return turn(cross, -(EDGE * place + ITERS), 1)


def edge_kernel(runs, omega, conductance, wet, static_out, edge_out):
    levels, rows, cols = omega.shape[1:]
    shape = (rows, cols)
    row_ids, col_ids = (ids(shape, 0), ids(shape, 1))
    wet_cells = wet[...].astype(jnp.float32)
    open_x = (col_ids >= runs[0, 0]) & (col_ids < runs[0, 0] + runs[0, 1])
    open_y = (row_ids >= runs[0, 2]) & (row_ids < runs[0, 2] + runs[0, 3])
    keep_x = (row_ids > 0) | open_x
    keep_y = (col_ids > 0) | open_y
    group = cols // EDGE
    chunks = omega.shape[0] // group
    for level in range(levels):
        statics = [
            jnp.where(keep_x, conductance[0, level], 0.0),
            jnp.where(keep_y, conductance[1, level], 0.0),
            conductance[2, level] if level else jnp.zeros(shape, jnp.float32),
            wet_cells,
        ]
        edge = None
        for kind, value in enumerate(statics):
            static_out[kind, level] = value
            edge = add_edge(edge, value, kind)
        edge_out[chunks, level] = edge
        for chunk in range(chunks):
            edge = None
            for place in range(group):
                edge = add_edge(edge, omega[chunk * group + place, level] * wet_cells, place)
            edge_out[chunk, level] = edge


def row_kernel(meta, statics, omega, wet, *row_outs):
    kinds, levels, rows, cols = statics.shape
    group = cols // EDGE
    chunks = omega.shape[0] // group
    directions = len(row_outs) // chunks
    is_first_row = meta[0] == 0
    wet_cells = wet[...].astype(jnp.float32)
    for level in range(levels):
        for kind in range(0, kinds, 2):
            at = (group // 2 + kind // 2, level)
            store_pair(row_outs[:directions], at, statics[kind, level], statics[kind + 1, level], is_first_row)
        for chunk in range(chunks):
            outs = row_outs[directions * chunk : directions * (chunk + 1)]
            for pair in range(group // 2):
                start = [omega[chunk * group + 2 * pair + i, level] * wet_cells for i in range(2)]
                store_pair(outs, (pair, level), start[0], start[1], is_first_row)


def corner_kernel(meta, left, right, *outs):
    is_first_row = meta[0] == 0
    groups, levels, rows, cols = left.shape
    take = left_lanes((rows, cols))
    for g in range(groups):
        for level in range(0, levels, 2):
            pair = [jnp.where(take, left[g, level + i], right[g, level + i]) for i in range(2)]
            store_pair(outs, (g, level // 2), pair[0], pair[1], is_first_row)


def rims_of_group(left, right, corner_below, corner_above):
    levels, rows, cols = left.shape[1:]
    take = left_lanes((rows, cols))
    rims = [[jnp.where(take, left[0, level], right[0, level]), None] for level in range(levels)]
    for level in range(0, levels, 2):
        pair = slots(corner_below[0, level // 2], corner_above[0, level // 2])
        rims[level][SLOT], rims[level + 1][SLOT] = pair
    return rims


def weight_kernel(meta, statics, below, above, edges, left, right, corner_below, corner_above, main_out, strip_out):
    kinds, levels, rows, cols = statics.shape
    shape = (rows, cols)
    low = low_half(shape)
    valid = (low & (meta[1] > 0)) | (jnp.logical_not(low) & (meta[0] > 0))
    first = below.shape[0] - kinds // 2
    rims = rims_of_group(left, right, corner_below, corner_above)
    field = [[[statics[kind, level], None] for level in range(levels)] for kind in range(kinds)]
    for level in range(levels):
        for kind in range(0, kinds, 2):
            pair = slots(below[first + kind // 2, level], above[first + kind // 2, level])
            for i in range(2):
                field[kind + i][level][SLOT] = jnp.where(valid, pair[i], 0.0)
    width = cols // EDGE
    lanes = ids(shape, 1) // EDGE

    def spread(strip, kind):
        value = jnp.where(lanes == 0, turn(strip, -EDGE * kind, 1), 0.0)
        span = 1
        while span < width:
            value = value + turn(value, EDGE * span, 1)
            span *= 2
        return value

    side = [[[[None, None] for _ in range(levels)] for _ in range(kinds)] for _ in range(2)]
    cross = [[None, None] for _ in range(levels)]
    for level in range(levels):
        for part in range(2):
            edge = edges[0, level] if part == MAIN else None
            if part == SLOT:
                for kind in range(kinds):
                    edge = add_edge(edge, field[kind][level][SLOT], kind)
            rim = rims[level][part]
            if part == SLOT:
                rim = jnp.where(valid, rim, 0.0)
            pair = strips(edge, rim)
            cross[level][part] = crossing(pair[0], pair[1])
            for s in range(2):
                for kind in range(kinds):
                    side[s][kind][level][part] = spread(pair[s], kind)

    def emit(out, values, after_of):
        for level in range(levels):
            for part in range(2):
                cond_x, cond_y, cond_z, wet = (values[kind][level][part] for kind in range(kinds))
                faces = [
                    cond_x,
                    next_row(cond_x, values[0][level][1 - part]),
                    cond_y,
                    after_of(cond_y, level, part),
                    cond_z,
                    values[2][level + 1][part] if level + 1 < levels else jnp.zeros(shape, jnp.float32),
                ]
                total = faces[0]
                for face in faces[1:]:
                    total = total + face
                out[0, level, part] = wet * (1.0 - total)
                for index, face in enumerate(faces):
                    out[index + 1, level, part] = wet * face

    emit(main_out, field, lambda cond, level, part: next_col(cond, rim_of(cross[level][part], 1)))
    for s in range(2):
        emit(strip_out.at[s], side[s], lambda cond, level, part: turn(cond, -1, 1))


def one_pass(state, weight, parts, rim_at):
    levels = len(state)
    result = [[None, None] for _ in range(levels)]
    for level in range(levels):
        for part in parts:
            value, other = (state[level][part], state[level][1 - part])
            rim = rim_at(level, part)
            before = turn(value, 1, 1) if rim is None else prev_col(value, rim)
            after = turn(value, -1, 1) if rim is None else next_col(value, rim)
            total = weight(0, level, part) * value
            total = total + weight(1, level, part) * prev_row(value, other)
            total = total + weight(2, level, part) * next_row(value, other)
            total = total + weight(3, level, part) * before
            total = total + weight(4, level, part) * after
            if level > 0:
                total = total + weight(5, level, part) * state[level - 1][part]
            if level < levels - 1:
                total = total + weight(6, level, part) * state[level + 1][part]
            result[level][part] = total
    return result


def diffuse_kernel(
    batch, meta, omega, wet, volume, below, above, edges, left, right, corner_below, corner_above,
    main_weights, strip_weights, *rest
):
    field_out, keep_out, send_out, cross_scratch, slot_scratch = rest[-5:]
    group, levels, rows, cols = omega.shape
    shape = (rows, cols)
    wet_cells = wet[...].astype(jnp.float32)
    root = jnp.sqrt(volume[...])
    half = levels // 2
    keeps_low = meta[2] == 0
    rims = rims_of_group(left, right, corner_below, corner_above)
    slot_edges = [None] * levels
    for level in range(levels):
        for pair in range(group // 2):
            two = slots(below[pair, level], above[pair, level])
            for i in range(2):
                slot_scratch[2 * pair + i, level] = two[i]
                slot_edges[level] = add_edge(slot_edges[level], two[i], 2 * pair + i)
    state = [[[None, None] for _ in range(levels)] for _ in range(2)]
    for level in range(levels):
        for part in range(2):
            edge = edges[0, level] if part == MAIN else slot_edges[level]
            pair = strips(edge, rims[level][part])
            for s in range(2):
                state[s][level][part] = pair[s]
    for sweep in range(ITERS):
        for level in range(levels):
            for part in range(2):
                cross_scratch[sweep, level, part] = crossing(state[0][level][part], state[1][level][part])
        if sweep < ITERS - 1:
            for s in range(2):
                state[s] = one_pass(
                    state[s], lambda n, level, part: strip_weights[s, n, level, part], (MAIN, SLOT), lambda level, part: None
                )

    for first in range(0, group, batch):
        fields = []
        for place in range(first, first + batch):
            fields.append([[omega[place, level] * wet_cells, slot_scratch[place, level]] for level in range(levels)])
        for sweep in range(ITERS):
            parts = (MAIN, SLOT) if sweep < ITERS - 1 else (MAIN,)
            for i in range(batch):
                fields[i] = one_pass(
                    fields[i],
                    lambda n, level, part: main_weights[n, level, part],
                    parts,
                    lambda level, part: rim_of(cross_scratch[sweep, level, part], first + i),
                )
        for i in range(batch):
            scaled = []
            for level in range(levels):
                value = fields[i][level][MAIN]
                field_out[first + i, level] = value
                scaled.append(value * root)
            for level in range(half):
                at = ((first + i) * half + level) * rows
                keep_out[at : at + rows, :] = jnp.where(keeps_low, scaled[level], scaled[half + level])
                send_out[at : at + rows, :] = jnp.where(keeps_low, scaled[half + level], scaled[level])


def gram_kernel(chunks, slices, meta, *refs):
    mine, theirs = refs[-2:]
    sources = refs[:-2]
    stride = slices
    group = sources[0].shape[0] // stride
    order = group * len(sources)
    cols = sources[0].shape[1]
    exact = jnp.zeros((order, order), jnp.float32)
    cross = jnp.zeros((order, order), jnp.float32)
    for at in range(0, slices, 2):
        columns = []
        for i in range(2):
            columns.append(jnp.concatenate([ref[pl.ds(at + i, group, stride), :] for ref in sources], axis=0))
        values = jnp.concatenate(columns, axis=1)
        high = values.astype(jnp.bfloat16)
        rest = (values - high.astype(jnp.float32)).astype(jnp.bfloat16)
        dims = (((1,), (1,)), ((), ()))
        exact = exact + lax.dot_general(high, high, dims, preferred_element_type=jnp.float32)
        cross = cross + lax.dot_general(high, rest, dims, preferred_element_type=jnp.float32)
    gram = exact + (cross + cross.T)
    moved = turn(turn(gram, order // 2, 0), order // 2, 1)
    first, second = halves_of_gram(jnp.where(meta[2] == 0, gram, moved))
    is_first = meta[3] == 0
    mine[...] = jnp.where(is_first, first, second)
    theirs[...] = jnp.where(is_first, second, first)


def swapped(value, axis, bit):
    count = lax.axis_size(axis)
    return lax.ppermute(value, axis, [(source, source ^ bit) for source in range(count)])


def total_over_chips(value):
    for axis, bit in (("tiles", 2), ("vec", 1)):
        while bit < lax.axis_size(axis):
            value = value + swapped(value, axis, bit)
            bit *= 2
    return value


def fold(a, b):
    half = a.shape[1] // 2
    return jnp.where(ids(a.shape, 1) < half, a, b)


def flip(value):
    return turn(value, value.shape[1] // 2, 1)


def halves_of_gram(gram):
    q = gram.shape[0] // 8
    first = [fold(gram[: 2 * q], flip(gram[2 * q : 4 * q])), fold(flip(gram[:q]), gram[q : 2 * q])]
    second = [fold(flip(gram[4 * q : 6 * q]), gram[6 * q :]), fold(flip(gram[2 * q : 3 * q]), gram[3 * q : 4 * q])]
    return (jnp.concatenate(first, axis=0), jnp.concatenate(second, axis=0))


def gram_of_halves(first, second):
    q = first.shape[0] // 3
    return jnp.concatenate(
        [
            fold(first[:q], flip(first[2 * q :])),
            fold(first[q : 2 * q], first[2 * q :]),
            fold(flip(first[:q]), flip(second[2 * q :])),
            fold(flip(first[q : 2 * q]), second[2 * q :]),
            flip(second[: 2 * q]),
            second[: 2 * q],
        ],
        axis=0,
    )


def spread_lane(value, lane):
    return jnp.broadcast_to(value[:, lane : lane + 1], value.shape)


def squares(rows):
    high = rows.astype(jnp.bfloat16).astype(jnp.float32)
    rest = rows - high
    middle = rest.astype(jnp.bfloat16).astype(jnp.float32)
    low = rest - middle
    one = jnp.concatenate([high, high, middle, high, low, middle], axis=0).astype(jnp.bfloat16)
    two = jnp.concatenate([high, middle, high, low, high, middle], axis=0).astype(jnp.bfloat16)
    return lax.dot_general(one, two, (((0,), (0,)), ((), ())), preferred_element_type=jnp.float32)


def factor_kernel(scale, meta, own, other, out_ref):
    order = out_ref.shape[0]
    height = 8
    count = order // height
    shape = (height, order)
    is_first = meta[3] == 0
    mine, theirs = (own[...], other[...])
    gram = gram_of_halves(jnp.where(is_first, mine, theirs), jnp.where(is_first, theirs, mine)) * scale
    blocks = [gram[height * b : height * (b + 1), :] for b in range(count)]
    row_ids, col_ids = (ids(shape, 0), ids(shape, 1))
    previous = None
    for p in range(count):
        base = height * p
        rows = [jnp.broadcast_to(blocks[p][j : j + 1, :], shape) for j in range(height)]
        corner = {(i, j): spread_lane(rows[j], base + i) for j in range(height) for i in range(j, height)}
        if previous is not None:
            for done in previous:
                lanes = [spread_lane(done, base + j) for j in range(height)]
                for j in range(height):
                    rows[j] = rows[j] - lanes[j] * done
                    for i in range(j, height):
                        corner[i, j] = corner[i, j] - lanes[i] * lanes[j]
        panel = jnp.zeros(shape, jnp.float32)
        for s in range(height):
            inverse = lax.rsqrt(corner[s, s])
            rows[s] = rows[s] * inverse
            lanes = {j: corner[j, s] * inverse for j in range(s + 1, height)}
            for j in range(s + 1, height):
                for i in range(j, height):
                    corner[i, j] = corner[i, j] - lanes[i] * lanes[j]
                rows[j] = rows[j] - lanes[j] * rows[s]
            panel = jnp.where(row_ids == s, rows[s], panel)
        panel = jnp.where(col_ids >= base + row_ids, panel, 0.0)
        out_ref[base : base + height, :] = panel
        if p + 2 < count:
            update = squares(panel)
            for q in range(p + 2, count):
                blocks[q] = blocks[q] - update[height * q : height * (q + 1), :]
        previous = rows


def shifted(value, axis, steps):
    count = lax.axis_size(axis)
    first, last = (max(0, -steps), min(count, count - steps))
    return lax.ppermute(value, axis, [(source, source + steps) for source in range(first, last)])


def beside(value, steps):
    count = lax.axis_size("tiles")
    pairs = [(source, source + steps) for source in range(count)]
    return lax.ppermute(value, "tiles", [(a, b) for a, b in pairs if 0 <= b < count and a // TGY == b // TGY])


def after(values, *done):
    return lax.optimization_barrier((values, done))[0]


def exchange_rows(messages, grid_rows):
    if len(messages) == 1:
        received = swapped(messages[0], "tiles", TGY)
        return (received, received)
    return (shifted(messages[0], "tiles", -TGY), shifted(messages[1], "tiles", TGY))


def f32(*shape):
    return jax.ShapeDtypeStruct(shape, jnp.float32)


def block(shape, *at):
    return pl.BlockSpec(shape, lambda i: at)


def call(kernel, in_specs, out_specs, out_shape, flops=0, scratch=(), aliases=None, limit=VMEM_LIMIT):
    return pl.pallas_call(
        kernel,
        grid=(1,),
        in_specs=in_specs,
        out_specs=out_specs,
        out_shape=out_shape,
        scratch_shapes=scratch,
        input_output_aliases=aliases or {},
        compiler_params=pltpu.CompilerParams(vmem_limit_bytes=limit),
        cost_estimate=pl.CostEstimate(flops=flops, bytes_accessed=1 << 20, transcendentals=0),
    )


def whole(array):
    zeros = (0,) * array.ndim
    return pl.BlockSpec(array.shape, lambda i: zeros)


def shards(omega, conductance, wet, volume, face_runs):
    vectors, levels, rows, cols = omega.shape
    tiles = lax.axis_size("tiles")
    grid_rows = tiles // TGY
    tile_row = lax.axis_index("tiles") // TGY
    core = lax.axis_index("tiles") % 2
    meta = jnp.stack([tile_row, grid_rows - 1 - tile_row, lax.axis_index("vec"), core]).astype(jnp.int32)
    smem = pl.BlockSpec(memory_space=pltpu.SMEM)
    group = cols // EDGE
    chunks = vectors // group
    directions = 1 if grid_rows == 2 else 2
    kinds = 4
    half = levels // 2

    row_shapes = [f32(group // 2 + (kinds // 2 if c == 0 else 0), levels, rows, cols) for c in range(chunks)]
    row_shapes = [shape for shape in row_shapes for _ in range(directions)]
    edge_shapes = [f32(kinds, levels, rows, cols), f32(chunks + 1, levels, rows, cols)]
    statics, edges = call(
        edge_kernel,
        [smem, whole(omega), whole(conductance), whole(wet)],
        [whole(s) for s in edge_shapes],
        edge_shapes,
        limit=EDGE_LIMIT,
    )(face_runs, omega, conductance, wet)
    left = beside(edges, 1)
    right = beside(edges, -1)
    messages = call(
        row_kernel,
        [smem, whole(statics), whole(omega), whole(wet)],
        [whole(s) for s in row_shapes],
        row_shapes,
        flops=10**9,
    )(meta, statics, omega, wet)
    messages = [messages[directions * c : directions * (c + 1)] for c in range(chunks)]
    received = [exchange_rows(after(messages[0], left, right), grid_rows)]
    corner_shapes = [f32(chunks + 1, levels // 2, rows, cols)] * directions
    corners = call(
        corner_kernel, [smem, whole(left), whole(right)], [whole(s) for s in corner_shapes], corner_shapes
    )(meta, left, right)
    corners = exchange_rows(corners, grid_rows)
    for c in range(1, chunks):
        gate = corners if c == 1 else received[c - 2]
        received.append(exchange_rows(after(messages[c], *gate), grid_rows))

    def group_specs(c):
        edge = block((1, levels, rows, cols), c, 0, 0, 0)
        corner = block((1, levels // 2, rows, cols), c, 0, 0, 0)
        return [edge, edge, edge, corner, corner]

    around = (edges, left, right, *corners)
    weight_shapes = [f32(7, levels, 2, rows, cols), f32(2, 7, levels, 2, rows, cols)]
    main_weights, strip_weights = call(
        weight_kernel,
        [smem, whole(statics), whole(received[0][0]), whole(received[0][1])] + group_specs(chunks),
        [whole(s) for s in weight_shapes],
        weight_shapes,
    )(meta, statics, *received[0], *around)

    field = None
    kept, sent = ([], [])
    half_shape = f32(group * half * rows, cols)
    for c in range(chunks):
        rims = after(received[c], sent[c - 2]) if c >= 2 else received[c]
        operands = [meta, omega, wet, volume, *rims, *around, main_weights, strip_weights]
        row_block = block((group // 2, levels, rows, cols), 0, 0, 0, 0)
        chunk_block = block((group, levels, rows, cols), c, 0, 0, 0)
        specs = [smem, chunk_block, whole(wet), whole(volume), row_block, row_block] + group_specs(c)
        specs += [whole(main_weights), whole(strip_weights)]
        aliases = {}
        if field is not None:
            aliases = {len(operands): 0}
            operands.append(field)
            specs.append(pl.BlockSpec(memory_space=pl.ANY))
        field, keep, send = call(
            functools.partial(diffuse_kernel, 4),
            specs,
            [chunk_block, whole(half_shape), whole(half_shape)],
            [f32(*omega.shape), half_shape, half_shape],
            flops=4 * 10**9,
            scratch=[pltpu.VMEM((ITERS, levels, 2, rows, cols), jnp.float32), pltpu.VMEM((group, levels, rows, cols), jnp.float32)],
            aliases=aliases,
        )(*operands)
        kept.append(keep)
        sent.append(swapped(send, "vec", 1))

    order = 2 * vectors
    half_gram = f32(3 * order // 8, order)
    mine, theirs = call(
        functools.partial(gram_kernel, chunks, half * rows),
        [smem] + [whole(half_shape)] * (2 * chunks),
        [whole(half_gram)] * 2,
        [half_gram] * 2,
    )(meta, *kept, *sent)
    mine = total_over_chips(mine + swapped(theirs, "tiles", 1))
    total_cells = levels * tiles * rows * cols
    r_factor = call(
        functools.partial(factor_kernel, 1.0 / total_cells),
        [smem, whole(half_gram), whole(half_gram)],
        whole(f32(order, order)),
        f32(order, order),
    )(meta, mine, swapped(mine, "tiles", 1))
    return (field, r_factor)


def solution(mesh):
    in_specs = (
        P("vec", None, "tiles", None),
        P(None, None, "tiles", None),
        P("tiles", None),
        P("tiles", None),
        P("tiles", None),
    )
    out_specs = (P("vec", None, "tiles", None), P())
    return jax.shard_map(shards, mesh=mesh, in_specs=in_specs, out_specs=out_specs, check_vma=False)
```

```python
import functools
import jax
import jax.numpy as jnp
from jax import lax
from jax.experimental import pallas as pl
from jax.experimental.pallas import tpu as pltpu
from jax.sharding import PartitionSpec as P

TGY = 8
ITERS = 4
EDGE = 2 * ITERS
VMEM_LIMIT = 32 * 1024 * 1024
MAIN, SLOT = (0, 1)


def ids(shape, axis):
    return lax.broadcasted_iota(jnp.int32, shape, axis)


def turn(value, steps, axis):
    size = value.shape[axis]
    steps = steps % size
    return value if steps == 0 else pltpu.roll(value, steps, axis)


def low_half(shape):
    return ids(shape, 0) < ITERS


def left_lanes(shape):
    return ids(shape, 1) % EDGE < ITERS


def first_pair(a, b):
    return jnp.where(low_half(a.shape), a, turn(b, ITERS, 0))


def last_pair(a, b):
    return jnp.where(low_half(a.shape), turn(a, ITERS, 0), b)


def slots(below, above):
    low = low_half(below.shape)
    return (
        jnp.where(low, below, turn(above, ITERS, 0)),
        jnp.where(low, turn(below, ITERS, 0), above),
    )


def store_pair(outs, index, a, b, is_first_row):
    if len(outs) == 1:
        outs[0][index] = jnp.where(is_first_row, last_pair(a, b), first_pair(a, b))
    else:
        outs[0][index] = first_pair(a, b)
        outs[1][index] = last_pair(a, b)


def add_edge(acc, value, place):
    lanes = ids(value.shape, 1) // EDGE
    moved = turn(value, EDGE * place + ITERS, 1)
    return moved if acc is None else jnp.where(lanes == place, moved, acc)


def prev_row(part, other):
    return jnp.where(ids(part.shape, 0) == 0, turn(other, 1, 0), turn(part, 1, 0))


def next_row(part, other):
    last = part.shape[0] - 1
    return jnp.where(ids(part.shape, 0) == last, turn(other, -1, 0), turn(part, -1, 0))


def prev_col(part, rim):
    return jnp.where(ids(part.shape, 1) == 0, rim, turn(part, 1, 1))


def next_col(part, rim):
    last = part.shape[1] - 1
    return jnp.where(ids(part.shape, 1) == last, rim, turn(part, -1, 1))


def strips(edges, rims):
    left = left_lanes(edges.shape)
    return (jnp.where(left, rims, edges), jnp.where(left, edges, rims))


def crossing(left_strip, right_strip):
    lanes = ids(left_strip.shape, 1) % EDGE
    return jnp.where(lanes == ITERS - 1, turn(right_strip, -1, 1), turn(left_strip, 1, 1))


def rim_of(cross, place):
    return turn(cross, -(EDGE * place + ITERS), 1)


def pack_kernel(chunks, meta, runs, omega, conductance, wet, static_out, edge_out, *row_outs):
    directions = len(row_outs) // chunks
    levels, rows, cols = omega.shape[1:]
    shape = (rows, cols)
    is_first_row = meta[0] == 0
    row_ids, col_ids = (ids(shape, 0), ids(shape, 1))
    wet_cells = wet[...].astype(jnp.float32)
    open_x = (col_ids >= runs[0, 0]) & (col_ids < runs[0, 0] + runs[0, 1])
    open_y = (row_ids >= runs[0, 2]) & (row_ids < runs[0, 2] + runs[0, 3])
    keep_x = (row_ids > 0) | open_x
    keep_y = (col_ids > 0) | open_y
    statics = []
    for level in range(levels):
        statics.append(
            [
                jnp.where(keep_x, conductance[0, level], 0.0),
                jnp.where(keep_y, conductance[1, level], 0.0),
                conductance[2, level] if level else jnp.zeros(shape, jnp.float32),
                wet_cells,
            ]
        )
    kinds = len(statics[0])
    group = cols // EDGE
    for level in range(levels):
        edge = None
        for kind in range(kinds):
            static_out[kind, level] = statics[level][kind]
            edge = add_edge(edge, statics[level][kind], kind)
        edge_out[chunks, level] = edge
        for kind in range(0, kinds, 2):
            outs = row_outs[:directions]
            store_pair(outs, (group // 2 + kind // 2, level), statics[level][kind], statics[level][kind + 1], is_first_row)
        for chunk in range(chunks):
            outs = row_outs[directions * chunk : directions * (chunk + 1)]
            edge = None
            for pair in range(group // 2):
                start = [omega[chunk * group + 2 * pair + i, level] * wet_cells for i in range(2)]
                edge = add_edge(edge, start[0], 2 * pair)
                edge = add_edge(edge, start[1], 2 * pair + 1)
                store_pair(outs, (pair, level), start[0], start[1], is_first_row)
            edge_out[chunk, level] = edge


def corner_kernel(meta, left, right, *outs):
    is_first_row = meta[0] == 0
    groups, levels, rows, cols = left.shape
    take = left_lanes((rows, cols))
    for g in range(groups):
        for level in range(0, levels, 2):
            pair = [jnp.where(take, left[g, level + i], right[g, level + i]) for i in range(2)]
            store_pair(outs, (g, level // 2), pair[0], pair[1], is_first_row)


def rims_of_group(left, right, corner_below, corner_above):
    levels, rows, cols = left.shape[1:]
    take = left_lanes((rows, cols))
    rims = [[jnp.where(take, left[0, level], right[0, level]), None] for level in range(levels)]
    for level in range(0, levels, 2):
        pair = slots(corner_below[0, level // 2], corner_above[0, level // 2])
        rims[level][SLOT], rims[level + 1][SLOT] = pair
    return rims


def weight_kernel(meta, statics, below, above, edges, left, right, corner_below, corner_above, main_out, strip_out):
    kinds, levels, rows, cols = statics.shape
    shape = (rows, cols)
    low = low_half(shape)
    valid = (low & (meta[1] > 0)) | (jnp.logical_not(low) & (meta[0] > 0))
    first = below.shape[0] - kinds // 2
    rims = rims_of_group(left, right, corner_below, corner_above)
    field = [[[statics[kind, level], None] for level in range(levels)] for kind in range(kinds)]
    for level in range(levels):
        for kind in range(0, kinds, 2):
            pair = slots(below[first + kind // 2, level], above[first + kind // 2, level])
            for i in range(2):
                field[kind + i][level][SLOT] = jnp.where(valid, pair[i], 0.0)
    width = cols // EDGE
    lanes = ids(shape, 1) // EDGE

    def spread(strip, kind):
        value = jnp.where(lanes == 0, turn(strip, -EDGE * kind, 1), 0.0)
        span = 1
        while span < width:
            value = value + turn(value, EDGE * span, 1)
            span *= 2
        return value

    side = [[[[None, None] for _ in range(levels)] for _ in range(kinds)] for _ in range(2)]
    cross = [[None, None] for _ in range(levels)]
    for level in range(levels):
        for part in range(2):
            edge = edges[0, level] if part == MAIN else None
            if part == SLOT:
                for kind in range(kinds):
                    edge = add_edge(edge, field[kind][level][SLOT], kind)
            rim = rims[level][part]
            if part == SLOT:
                rim = jnp.where(valid, rim, 0.0)
            pair = strips(edge, rim)
            cross[level][part] = crossing(pair[0], pair[1])
            for s in range(2):
                for kind in range(kinds):
                    side[s][kind][level][part] = spread(pair[s], kind)

    def emit(out, values, after_of):
        for level in range(levels):
            for part in range(2):
                cond_x, cond_y, cond_z, wet = (values[kind][level][part] for kind in range(kinds))
                faces = [
                    cond_x,
                    next_row(cond_x, values[0][level][1 - part]),
                    cond_y,
                    after_of(cond_y, level, part),
                    cond_z,
                    values[2][level + 1][part] if level + 1 < levels else jnp.zeros(shape, jnp.float32),
                ]
                total = faces[0]
                for face in faces[1:]:
                    total = total + face
                out[0, level, part] = wet * (1.0 - total)
                for index, face in enumerate(faces):
                    out[index + 1, level, part] = wet * face

    emit(main_out, field, lambda cond, level, part: next_col(cond, rim_of(cross[level][part], 1)))
    for s in range(2):
        emit(strip_out.at[s], side[s], lambda cond, level, part: turn(cond, -1, 1))


def one_pass(state, weight, parts, rim_at):
    levels = len(state)
    result = [[None, None] for _ in range(levels)]
    for level in range(levels):
        for part in parts:
            value, other = (state[level][part], state[level][1 - part])
            rim = rim_at(level, part)
            before = turn(value, 1, 1) if rim is None else prev_col(value, rim)
            after = turn(value, -1, 1) if rim is None else next_col(value, rim)
            total = weight(0, level, part) * value
            total = total + weight(1, level, part) * prev_row(value, other)
            total = total + weight(2, level, part) * next_row(value, other)
            total = total + weight(3, level, part) * before
            total = total + weight(4, level, part) * after
            if level > 0:
                total = total + weight(5, level, part) * state[level - 1][part]
            if level < levels - 1:
                total = total + weight(6, level, part) * state[level + 1][part]
            result[level][part] = total
    return result


def diffuse_kernel(
    batch, meta, omega, wet, volume, below, above, edges, left, right, corner_below, corner_above,
    main_weights, strip_weights, *rest
):
    field_out, keep_out, send_out, cross_scratch, slot_scratch = rest[-5:]
    group, levels, rows, cols = omega.shape
    shape = (rows, cols)
    wet_cells = wet[...].astype(jnp.float32)
    root = jnp.sqrt(volume[...])
    half = levels // 2
    keeps_low = meta[2] == 0
    rims = rims_of_group(left, right, corner_below, corner_above)
    slot_edges = [None] * levels
    for level in range(levels):
        for pair in range(group // 2):
            two = slots(below[pair, level], above[pair, level])
            for i in range(2):
                slot_scratch[2 * pair + i, level] = two[i]
                slot_edges[level] = add_edge(slot_edges[level], two[i], 2 * pair + i)
    state = [[[None, None] for _ in range(levels)] for _ in range(2)]
    for level in range(levels):
        for part in range(2):
            edge = edges[0, level] if part == MAIN else slot_edges[level]
            pair = strips(edge, rims[level][part])
            for s in range(2):
                state[s][level][part] = pair[s]
    for sweep in range(ITERS):
        for level in range(levels):
            for part in range(2):
                cross_scratch[sweep, level, part] = crossing(state[0][level][part], state[1][level][part])
        if sweep < ITERS - 1:
            for s in range(2):
                state[s] = one_pass(
                    state[s], lambda n, level, part: strip_weights[s, n, level, part], (MAIN, SLOT), lambda level, part: None
                )

    for first in range(0, group, batch):
        fields = []
        for place in range(first, first + batch):
            fields.append([[omega[place, level] * wet_cells, slot_scratch[place, level]] for level in range(levels)])
        for sweep in range(ITERS):
            parts = (MAIN, SLOT) if sweep < ITERS - 1 else (MAIN,)
            for i in range(batch):
                fields[i] = one_pass(
                    fields[i],
                    lambda n, level, part: main_weights[n, level, part],
                    parts,
                    lambda level, part: rim_of(cross_scratch[sweep, level, part], first + i),
                )
        for i in range(batch):
            scaled = []
            for level in range(levels):
                value = fields[i][level][MAIN]
                field_out[first + i, level] = value
                scaled.append(value * root)
            for level in range(half):
                at = ((first + i) * half + level) * rows
                keep_out[at : at + rows, :] = jnp.where(keeps_low, scaled[level], scaled[half + level])
                send_out[at : at + rows, :] = jnp.where(keeps_low, scaled[half + level], scaled[level])


def gram_kernel(chunks, slices, meta, *refs):
    out = refs[-1]
    sources = refs[:-1]
    stride = slices
    group = sources[0].shape[0] // stride
    order = group * len(sources)
    cols = sources[0].shape[1]
    exact = jnp.zeros((order, order), jnp.float32)
    cross = jnp.zeros((order, order), jnp.float32)
    for at in range(0, slices, 2):
        columns = []
        for i in range(2):
            columns.append(jnp.concatenate([ref[pl.ds(at + i, group, stride), :] for ref in sources], axis=0))
        values = jnp.concatenate(columns, axis=1)
        high = values.astype(jnp.bfloat16)
        rest = (values - high.astype(jnp.float32)).astype(jnp.bfloat16)
        dims = (((1,), (1,)), ((), ()))
        exact = exact + lax.dot_general(high, high, dims, preferred_element_type=jnp.float32)
        cross = cross + lax.dot_general(high, rest, dims, preferred_element_type=jnp.float32)
    gram = exact + (cross + cross.T)
    moved = turn(turn(gram, order // 2, 0), order // 2, 1)
    out[...] = jnp.where(meta[2] == 0, gram, moved)


def swapped(value, axis, bit):
    count = lax.axis_size(axis)
    return lax.ppermute(value, axis, [(source, source ^ bit) for source in range(count)])


def total_over_mesh(value):
    axes = ("tiles", "vec")
    devices = lax.axis_size("tiles") * lax.axis_size("vec")
    rows, cols = value.shape
    piece = (rows // devices, cols) if rows % devices == 0 else (1, value.size // devices)
    parts = lax.all_to_all(value.reshape((devices,) + piece), axes, 0, 0, tiled=True)
    summed = jnp.broadcast_to(jnp.sum(parts, axis=0, keepdims=True), (devices,) + piece)
    return lax.all_to_all(summed, axes, 0, 0, tiled=True).reshape(value.shape)


def spread_lane(value, lane):
    return jnp.broadcast_to(value[:, lane : lane + 1], value.shape)


def squares(rows):
    high = rows.astype(jnp.bfloat16).astype(jnp.float32)
    rest = rows - high
    middle = rest.astype(jnp.bfloat16).astype(jnp.float32)
    low = rest - middle
    one = jnp.concatenate([high, high, middle, high, low, middle], axis=0).astype(jnp.bfloat16)
    two = jnp.concatenate([high, middle, high, low, high, middle], axis=0).astype(jnp.bfloat16)
    return lax.dot_general(one, two, (((0,), (0,)), ((), ())), preferred_element_type=jnp.float32)


def factor_kernel(scale, gram, out_ref):
    order = out_ref.shape[0]
    height = 8
    count = order // height
    shape = (height, order)
    blocks = [gram[height * b : height * (b + 1), :] * scale for b in range(count)]
    row_ids, col_ids = (ids(shape, 0), ids(shape, 1))
    previous = None
    for p in range(count):
        base = height * p
        rows = [jnp.broadcast_to(blocks[p][j : j + 1, :], shape) for j in range(height)]
        corner = {(i, j): spread_lane(rows[j], base + i) for j in range(height) for i in range(j, height)}
        if previous is not None:
            for done in previous:
                lanes = [spread_lane(done, base + j) for j in range(height)]
                for j in range(height):
                    rows[j] = rows[j] - lanes[j] * done
                    for i in range(j, height):
                        corner[i, j] = corner[i, j] - lanes[i] * lanes[j]
        panel = jnp.zeros(shape, jnp.float32)
        for s in range(height):
            inverse = lax.rsqrt(corner[s, s])
            rows[s] = rows[s] * inverse
            lanes = {j: corner[j, s] * inverse for j in range(s + 1, height)}
            for j in range(s + 1, height):
                for i in range(j, height):
                    corner[i, j] = corner[i, j] - lanes[i] * lanes[j]
                rows[j] = rows[j] - lanes[j] * rows[s]
            panel = jnp.where(row_ids == s, rows[s], panel)
        panel = jnp.where(col_ids >= base + row_ids, panel, 0.0)
        out_ref[base : base + height, :] = panel
        if p + 2 < count:
            update = squares(panel)
            for q in range(p + 2, count):
                blocks[q] = blocks[q] - update[height * q : height * (q + 1), :]
        previous = rows


def shifted(value, axis, steps):
    count = lax.axis_size(axis)
    first, last = (max(0, -steps), min(count, count - steps))
    return lax.ppermute(value, axis, [(source, source + steps) for source in range(first, last)])


def beside(value, steps):
    count = lax.axis_size("tiles")
    pairs = [(source, source + steps) for source in range(count)]
    return lax.ppermute(value, "tiles", [(a, b) for a, b in pairs if 0 <= b < count and a // TGY == b // TGY])


def after(values, *done):
    return lax.optimization_barrier((values, done))[0]


def exchange_rows(messages, grid_rows):
    if len(messages) == 1:
        received = swapped(messages[0], "tiles", TGY)
        return (received, received)
    return (shifted(messages[0], "tiles", -TGY), shifted(messages[1], "tiles", TGY))


def f32(*shape):
    return jax.ShapeDtypeStruct(shape, jnp.float32)


def block(shape, *at):
    return pl.BlockSpec(shape, lambda i: at)


def call(kernel, in_specs, out_specs, out_shape, flops=0, scratch=(), aliases=None):
    return pl.pallas_call(
        kernel,
        grid=(1,),
        in_specs=in_specs,
        out_specs=out_specs,
        out_shape=out_shape,
        scratch_shapes=scratch,
        input_output_aliases=aliases or {},
        compiler_params=pltpu.CompilerParams(vmem_limit_bytes=VMEM_LIMIT),
        cost_estimate=pl.CostEstimate(flops=flops, bytes_accessed=1 << 20, transcendentals=0),
    )


def whole(array):
    zeros = (0,) * array.ndim
    return pl.BlockSpec(array.shape, lambda i: zeros)


def shards(omega, conductance, wet, volume, face_runs):
    vectors, levels, rows, cols = omega.shape
    tiles = lax.axis_size("tiles")
    grid_rows = tiles // TGY
    tile_row = lax.axis_index("tiles") // TGY
    meta = jnp.stack([tile_row, grid_rows - 1 - tile_row, lax.axis_index("vec")]).astype(jnp.int32)
    smem = pl.BlockSpec(memory_space=pltpu.SMEM)
    group = cols // EDGE
    chunks = vectors // group
    directions = 1 if grid_rows == 2 else 2
    kinds = 4
    half = levels // 2

    row_shapes = [f32(group // 2 + (kinds // 2 if c == 0 else 0), levels, rows, cols) for c in range(chunks)]
    row_shapes = [shape for shape in row_shapes for _ in range(directions)]
    packed_shapes = [f32(kinds, levels, rows, cols), f32(chunks + 1, levels, rows, cols)] + row_shapes
    statics, edges, *messages = call(
        functools.partial(pack_kernel, chunks),
        [smem, smem, whole(omega), whole(conductance), whole(wet)],
        [whole(s) for s in packed_shapes],
        packed_shapes,
    )(meta, face_runs, omega, conductance, wet)
    messages = [messages[directions * c : directions * (c + 1)] for c in range(chunks)]
    received = [exchange_rows(messages[0], grid_rows)]
    left = beside(edges, 1)
    right = beside(edges, -1)
    corner_shapes = [f32(chunks + 1, levels // 2, rows, cols)] * directions
    corners = call(
        corner_kernel, [smem, whole(left), whole(right)], [whole(s) for s in corner_shapes], corner_shapes
    )(meta, left, right)
    corners = exchange_rows(corners, grid_rows)
    gates = [(left, right), corners]
    for c in range(1, chunks):
        gate = gates[c - 1] if c <= 2 else received[c - 2]
        received.append(exchange_rows(after(messages[c], *gate), grid_rows))

    def group_specs(c):
        edge = block((1, levels, rows, cols), c, 0, 0, 0)
        corner = block((1, levels // 2, rows, cols), c, 0, 0, 0)
        return [edge, edge, edge, corner, corner]

    around = (edges, left, right, *corners)
    weight_shapes = [f32(7, levels, 2, rows, cols), f32(2, 7, levels, 2, rows, cols)]
    main_weights, strip_weights = call(
        weight_kernel,
        [smem, whole(statics), whole(received[0][0]), whole(received[0][1])] + group_specs(chunks),
        [whole(s) for s in weight_shapes],
        weight_shapes,
    )(meta, statics, *received[0], *around)

    field = None
    kept, sent = ([], [])
    half_shape = f32(group * half * rows, cols)
    for c in range(chunks):
        rims = after(received[c], sent[c - 2]) if c >= 2 else received[c]
        operands = [meta, omega, wet, volume, *rims, *around, main_weights, strip_weights]
        row_block = block((group // 2, levels, rows, cols), 0, 0, 0, 0)
        chunk_block = block((group, levels, rows, cols), c, 0, 0, 0)
        specs = [smem, chunk_block, whole(wet), whole(volume), row_block, row_block] + group_specs(c)
        specs += [whole(main_weights), whole(strip_weights)]
        aliases = {}
        if field is not None:
            aliases = {len(operands): 0}
            operands.append(field)
            specs.append(pl.BlockSpec(memory_space=pl.ANY))
        field, keep, send = call(
            functools.partial(diffuse_kernel, 4),
            specs,
            [chunk_block, whole(half_shape), whole(half_shape)],
            [f32(*omega.shape), half_shape, half_shape],
            flops=4 * 10**9,
            scratch=[pltpu.VMEM((ITERS, levels, 2, rows, cols), jnp.float32), pltpu.VMEM((group, levels, rows, cols), jnp.float32)],
            aliases=aliases,
        )(*operands)
        kept.append(keep)
        sent.append(swapped(send, "vec", 1))

    order = 2 * vectors
    gram_shape = f32(order, order)
    gram = call(
        functools.partial(gram_kernel, chunks, half * rows),
        [smem] + [whole(half_shape)] * (2 * chunks),
        whole(gram_shape),
        gram_shape,
    )(meta, *kept, *sent)
    total_cells = levels * tiles * rows * cols
    r_factor = call(
        functools.partial(factor_kernel, 1.0 / total_cells),
        [whole(gram_shape)],
        whole(gram_shape),
        gram_shape,
    )(total_over_mesh(gram))
    return (field, r_factor)


def solution(mesh):
    in_specs = (
        P("vec", None, "tiles", None),
        P(None, None, "tiles", None),
        P("tiles", None),
        P("tiles", None),
        P("tiles", None),
    )
    out_specs = (P("vec", None, "tiles", None), P())
    return jax.shard_map(shards, mesh=mesh, in_specs=in_specs, out_specs=out_specs, check_vma=False)
```

```python
import functools
import jax
import jax.numpy as jnp
from jax import lax
from jax.experimental import pallas as pl
from jax.experimental.pallas import tpu as pltpu
from jax.sharding import PartitionSpec as P

TGY = 8
ITERS = 4
EDGE = 2 * ITERS
VMEM_LIMIT = 32 * 1024 * 1024
EDGE_LIMIT = 63 * 1024 * 1024 + 256 * 1024
MAIN, SLOT = (0, 1)


def ids(shape, axis):
    return lax.broadcasted_iota(jnp.int32, shape, axis)


def turn(value, steps, axis):
    size = value.shape[axis]
    steps = steps % size
    return value if steps == 0 else pltpu.roll(value, steps, axis)


def low_half(shape):
    return ids(shape, 0) < ITERS


def left_lanes(shape):
    return ids(shape, 1) % EDGE < ITERS


def first_pair(a, b):
    return jnp.where(low_half(a.shape), a, turn(b, ITERS, 0))


def last_pair(a, b):
    return jnp.where(low_half(a.shape), turn(a, ITERS, 0), b)


def slots(below, above):
    low = low_half(below.shape)
    return (
        jnp.where(low, below, turn(above, ITERS, 0)),
        jnp.where(low, turn(below, ITERS, 0), above),
    )


def store_pair(outs, index, a, b, is_first_row):
    if len(outs) == 1:
        outs[0][index] = jnp.where(is_first_row, last_pair(a, b), first_pair(a, b))
    else:
        outs[0][index] = first_pair(a, b)
        outs[1][index] = last_pair(a, b)


def add_edge(acc, value, place):
    lanes = ids(value.shape, 1) // EDGE
    moved = turn(value, EDGE * place + ITERS, 1)
    return moved if acc is None else jnp.where(lanes == place, moved, acc)


def prev_row(part, other):
    return jnp.where(ids(part.shape, 0) == 0, turn(other, 1, 0), turn(part, 1, 0))


def next_row(part, other):
    last = part.shape[0] - 1
    return jnp.where(ids(part.shape, 0) == last, turn(other, -1, 0), turn(part, -1, 0))


def prev_col(part, rim):
    return jnp.where(ids(part.shape, 1) == 0, rim, turn(part, 1, 1))


def next_col(part, rim):
    last = part.shape[1] - 1
    return jnp.where(ids(part.shape, 1) == last, rim, turn(part, -1, 1))


def strips(edges, rims):
    left = left_lanes(edges.shape)
    return (jnp.where(left, rims, edges), jnp.where(left, edges, rims))


def crossing(left_strip, right_strip):
    lanes = ids(left_strip.shape, 1) % EDGE
    return jnp.where(lanes == ITERS - 1, turn(right_strip, -1, 1), turn(left_strip, 1, 1))


def rim_of(cross, place):
    return turn(cross, -(EDGE * place + ITERS), 1)


def pack_kernel(chunks, meta, runs, omega, conductance, wet, static_out, edge_out, *row_outs):
    directions = len(row_outs) // chunks
    levels, rows, cols = omega.shape[1:]
    shape = (rows, cols)
    is_first_row = meta[0] == 0
    row_ids, col_ids = (ids(shape, 0), ids(shape, 1))
    wet_cells = wet[...].astype(jnp.float32)
    open_x = (col_ids >= runs[0, 0]) & (col_ids < runs[0, 0] + runs[0, 1])
    open_y = (row_ids >= runs[0, 2]) & (row_ids < runs[0, 2] + runs[0, 3])
    keep_x = (row_ids > 0) | open_x
    keep_y = (col_ids > 0) | open_y
    statics = []
    for level in range(levels):
        statics.append(
            [
                jnp.where(keep_x, conductance[0, level], 0.0),
                jnp.where(keep_y, conductance[1, level], 0.0),
                conductance[2, level] if level else jnp.zeros(shape, jnp.float32),
                wet_cells,
            ]
        )
    kinds = len(statics[0])
    group = cols // EDGE
    for level in range(levels):
        edge = None
        for kind in range(kinds):
            static_out[kind, level] = statics[level][kind]
            edge = add_edge(edge, statics[level][kind], kind)
        edge_out[chunks, level] = edge
        for kind in range(0, kinds, 2):
            outs = row_outs[:directions]
            store_pair(outs, (group // 2 + kind // 2, level), statics[level][kind], statics[level][kind + 1], is_first_row)
        for chunk in range(chunks):
            outs = row_outs[directions * chunk : directions * (chunk + 1)]
            edge = None
            for pair in range(group // 2):
                start = [omega[chunk * group + 2 * pair + i, level] * wet_cells for i in range(2)]
                edge = add_edge(edge, start[0], 2 * pair)
                edge = add_edge(edge, start[1], 2 * pair + 1)
                store_pair(outs, (pair, level), start[0], start[1], is_first_row)
            edge_out[chunk, level] = edge


def corner_kernel(meta, left, right, *outs):
    is_first_row = meta[0] == 0
    groups, levels, rows, cols = left.shape
    take = left_lanes((rows, cols))
    for g in range(groups):
        for level in range(0, levels, 2):
            pair = [jnp.where(take, left[g, level + i], right[g, level + i]) for i in range(2)]
            store_pair(outs, (g, level // 2), pair[0], pair[1], is_first_row)


def rims_of_group(left, right, corner_below, corner_above):
    levels, rows, cols = left.shape[1:]
    take = left_lanes((rows, cols))
    rims = [[jnp.where(take, left[0, level], right[0, level]), None] for level in range(levels)]
    for level in range(0, levels, 2):
        pair = slots(corner_below[0, level // 2], corner_above[0, level // 2])
        rims[level][SLOT], rims[level + 1][SLOT] = pair
    return rims


def weight_kernel(meta, statics, below, above, edges, left, right, corner_below, corner_above, main_out, strip_out):
    kinds, levels, rows, cols = statics.shape
    shape = (rows, cols)
    low = low_half(shape)
    valid = (low & (meta[1] > 0)) | (jnp.logical_not(low) & (meta[0] > 0))
    first = below.shape[0] - kinds // 2
    rims = rims_of_group(left, right, corner_below, corner_above)
    field = [[[statics[kind, level], None] for level in range(levels)] for kind in range(kinds)]
    for level in range(levels):
        for kind in range(0, kinds, 2):
            pair = slots(below[first + kind // 2, level], above[first + kind // 2, level])
            for i in range(2):
                field[kind + i][level][SLOT] = jnp.where(valid, pair[i], 0.0)
    width = cols // EDGE
    lanes = ids(shape, 1) // EDGE

    def spread(strip, kind):
        value = jnp.where(lanes == 0, turn(strip, -EDGE * kind, 1), 0.0)
        span = 1
        while span < width:
            value = value + turn(value, EDGE * span, 1)
            span *= 2
        return value

    side = [[[[None, None] for _ in range(levels)] for _ in range(kinds)] for _ in range(2)]
    cross = [[None, None] for _ in range(levels)]
    for level in range(levels):
        for part in range(2):
            edge = edges[0, level] if part == MAIN else None
            if part == SLOT:
                for kind in range(kinds):
                    edge = add_edge(edge, field[kind][level][SLOT], kind)
            rim = rims[level][part]
            if part == SLOT:
                rim = jnp.where(valid, rim, 0.0)
            pair = strips(edge, rim)
            cross[level][part] = crossing(pair[0], pair[1])
            for s in range(2):
                for kind in range(kinds):
                    side[s][kind][level][part] = spread(pair[s], kind)

    def emit(out, values, after_of):
        for level in range(levels):
            for part in range(2):
                cond_x, cond_y, cond_z, wet = (values[kind][level][part] for kind in range(kinds))
                faces = [
                    cond_x,
                    next_row(cond_x, values[0][level][1 - part]),
                    cond_y,
                    after_of(cond_y, level, part),
                    cond_z,
                    values[2][level + 1][part] if level + 1 < levels else jnp.zeros(shape, jnp.float32),
                ]
                total = faces[0]
                for face in faces[1:]:
                    total = total + face
                out[0, level, part] = wet * (1.0 - total)
                for index, face in enumerate(faces):
                    out[index + 1, level, part] = wet * face

    emit(main_out, field, lambda cond, level, part: next_col(cond, rim_of(cross[level][part], 1)))
    for s in range(2):
        emit(strip_out.at[s], side[s], lambda cond, level, part: turn(cond, -1, 1))


def one_pass(state, weight, parts, rim_at):
    levels = len(state)
    result = [[None, None] for _ in range(levels)]
    for level in range(levels):
        for part in parts:
            value, other = (state[level][part], state[level][1 - part])
            rim = rim_at(level, part)
            before = turn(value, 1, 1) if rim is None else prev_col(value, rim)
            after = turn(value, -1, 1) if rim is None else next_col(value, rim)
            total = weight(0, level, part) * value
            total = total + weight(1, level, part) * prev_row(value, other)
            total = total + weight(2, level, part) * next_row(value, other)
            total = total + weight(3, level, part) * before
            total = total + weight(4, level, part) * after
            if level > 0:
                total = total + weight(5, level, part) * state[level - 1][part]
            if level < levels - 1:
                total = total + weight(6, level, part) * state[level + 1][part]
            result[level][part] = total
    return result


def diffuse_kernel(
    batch, meta, omega, wet, volume, below, above, edges, left, right, corner_below, corner_above,
    main_weights, strip_weights, *rest
):
    field_out, keep_out, send_out, cross_scratch, slot_scratch = rest[-5:]
    group, levels, rows, cols = omega.shape
    shape = (rows, cols)
    wet_cells = wet[...].astype(jnp.float32)
    root = jnp.sqrt(volume[...])
    half = levels // 2
    keeps_low = meta[2] == 0
    rims = rims_of_group(left, right, corner_below, corner_above)
    slot_edges = [None] * levels
    for level in range(levels):
        for pair in range(group // 2):
            two = slots(below[pair, level], above[pair, level])
            for i in range(2):
                slot_scratch[2 * pair + i, level] = two[i]
                slot_edges[level] = add_edge(slot_edges[level], two[i], 2 * pair + i)
    state = [[[None, None] for _ in range(levels)] for _ in range(2)]
    for level in range(levels):
        for part in range(2):
            edge = edges[0, level] if part == MAIN else slot_edges[level]
            pair = strips(edge, rims[level][part])
            for s in range(2):
                state[s][level][part] = pair[s]
    for sweep in range(ITERS):
        for level in range(levels):
            for part in range(2):
                cross_scratch[sweep, level, part] = crossing(state[0][level][part], state[1][level][part])
        if sweep < ITERS - 1:
            for s in range(2):
                state[s] = one_pass(
                    state[s], lambda n, level, part: strip_weights[s, n, level, part], (MAIN, SLOT), lambda level, part: None
                )

    for first in range(0, group, batch):
        fields = []
        for place in range(first, first + batch):
            fields.append([[omega[place, level] * wet_cells, slot_scratch[place, level]] for level in range(levels)])
        for sweep in range(ITERS):
            parts = (MAIN, SLOT) if sweep < ITERS - 1 else (MAIN,)
            for i in range(batch):
                fields[i] = one_pass(
                    fields[i],
                    lambda n, level, part: main_weights[n, level, part],
                    parts,
                    lambda level, part: rim_of(cross_scratch[sweep, level, part], first + i),
                )
        for i in range(batch):
            scaled = []
            for level in range(levels):
                value = fields[i][level][MAIN]
                field_out[first + i, level] = value
                scaled.append(value * root)
            for level in range(half):
                at = ((first + i) * half + level) * rows
                keep_out[at : at + rows, :] = jnp.where(keeps_low, scaled[level], scaled[half + level])
                send_out[at : at + rows, :] = jnp.where(keeps_low, scaled[half + level], scaled[level])


def gram_of_rows(slices, refs):
    group = refs[0].shape[0] // slices
    order = group * len(refs)
    exact = jnp.zeros((order, order), jnp.float32)
    cross = jnp.zeros((order, order), jnp.float32)
    for at in range(0, slices, 2):
        columns = []
        for i in range(2):
            columns.append(jnp.concatenate([ref[pl.ds(at + i, group, slices), :] for ref in refs], axis=0))
        values = jnp.concatenate(columns, axis=1)
        high = values.astype(jnp.bfloat16)
        rest = (values - high.astype(jnp.float32)).astype(jnp.bfloat16)
        dims = (((1,), (1,)), ((), ()))
        exact = exact + lax.dot_general(high, high, dims, preferred_element_type=jnp.float32)
        cross = cross + lax.dot_general(high, rest, dims, preferred_element_type=jnp.float32)
    return exact + (cross + cross.T)


def store_halves(meta, gram, mine, theirs):
    order = gram.shape[0]
    moved = turn(turn(gram, order // 2, 0), order // 2, 1)
    first, second = halves_of_gram(jnp.where(meta[2] == 0, gram, moved))
    is_first = meta[3] == 0
    mine[...] = jnp.where(is_first, first, second)
    theirs[...] = jnp.where(is_first, second, first)


def gram_kernel(chunks, slices, meta, *refs):
    store_halves(meta, gram_of_rows(slices, refs[:-2]), *refs[-2:])


def far_gram_kernel(slices, kept, received, out):
    out[...] = gram_of_rows(slices, (kept, received))


def near_gram_kernel(slices, meta, far, *refs):
    store_halves(meta, far[...] + gram_of_rows(slices, refs[:-2]), *refs[-2:])


def swapped(value, axis, bit):
    count = lax.axis_size(axis)
    return lax.ppermute(value, axis, [(source, source ^ bit) for source in range(count)])


def mesh_permute(value, mask):
    axes = ("tiles", "vec")
    count = lax.axis_size("tiles") * lax.axis_size("vec")
    return lax.ppermute(value, axes, [(source, source ^ mask) for source in range(count)])


def total_over_chips(value):
    vec = lax.axis_size("vec")
    masks = []
    bit = 1
    while bit < vec:
        masks.append(bit)
        bit *= 2
    bit = 2
    while bit < lax.axis_size("tiles"):
        masks.append(bit * vec)
        bit *= 2
    while masks:
        near, masks = (masks[:2], masks[2:])
        if len(near) == 1:
            value = value + mesh_permute(value, near[0])
        else:
            one, two, both = (mesh_permute(value, mask) for mask in (near[0], near[1], near[0] ^ near[1]))
            value = (value + one) + (two + both)
    return value


def fold(a, b):
    half = a.shape[1] // 2
    return jnp.where(ids(a.shape, 1) < half, a, b)


def flip(value):
    return turn(value, value.shape[1] // 2, 1)


def halves_of_gram(gram):
    q = gram.shape[0] // 8
    first = [fold(gram[: 2 * q], flip(gram[2 * q : 4 * q])), fold(flip(gram[:q]), gram[q : 2 * q])]
    second = [fold(flip(gram[4 * q : 6 * q]), gram[6 * q :]), fold(flip(gram[2 * q : 3 * q]), gram[3 * q : 4 * q])]
    return (jnp.concatenate(first, axis=0), jnp.concatenate(second, axis=0))


def gram_of_halves(first, second):
    q = first.shape[0] // 3
    return jnp.concatenate(
        [
            fold(first[:q], flip(first[2 * q :])),
            fold(first[q : 2 * q], first[2 * q :]),
            fold(flip(first[:q]), flip(second[2 * q :])),
            fold(flip(first[q : 2 * q]), second[2 * q :]),
            flip(second[: 2 * q]),
            second[: 2 * q],
        ],
        axis=0,
    )


def spread_lane(value, lane):
    return jnp.broadcast_to(value[:, lane : lane + 1], value.shape)


def squares(rows):
    high = rows.astype(jnp.bfloat16).astype(jnp.float32)
    rest = rows - high
    middle = rest.astype(jnp.bfloat16).astype(jnp.float32)
    low = rest - middle
    one = jnp.concatenate([high, high, middle, high, low, middle], axis=0).astype(jnp.bfloat16)
    two = jnp.concatenate([high, middle, high, low, high, middle], axis=0).astype(jnp.bfloat16)
    return lax.dot_general(one, two, (((0,), (0,)), ((), ())), preferred_element_type=jnp.float32)


def factor_kernel(scale, meta, own, other, out_ref):
    order = out_ref.shape[0]
    height = 8
    count = order // height
    shape = (height, order)
    is_first = meta[3] == 0
    mine, theirs = (own[...], other[...])
    gram = gram_of_halves(jnp.where(is_first, mine, theirs), jnp.where(is_first, theirs, mine)) * scale
    blocks = [gram[height * b : height * (b + 1), :] for b in range(count)]
    row_ids, col_ids = (ids(shape, 0), ids(shape, 1))
    previous = None
    for p in range(count):
        base = height * p
        rows = [jnp.broadcast_to(blocks[p][j : j + 1, :], shape) for j in range(height)]
        corner = {(i, j): spread_lane(rows[j], base + i) for j in range(height) for i in range(j, height)}
        if previous is not None:
            for done in previous:
                lanes = [spread_lane(done, base + j) for j in range(height)]
                for j in range(height):
                    rows[j] = rows[j] - lanes[j] * done
                    for i in range(j, height):
                        corner[i, j] = corner[i, j] - lanes[i] * lanes[j]
        panel = jnp.zeros(shape, jnp.float32)
        for s in range(height):
            inverse = lax.rsqrt(corner[s, s])
            rows[s] = rows[s] * inverse
            lanes = {j: corner[j, s] * inverse for j in range(s + 1, height)}
            for j in range(s + 1, height):
                for i in range(j, height):
                    corner[i, j] = corner[i, j] - lanes[i] * lanes[j]
                rows[j] = rows[j] - lanes[j] * rows[s]
            panel = jnp.where(row_ids == s, rows[s], panel)
        panel = jnp.where(col_ids >= base + row_ids, panel, 0.0)
        out_ref[base : base + height, :] = panel
        if p + 2 < count:
            update = squares(panel)
            for q in range(p + 2, count):
                blocks[q] = blocks[q] - update[height * q : height * (q + 1), :]
        previous = rows


def edge_kernel(runs, omega, conductance, wet, static_out, edge_out):
    levels, rows, cols = omega.shape[1:]
    shape = (rows, cols)
    row_ids, col_ids = (ids(shape, 0), ids(shape, 1))
    wet_cells = wet[...].astype(jnp.float32)
    open_x = (col_ids >= runs[0, 0]) & (col_ids < runs[0, 0] + runs[0, 1])
    open_y = (row_ids >= runs[0, 2]) & (row_ids < runs[0, 2] + runs[0, 3])
    keep_x = (row_ids > 0) | open_x
    keep_y = (col_ids > 0) | open_y
    group = cols // EDGE
    chunks = omega.shape[0] // group
    for level in range(levels):
        statics = [
            jnp.where(keep_x, conductance[0, level], 0.0),
            jnp.where(keep_y, conductance[1, level], 0.0),
            conductance[2, level] if level else jnp.zeros(shape, jnp.float32),
            wet_cells,
        ]
        edge = None
        for kind, value in enumerate(statics):
            static_out[kind, level] = value
            edge = add_edge(edge, value, kind)
        edge_out[chunks, level] = edge
        for chunk in range(chunks):
            edge = None
            for place in range(group):
                edge = add_edge(edge, omega[chunk * group + place, level] * wet_cells, place)
            edge_out[chunk, level] = edge


def face_kernel(meta, omega, wet, *row_outs):
    levels, rows, cols = omega.shape[1:]
    group = cols // EDGE
    is_first_row = meta[0] == 0
    wet_cells = wet[...].astype(jnp.float32)
    for chunk, out in enumerate(row_outs):
        for level in range(levels):
            for pair in range(group // 2):
                start = [omega[chunk * group + 2 * pair + i, level] * wet_cells for i in range(2)]
                store_pair((out,), (pair, level), start[0], start[1], is_first_row)


def rim_kernel(meta, statics, left, right, out):
    is_first_row = meta[0] == 0
    groups, levels, rows, cols = left.shape
    kinds = statics.shape[0]
    take = left_lanes((rows, cols))
    for g in range(groups):
        for level in range(0, levels, 2):
            pair = [jnp.where(take, left[g, level + i], right[g, level + i]) for i in range(2)]
            store_pair((out,), g * levels // 2 + level // 2, pair[0], pair[1], is_first_row)
    first = groups * levels // 2
    for kind in range(0, kinds, 2):
        for level in range(levels):
            at = first + kind // 2 * levels + level
            store_pair((out,), at, statics[kind, level], statics[kind + 1, level], is_first_row)


def near_rows(is_first_row, a, b, halo):
    low = low_half(halo.shape)
    turned = turn(halo, ITERS, 0)
    result = []
    for own, across, moved in ((a, halo, turned), (b, turned, halo)):
        near = turn(own, ITERS, 0)
        result.append(jnp.where(low, jnp.where(is_first_row, near, across), jnp.where(is_first_row, moved, near)))
    return result


def spread_kind(strip, kind):
    cols = strip.shape[1]
    value = jnp.where(ids(strip.shape, 1) // EDGE == 0, turn(strip, -EDGE * kind, 1), 0.0)
    span = EDGE
    while span < cols:
        value = value + turn(value, span, 1)
        span *= 2
    return value


def store_weights(out, values, after_row, after_col):
    levels = len(values[0])
    for level in range(levels):
        cond_x, cond_y, cond_z, wet = (kind[level] for kind in values)
        below = values[2][level + 1] if level + 1 < levels else jnp.zeros_like(cond_z)
        faces = [cond_x, after_row(level), cond_y, after_col(level), cond_z, below]
        total = faces[0]
        for face in faces[1:]:
            total = total + face
        out[0, level] = wet * (1.0 - total)
        for index, face in enumerate(faces):
            out[index + 1, level] = wet * face


def plane_pass(state, weight, row_before, row_after, rim_at):
    levels = len(state)
    result = []
    for level in range(levels):
        value = state[level]
        rim = rim_at(level)
        before = turn(value, 1, 1) if rim is None else prev_col(value, rim)
        after = turn(value, -1, 1) if rim is None else next_col(value, rim)
        total = weight(0, level) * value
        total = total + weight(1, level) * row_before(value, level)
        total = total + weight(2, level) * row_after(value, level)
        total = total + weight(3, level) * before
        total = total + weight(4, level) * after
        if level > 0:
            total = total + weight(5, level) * state[level - 1]
        if level < levels - 1:
            total = total + weight(6, level) * state[level + 1]
        result.append(total)
    return result


def no_rim(level):
    return None


def pack_levels(values, use_first):
    pairs = []
    for level in range(0, len(values), 2):
        a, b = values[level : level + 2]
        pairs.append(jnp.where(use_first, first_pair(a, b), last_pair(a, b)))
    return pairs


def store_half(keep, send, place, pairs, keeps_low):
    rows = pairs[0].shape[0]
    half = len(pairs) // 2
    for i in range(half):
        at = (place * half + i) * rows
        keep[at : at + rows, :] = jnp.where(keeps_low, pairs[i], pairs[half + i])
        send[at : at + rows, :] = jnp.where(keeps_low, pairs[half + i], pairs[i])


def far_kernel(
    batch, meta, statics, omega, wet, volume, edges, left, right,
    final_out, bound_out, strip_bound_out, keep_out, send_out, weights, strip_weights, cross_scratch
):
    vectors, levels, rows, cols = omega.shape
    kinds = statics.shape[0]
    shape = (rows, cols)
    group = cols // EDGE
    chunks = vectors // group
    is_first_row = meta[0] == 0
    keeps_low = meta[2] == 0
    row_ids = ids(shape, 0)
    take = left_lanes(shape)
    wet_cells = wet[...].astype(jnp.float32)
    root = jnp.sqrt(volume[...])

    def sides(g, level):
        return strips(edges[g, level], jnp.where(take, left[g, level], right[g, level]))

    def roll_before(value, level):
        return turn(value, 1, 0)

    def roll_after(value, level):
        return turn(value, -1, 0)

    def closed_after(value):
        return jnp.where(row_ids == rows - 1, 0.0, turn(value, -1, 0))

    field = [[statics[kind, level] for level in range(levels)] for kind in range(kinds)]
    pairs = [sides(chunks, level) for level in range(levels)]
    crosses = [crossing(*pair) for pair in pairs]
    store_weights(
        weights, field, lambda level: closed_after(field[0][level]),
        lambda level: next_col(field[1][level], rim_of(crosses[level], 1)),
    )
    for s in range(2):
        side = [[spread_kind(pairs[level][s], kind) for level in range(levels)] for kind in range(kinds)]
        store_weights(
            strip_weights.at[s], side, lambda level: closed_after(side[0][level]), lambda level: turn(side[1][level], -1, 1)
        )

    def keep_bound(acc, value, sweep):
        edge = jnp.where(is_first_row, value, turn(value, -1, 0))
        moved = turn(edge, sweep - (ITERS - 1), 0)
        return moved if acc is None else jnp.where(row_ids == sweep, moved, acc)

    for g in range(chunks):
        state = [[sides(g, level)[s] for level in range(levels)] for s in range(2)]
        bounds = [[None] * levels for _ in range(2)]
        for sweep in range(ITERS):
            for level in range(levels):
                cross_scratch[g, sweep, level] = crossing(state[0][level], state[1][level])
                for s in range(2):
                    bounds[s][level] = keep_bound(bounds[s][level], state[s][level], sweep)
            if sweep < ITERS - 1:
                for s in range(2):
                    state[s] = plane_pass(
                        state[s], lambda n, level: strip_weights[s, n, level], roll_before, roll_after, no_rim
                    )
        for s in range(2):
            for level in range(levels):
                strip_bound_out[g, s, level] = bounds[s][level]

    for first in range(0, vectors, batch):
        g = first // group
        fields = [[omega[place, level] * wet_cells for level in range(levels)] for place in range(first, first + batch)]
        bounds = [[None] * levels for _ in range(batch)]
        for sweep in range(ITERS):
            for i in range(batch):
                for level in range(levels):
                    bounds[i][level] = keep_bound(bounds[i][level], fields[i][level], sweep)
                fields[i] = plane_pass(
                    fields[i], lambda n, level: weights[n, level], roll_before, roll_after,
                    lambda level: rim_of(cross_scratch[g, sweep, level], (first + i) % group),
                )
        for i in range(batch):
            for level in range(levels):
                final_out[first + i, level] = fields[i][level]
                bound_out[first + i, level] = bounds[i][level]
            scaled = [value * root for value in fields[i]]
            store_half(keep_out, send_out, first + i, pack_levels(scaled, is_first_row), keeps_low)


def near_weight_kernel(meta, statics, rims, edges, left, right, weights, strip_weights):
    kinds, levels, rows, cols = statics.shape
    shape = (rows, cols)
    is_first_row = meta[0] == 0
    take = left_lanes(shape)
    last = ids(shape, 0) == rows - 1
    g = edges.shape[0] - 1
    groups = edges.shape[0]
    first = groups * levels // 2
    field = [[None] * levels for _ in range(kinds)]
    for kind in range(0, kinds, 2):
        for level in range(levels):
            own = (statics[kind, level], statics[kind + 1, level])
            pair = near_rows(is_first_row, *own, rims[first + kind // 2 * levels + level])
            field[kind][level], field[kind + 1][level] = pair
    rim = [jnp.where(take, left[g, level], right[g, level]) for level in range(levels)]
    near_rim = []
    for level in range(0, levels, 2):
        near_rim += near_rows(is_first_row, rim[level], rim[level + 1], rims[g * levels // 2 + level // 2])
    near_edge = []
    for level in range(levels):
        edge = None
        for kind in range(kinds):
            edge = add_edge(edge, field[kind][level], kind)
        near_edge.append(edge)
    pairs = [strips(near_edge[level], near_rim[level]) for level in range(levels)]
    tile_pairs = [strips(edges[g, level], rim[level]) for level in range(levels)]
    crosses = [crossing(*pair) for pair in pairs]

    def with_next(value, tile_value):
        beyond = jnp.broadcast_to(tile_value[ITERS : ITERS + 1, :], shape)
        return jnp.where(last, beyond, turn(value, -1, 0))

    store_weights(
        weights, field, lambda level: with_next(field[0][level], statics[0, level]),
        lambda level: next_col(field[1][level], rim_of(crosses[level], 1)),
    )
    for s in range(2):
        side = [[spread_kind(pairs[level][s], kind) for level in range(levels)] for kind in range(kinds)]
        tile_side = [spread_kind(tile_pairs[level][s], 0) for level in range(levels)]
        store_weights(
            strip_weights.at[s], side, lambda level: with_next(side[0][level], tile_side[level]),
            lambda level: turn(side[1][level], -1, 1),
        )


def near_kernel(
    batch, chunk, meta, omega, wet, volume, halo, rims, left, right, weights, strip_weights, bound, strip_bound, final, *rest
):
    field_out, keep_out, send_out, cross_scratch, start = rest[-5:]
    group, levels, rows, cols = omega.shape
    shape = (rows, cols)
    is_first_row = meta[0] == 0
    keeps_low = meta[2] == 0
    row_ids = ids(shape, 0)
    take = left_lanes(shape)
    top = (row_ids == 0) & is_first_row
    bottom = (row_ids == rows - 1) & jnp.logical_not(is_first_row)
    is_near = low_half(shape) != is_first_row
    wet_cells = wet[...].astype(jnp.float32)
    root = jnp.sqrt(volume[...])

    near_edge = [None] * levels
    for level in range(levels):
        for pair in range(group // 2):
            own = [omega[2 * pair + i, level] * wet_cells for i in range(2)]
            two = near_rows(is_first_row, *own, halo[pair, level])
            for i in range(2):
                start[2 * pair + i, level] = two[i]
                near_edge[level] = add_edge(near_edge[level], two[i], 2 * pair + i)
    rim = [jnp.where(take, left[0, level], right[0, level]) for level in range(levels)]
    near_rim = []
    for level in range(0, levels, 2):
        near_rim += near_rows(is_first_row, rim[level], rim[level + 1], rims[chunk * levels // 2 + level // 2])

    def around(bound_at, sweep):
        def kept(level):
            return jnp.broadcast_to(bound_at(level)[sweep : sweep + 1, :], shape)

        return (
            lambda value, level: jnp.where(top, kept(level), turn(value, 1, 0)),
            lambda value, level: jnp.where(bottom, kept(level), turn(value, -1, 0)),
        )

    pairs = [strips(near_edge[level], near_rim[level]) for level in range(levels)]
    state = [[pairs[level][s] for level in range(levels)] for s in range(2)]
    for sweep in range(ITERS):
        for level in range(levels):
            cross_scratch[sweep, level] = crossing(state[0][level], state[1][level])
        if sweep < ITERS - 1:
            for s in range(2):
                state[s] = plane_pass(
                    state[s], lambda n, level: strip_weights[s, n, level],
                    *around(lambda level: strip_bound[0, s, level], sweep), no_rim,
                )

    for first in range(0, group, batch):
        fields = [[start[place, level] for level in range(levels)] for place in range(first, first + batch)]
        for sweep in range(ITERS):
            for i in range(batch):
                fields[i] = plane_pass(
                    fields[i], lambda n, level: weights[n, level],
                    *around(lambda level: bound[first + i, level], sweep),
                    lambda level: rim_of(cross_scratch[sweep, level], first + i),
                )
        for i in range(batch):
            scaled = []
            for level in range(levels):
                value = jnp.where(is_near, turn(fields[i][level], ITERS, 0), final[first + i, level])
                field_out[first + i, level] = value
                scaled.append(value * root)
            store_half(keep_out, send_out, first + i, pack_levels(scaled, jnp.logical_not(is_first_row)), keeps_low)


def shifted(value, axis, steps):
    count = lax.axis_size(axis)
    first, last = (max(0, -steps), min(count, count - steps))
    return lax.ppermute(value, axis, [(source, source + steps) for source in range(first, last)])


def beside(value, steps):
    count = lax.axis_size("tiles")
    pairs = [(source, source + steps) for source in range(count)]
    return lax.ppermute(value, "tiles", [(a, b) for a, b in pairs if 0 <= b < count and a // TGY == b // TGY])


def after(values, *done):
    return lax.optimization_barrier((values, done))[0]


def exchange_rows(messages, grid_rows):
    if len(messages) == 1:
        received = swapped(messages[0], "tiles", TGY)
        return (received, received)
    return (shifted(messages[0], "tiles", -TGY), shifted(messages[1], "tiles", TGY))


def f32(*shape):
    return jax.ShapeDtypeStruct(shape, jnp.float32)


def block(shape, *at):
    return pl.BlockSpec(shape, lambda i: at)


def call(kernel, in_specs, out_specs, out_shape, flops=0, scratch=(), aliases=None, limit=VMEM_LIMIT):
    return pl.pallas_call(
        kernel,
        grid=(1,),
        in_specs=in_specs,
        out_specs=out_specs,
        out_shape=out_shape,
        scratch_shapes=scratch,
        input_output_aliases=aliases or {},
        compiler_params=pltpu.CompilerParams(vmem_limit_bytes=limit),
        cost_estimate=pl.CostEstimate(flops=flops, bytes_accessed=1 << 20, transcendentals=0),
    )


def whole(array):
    zeros = (0,) * array.ndim
    return pl.BlockSpec(array.shape, lambda i: zeros)


def factor(meta, mine, theirs, order, scale):
    mine = total_over_chips(mine + swapped(theirs, "tiles", 1))
    smem = pl.BlockSpec(memory_space=pltpu.SMEM)
    return call(
        functools.partial(factor_kernel, scale),
        [smem, whole(mine), whole(mine)],
        whole(f32(order, order)),
        f32(order, order),
    )(meta, mine, swapped(mine, "tiles", 1))


def shards_any(omega, conductance, wet, volume, face_runs):
    vectors, levels, rows, cols = omega.shape
    tiles = lax.axis_size("tiles")
    grid_rows = tiles // TGY
    tile_row = lax.axis_index("tiles") // TGY
    core = lax.axis_index("tiles") % 2
    meta = jnp.stack([tile_row, grid_rows - 1 - tile_row, lax.axis_index("vec"), core]).astype(jnp.int32)
    smem = pl.BlockSpec(memory_space=pltpu.SMEM)
    group = cols // EDGE
    chunks = vectors // group
    directions = 1 if grid_rows == 2 else 2
    kinds = 4
    half = levels // 2

    row_shapes = [f32(group // 2 + (kinds // 2 if c == 0 else 0), levels, rows, cols) for c in range(chunks)]
    row_shapes = [shape for shape in row_shapes for _ in range(directions)]
    packed_shapes = [f32(kinds, levels, rows, cols), f32(chunks + 1, levels, rows, cols)] + row_shapes
    statics, edges, *messages = call(
        functools.partial(pack_kernel, chunks),
        [smem, smem, whole(omega), whole(conductance), whole(wet)],
        [whole(s) for s in packed_shapes],
        packed_shapes,
    )(meta, face_runs, omega, conductance, wet)
    messages = [messages[directions * c : directions * (c + 1)] for c in range(chunks)]
    received = [exchange_rows(messages[0], grid_rows)]
    left = beside(edges, 1)
    right = beside(edges, -1)
    corner_shapes = [f32(chunks + 1, levels // 2, rows, cols)] * directions
    corners = call(
        corner_kernel, [smem, whole(left), whole(right)], [whole(s) for s in corner_shapes], corner_shapes
    )(meta, left, right)
    corners = exchange_rows(corners, grid_rows)
    gates = [(left, right), corners]
    for c in range(1, chunks):
        gate = gates[c - 1] if c <= 2 else received[c - 2]
        received.append(exchange_rows(after(messages[c], *gate), grid_rows))

    def group_specs(c):
        edge = block((1, levels, rows, cols), c, 0, 0, 0)
        corner = block((1, levels // 2, rows, cols), c, 0, 0, 0)
        return [edge, edge, edge, corner, corner]

    around = (edges, left, right, *corners)
    weight_shapes = [f32(7, levels, 2, rows, cols), f32(2, 7, levels, 2, rows, cols)]
    main_weights, strip_weights = call(
        weight_kernel,
        [smem, whole(statics), whole(received[0][0]), whole(received[0][1])] + group_specs(chunks),
        [whole(s) for s in weight_shapes],
        weight_shapes,
    )(meta, statics, *received[0], *around)

    field = None
    kept, sent = ([], [])
    half_shape = f32(group * half * rows, cols)
    for c in range(chunks):
        rims = after(received[c], sent[c - 2]) if c >= 2 else received[c]
        operands = [meta, omega, wet, volume, *rims, *around, main_weights, strip_weights]
        row_block = block((group // 2, levels, rows, cols), 0, 0, 0, 0)
        chunk_block = block((group, levels, rows, cols), c, 0, 0, 0)
        specs = [smem, chunk_block, whole(wet), whole(volume), row_block, row_block] + group_specs(c)
        specs += [whole(main_weights), whole(strip_weights)]
        aliases = {}
        if field is not None:
            aliases = {len(operands): 0}
            operands.append(field)
            specs.append(pl.BlockSpec(memory_space=pl.ANY))
        field, keep, send = call(
            functools.partial(diffuse_kernel, 4),
            specs,
            [chunk_block, whole(half_shape), whole(half_shape)],
            [f32(*omega.shape), half_shape, half_shape],
            flops=4 * 10**9,
            scratch=[pltpu.VMEM((ITERS, levels, 2, rows, cols), jnp.float32), pltpu.VMEM((group, levels, rows, cols), jnp.float32)],
            aliases=aliases,
        )(*operands)
        kept.append(keep)
        sent.append(swapped(send, "vec", 1))

    order = 2 * vectors
    half_gram = f32(3 * order // 8, order)
    mine, theirs = call(
        functools.partial(gram_kernel, chunks, half * rows),
        [smem] + [whole(half_shape)] * (2 * chunks),
        [whole(half_gram)] * 2,
        [half_gram] * 2,
    )(meta, *kept, *sent)
    r_factor = factor(meta, mine, theirs, order, 1.0 / (levels * tiles * rows * cols))
    return (field, r_factor)


def shards_of_two_rows(omega, conductance, wet, volume, face_runs):
    vectors, levels, rows, cols = omega.shape
    tiles = lax.axis_size("tiles")
    tile_row = lax.axis_index("tiles") // TGY
    core = lax.axis_index("tiles") % 2
    meta = jnp.stack([tile_row, 1 - tile_row, lax.axis_index("vec"), core]).astype(jnp.int32)
    smem = pl.BlockSpec(memory_space=pltpu.SMEM)
    group = cols // EDGE
    chunks = vectors // group
    kinds = 4
    half = levels // 4
    plane = (rows, cols)

    def vmem(*lead):
        return pltpu.VMEM(lead + plane, jnp.float32)

    edge_shapes = [f32(kinds, levels, *plane), f32(chunks + 1, levels, *plane)]
    statics, edges = call(
        edge_kernel,
        [smem, whole(omega), whole(conductance), whole(wet)],
        [whole(s) for s in edge_shapes],
        edge_shapes,
        limit=EDGE_LIMIT,
    )(face_runs, omega, conductance, wet)
    left = beside(edges, 1)
    right = beside(edges, -1)
    row_shapes = [f32(group // 2, levels, *plane)] * chunks
    messages = call(
        face_kernel,
        [smem, whole(omega), whole(wet)],
        [whole(s) for s in row_shapes],
        row_shapes,
        flops=10**9,
    )(meta, omega, wet)
    halos = [swapped(messages[0], "tiles", TGY)]
    rim_shape = f32((chunks + 1) * levels // 2 + kinds // 2 * levels, *plane)
    rims = call(rim_kernel, [smem, whole(statics), whole(left), whole(right)], whole(rim_shape), rim_shape)(
        meta, statics, left, right
    )
    rims = swapped(rims, "tiles", TGY)
    gates = [(left, right), (halos[0], rims)]
    for c in range(1, chunks):
        gate = gates[c - 1] if c <= 2 else halos[c - 2]
        halos.append(swapped(after(messages[c], gate), "tiles", TGY))

    far_shape = f32(vectors * half * rows, cols)
    far_shapes = [f32(*omega.shape), f32(*omega.shape), f32(chunks, 2, levels, *plane), far_shape, far_shape]
    final, bound, strip_bound, far_kept, far_sent = call(
        functools.partial(far_kernel, 4),
        [smem] + [whole(x) for x in (statics, omega, wet, volume, edges, left, right)],
        [whole(s) for s in far_shapes],
        far_shapes,
        flops=8 * 10**9,
        scratch=[vmem(7, levels), vmem(2, 7, levels), vmem(chunks, ITERS, levels)],
    )(meta, statics, omega, wet, volume, edges, left, right)
    far_received = swapped(far_sent, "vec", 1)

    weight_shapes = [f32(7, levels, *plane), f32(2, 7, levels, *plane)]
    weights, strip_weights = call(
        near_weight_kernel,
        [smem] + [whole(x) for x in (statics, rims, edges, left, right)],
        [whole(s) for s in weight_shapes],
        weight_shapes,
    )(meta, statics, rims, edges, left, right)

    field = None
    kept, sent = ([], [])
    near_shape = f32(group * half * rows, cols)
    for c in range(chunks):
        waits = [(halos[1],), (far_received,)]
        halo = after(halos[c], *(waits[c] if c < 2 else sent[c - 2 : c - 1]))
        chunk_block = block((group, levels, *plane), c, 0, 0, 0)
        edge_block = block((1, levels, *plane), c, 0, 0, 0)
        operands = [meta, omega, wet, volume, halo, rims, left, right, weights, strip_weights, bound, strip_bound, final]
        specs = [smem, chunk_block, whole(wet), whole(volume), whole(halo), whole(rims), edge_block, edge_block]
        specs += [whole(weights), whole(strip_weights), chunk_block, block((1, 2, levels, *plane), c, 0, 0, 0, 0), chunk_block]
        aliases = {}
        if field is not None:
            aliases = {len(operands): 0}
            operands.append(field)
            specs.append(pl.BlockSpec(memory_space=pl.ANY))
        field, keep, send = call(
            functools.partial(near_kernel, 4, c),
            specs,
            [chunk_block, whole(near_shape), whole(near_shape)],
            [f32(*omega.shape), near_shape, near_shape],
            flops=2 * 10**9,
            scratch=[vmem(ITERS, levels), vmem(group, levels)],
            aliases=aliases,
        )(*operands)
        kept.append(keep)
        sent.append(swapped(send, "vec", 1))

    order = 2 * vectors
    gram_shape = f32(order, order)
    far_gram = call(
        functools.partial(far_gram_kernel, half * rows), [whole(far_shape)] * 2, whole(gram_shape), gram_shape
    )(far_kept, far_received)
    half_gram = f32(3 * order // 8, order)
    mine, theirs = call(
        functools.partial(near_gram_kernel, half * rows),
        [smem, whole(gram_shape)] + [whole(near_shape)] * (2 * chunks),
        [whole(half_gram)] * 2,
        [half_gram] * 2,
    )(meta, far_gram, *kept, *sent)
    r_factor = factor(meta, mine, theirs, order, 1.0 / (levels * tiles * rows * cols))
    return (field, r_factor)


def solution(mesh):
    shards = shards_of_two_rows if mesh.shape["tiles"] == 2 * TGY else shards_any
    in_specs = (
        P("vec", None, "tiles", None),
        P(None, None, "tiles", None),
        P("tiles", None),
        P("tiles", None),
        P("tiles", None),
    )
    out_specs = (P("vec", None, "tiles", None), P())
    return jax.shard_map(shards, mesh=mesh, in_specs=in_specs, out_specs=out_specs, check_vma=False)
```

```python
import functools
import jax
import jax.numpy as jnp
from jax import lax
from jax.experimental import pallas as pl
from jax.experimental.pallas import tpu as pltpu
from jax.sharding import PartitionSpec as P

TGY = 8
ITERS = 4
EDGE = 2 * ITERS
VMEM_LIMIT = 32 * 1024 * 1024
EDGE_LIMIT = 63 * 1024 * 1024 + 256 * 1024
MAIN, SLOT = (0, 1)


def ids(shape, axis):
    return lax.broadcasted_iota(jnp.int32, shape, axis)


def turn(value, steps, axis):
    size = value.shape[axis]
    steps = steps % size
    return value if steps == 0 else pltpu.roll(value, steps, axis)


def low_half(shape):
    return ids(shape, 0) < ITERS


def left_lanes(shape):
    return ids(shape, 1) % EDGE < ITERS


def first_pair(a, b):
    return jnp.where(low_half(a.shape), a, turn(b, ITERS, 0))


def last_pair(a, b):
    return jnp.where(low_half(a.shape), turn(a, ITERS, 0), b)


def slots(below, above):
    low = low_half(below.shape)
    return (
        jnp.where(low, below, turn(above, ITERS, 0)),
        jnp.where(low, turn(below, ITERS, 0), above),
    )


def store_pair(outs, index, a, b, is_first_row):
    if len(outs) == 1:
        outs[0][index] = jnp.where(is_first_row, last_pair(a, b), first_pair(a, b))
    else:
        outs[0][index] = first_pair(a, b)
        outs[1][index] = last_pair(a, b)


def add_edge(acc, value, place):
    lanes = ids(value.shape, 1) // EDGE
    moved = turn(value, EDGE * place + ITERS, 1)
    return moved if acc is None else jnp.where(lanes == place, moved, acc)


def prev_row(part, other):
    return jnp.where(ids(part.shape, 0) == 0, turn(other, 1, 0), turn(part, 1, 0))


def next_row(part, other):
    last = part.shape[0] - 1
    return jnp.where(ids(part.shape, 0) == last, turn(other, -1, 0), turn(part, -1, 0))


def prev_col(part, rim):
    return jnp.where(ids(part.shape, 1) == 0, rim, turn(part, 1, 1))


def next_col(part, rim):
    last = part.shape[1] - 1
    return jnp.where(ids(part.shape, 1) == last, rim, turn(part, -1, 1))


def strips(edges, rims):
    left = left_lanes(edges.shape)
    return (jnp.where(left, rims, edges), jnp.where(left, edges, rims))


def crossing(left_strip, right_strip):
    lanes = ids(left_strip.shape, 1) % EDGE
    return jnp.where(lanes == ITERS - 1, turn(right_strip, -1, 1), turn(left_strip, 1, 1))


def rim_of(cross, place):
    return turn(cross, -(EDGE * place + ITERS), 1)


def pack_kernel(chunks, meta, runs, omega, conductance, wet, static_out, edge_out, *row_outs):
    directions = len(row_outs) // chunks
    levels, rows, cols = omega.shape[1:]
    shape = (rows, cols)
    is_first_row = meta[0] == 0
    row_ids, col_ids = (ids(shape, 0), ids(shape, 1))
    wet_cells = wet[...].astype(jnp.float32)
    open_x = (col_ids >= runs[0, 0]) & (col_ids < runs[0, 0] + runs[0, 1])
    open_y = (row_ids >= runs[0, 2]) & (row_ids < runs[0, 2] + runs[0, 3])
    keep_x = (row_ids > 0) | open_x
    keep_y = (col_ids > 0) | open_y
    statics = []
    for level in range(levels):
        statics.append(
            [
                jnp.where(keep_x, conductance[0, level], 0.0),
                jnp.where(keep_y, conductance[1, level], 0.0),
                conductance[2, level] if level else jnp.zeros(shape, jnp.float32),
                wet_cells,
            ]
        )
    kinds = len(statics[0])
    group = cols // EDGE
    for level in range(levels):
        edge = None
        for kind in range(kinds):
            static_out[kind, level] = statics[level][kind]
            edge = add_edge(edge, statics[level][kind], kind)
        edge_out[chunks, level] = edge
        for kind in range(0, kinds, 2):
            outs = row_outs[:directions]
            store_pair(outs, (group // 2 + kind // 2, level), statics[level][kind], statics[level][kind + 1], is_first_row)
        for chunk in range(chunks):
            outs = row_outs[directions * chunk : directions * (chunk + 1)]
            edge = None
            for pair in range(group // 2):
                start = [omega[chunk * group + 2 * pair + i, level] * wet_cells for i in range(2)]
                edge = add_edge(edge, start[0], 2 * pair)
                edge = add_edge(edge, start[1], 2 * pair + 1)
                store_pair(outs, (pair, level), start[0], start[1], is_first_row)
            edge_out[chunk, level] = edge


def corner_kernel(meta, left, right, *outs):
    is_first_row = meta[0] == 0
    groups, levels, rows, cols = left.shape
    take = left_lanes((rows, cols))
    for g in range(groups):
        for level in range(0, levels, 2):
            pair = [jnp.where(take, left[g, level + i], right[g, level + i]) for i in range(2)]
            store_pair(outs, (g, level // 2), pair[0], pair[1], is_first_row)


def rims_of_group(left, right, corner_below, corner_above):
    levels, rows, cols = left.shape[1:]
    take = left_lanes((rows, cols))
    rims = [[jnp.where(take, left[0, level], right[0, level]), None] for level in range(levels)]
    for level in range(0, levels, 2):
        pair = slots(corner_below[0, level // 2], corner_above[0, level // 2])
        rims[level][SLOT], rims[level + 1][SLOT] = pair
    return rims


def weight_kernel(meta, statics, below, above, edges, left, right, corner_below, corner_above, main_out, strip_out):
    kinds, levels, rows, cols = statics.shape
    shape = (rows, cols)
    low = low_half(shape)
    valid = (low & (meta[1] > 0)) | (jnp.logical_not(low) & (meta[0] > 0))
    first = below.shape[0] - kinds // 2
    rims = rims_of_group(left, right, corner_below, corner_above)
    field = [[[statics[kind, level], None] for level in range(levels)] for kind in range(kinds)]
    for level in range(levels):
        for kind in range(0, kinds, 2):
            pair = slots(below[first + kind // 2, level], above[first + kind // 2, level])
            for i in range(2):
                field[kind + i][level][SLOT] = jnp.where(valid, pair[i], 0.0)
    width = cols // EDGE
    lanes = ids(shape, 1) // EDGE

    def spread(strip, kind):
        value = jnp.where(lanes == 0, turn(strip, -EDGE * kind, 1), 0.0)
        span = 1
        while span < width:
            value = value + turn(value, EDGE * span, 1)
            span *= 2
        return value

    side = [[[[None, None] for _ in range(levels)] for _ in range(kinds)] for _ in range(2)]
    cross = [[None, None] for _ in range(levels)]
    for level in range(levels):
        for part in range(2):
            edge = edges[0, level] if part == MAIN else None
            if part == SLOT:
                for kind in range(kinds):
                    edge = add_edge(edge, field[kind][level][SLOT], kind)
            rim = rims[level][part]
            if part == SLOT:
                rim = jnp.where(valid, rim, 0.0)
            pair = strips(edge, rim)
            cross[level][part] = crossing(pair[0], pair[1])
            for s in range(2):
                for kind in range(kinds):
                    side[s][kind][level][part] = spread(pair[s], kind)

    def emit(out, values, after_of):
        for level in range(levels):
            for part in range(2):
                cond_x, cond_y, cond_z, wet = (values[kind][level][part] for kind in range(kinds))
                faces = [
                    cond_x,
                    next_row(cond_x, values[0][level][1 - part]),
                    cond_y,
                    after_of(cond_y, level, part),
                    cond_z,
                    values[2][level + 1][part] if level + 1 < levels else jnp.zeros(shape, jnp.float32),
                ]
                total = faces[0]
                for face in faces[1:]:
                    total = total + face
                out[0, level, part] = wet * (1.0 - total)
                for index, face in enumerate(faces):
                    out[index + 1, level, part] = wet * face

    emit(main_out, field, lambda cond, level, part: next_col(cond, rim_of(cross[level][part], 1)))
    for s in range(2):
        emit(strip_out.at[s], side[s], lambda cond, level, part: turn(cond, -1, 1))


def one_pass(state, weight, parts, rim_at):
    levels = len(state)
    result = [[None, None] for _ in range(levels)]
    for level in range(levels):
        for part in parts:
            value, other = (state[level][part], state[level][1 - part])
            rim = rim_at(level, part)
            before = turn(value, 1, 1) if rim is None else prev_col(value, rim)
            after = turn(value, -1, 1) if rim is None else next_col(value, rim)
            total = weight(0, level, part) * value
            total = total + weight(1, level, part) * prev_row(value, other)
            total = total + weight(2, level, part) * next_row(value, other)
            total = total + weight(3, level, part) * before
            total = total + weight(4, level, part) * after
            if level > 0:
                total = total + weight(5, level, part) * state[level - 1][part]
            if level < levels - 1:
                total = total + weight(6, level, part) * state[level + 1][part]
            result[level][part] = total
    return result


def diffuse_kernel(
    batch, meta, omega, wet, volume, below, above, edges, left, right, corner_below, corner_above,
    main_weights, strip_weights, *rest
):
    field_out, keep_out, send_out, cross_scratch, slot_scratch = rest[-5:]
    group, levels, rows, cols = omega.shape
    shape = (rows, cols)
    wet_cells = wet[...].astype(jnp.float32)
    root = jnp.sqrt(volume[...])
    half = levels // 2
    keeps_low = meta[2] == 0
    rims = rims_of_group(left, right, corner_below, corner_above)
    slot_edges = [None] * levels
    for level in range(levels):
        for pair in range(group // 2):
            two = slots(below[pair, level], above[pair, level])
            for i in range(2):
                slot_scratch[2 * pair + i, level] = two[i]
                slot_edges[level] = add_edge(slot_edges[level], two[i], 2 * pair + i)
    state = [[[None, None] for _ in range(levels)] for _ in range(2)]
    for level in range(levels):
        for part in range(2):
            edge = edges[0, level] if part == MAIN else slot_edges[level]
            pair = strips(edge, rims[level][part])
            for s in range(2):
                state[s][level][part] = pair[s]
    for sweep in range(ITERS):
        for level in range(levels):
            for part in range(2):
                cross_scratch[sweep, level, part] = crossing(state[0][level][part], state[1][level][part])
        if sweep < ITERS - 1:
            for s in range(2):
                state[s] = one_pass(
                    state[s], lambda n, level, part: strip_weights[s, n, level, part], (MAIN, SLOT), lambda level, part: None
                )

    for first in range(0, group, batch):
        fields = []
        for place in range(first, first + batch):
            fields.append([[omega[place, level] * wet_cells, slot_scratch[place, level]] for level in range(levels)])
        for sweep in range(ITERS):
            parts = (MAIN, SLOT) if sweep < ITERS - 1 else (MAIN,)
            for i in range(batch):
                fields[i] = one_pass(
                    fields[i],
                    lambda n, level, part: main_weights[n, level, part],
                    parts,
                    lambda level, part: rim_of(cross_scratch[sweep, level, part], first + i),
                )
        for i in range(batch):
            scaled = []
            for level in range(levels):
                value = fields[i][level][MAIN]
                field_out[first + i, level] = value
                scaled.append(value * root)
            for level in range(half):
                at = ((first + i) * half + level) * rows
                keep_out[at : at + rows, :] = jnp.where(keeps_low, scaled[level], scaled[half + level])
                send_out[at : at + rows, :] = jnp.where(keeps_low, scaled[half + level], scaled[level])


def gram_of_rows(slices, refs):
    groups = [ref.shape[0] // slices for ref in refs]
    order = sum(groups)
    exact = jnp.zeros((order, order), jnp.float32)
    cross = jnp.zeros((order, order), jnp.float32)
    for at in range(0, slices, 2):
        columns = []
        for i in range(2):
            picked = [ref[pl.ds(at + i, group, slices), :] for ref, group in zip(refs, groups)]
            columns.append(jnp.concatenate(picked, axis=0))
        values = jnp.concatenate(columns, axis=1)
        high = values.astype(jnp.bfloat16)
        rest = (values - high.astype(jnp.float32)).astype(jnp.bfloat16)
        dims = (((1,), (1,)), ((), ()))
        exact = exact + lax.dot_general(high, high, dims, preferred_element_type=jnp.float32)
        cross = cross + lax.dot_general(high, rest, dims, preferred_element_type=jnp.float32)
    return exact + (cross + cross.T)


def store_halves(meta, gram, mine, theirs):
    order = gram.shape[0]
    moved = turn(turn(gram, order // 2, 0), order // 2, 1)
    first, second = halves_of_gram(jnp.where(meta[2] == 0, gram, moved))
    is_first = meta[3] == 0
    mine[...] = jnp.where(is_first, first, second)
    theirs[...] = jnp.where(is_first, second, first)


def gram_kernel(chunks, slices, meta, *refs):
    store_halves(meta, gram_of_rows(slices, refs[:-2]), *refs[-2:])


def far_gram_kernel(slices, kept, received, out):
    out[...] = gram_of_rows(slices, (kept, received))


def near_gram_kernel(slices, meta, far, *refs):
    store_halves(meta, far[...] + gram_of_rows(slices, refs[:-2]), *refs[-2:])


def swapped(value, axis, bit):
    count = lax.axis_size(axis)
    return lax.ppermute(value, axis, [(source, source ^ bit) for source in range(count)])


def mesh_permute(value, mask):
    axes = ("tiles", "vec")
    count = lax.axis_size("tiles") * lax.axis_size("vec")
    return lax.ppermute(value, axes, [(source, source ^ mask) for source in range(count)])


def total_over_chips(value):
    vec = lax.axis_size("vec")
    masks = []
    bit = 1
    while bit < vec:
        masks.append(bit)
        bit *= 2
    bit = 2
    while bit < lax.axis_size("tiles"):
        masks.append(bit * vec)
        bit *= 2
    while masks:
        near, masks = (masks[:2], masks[2:])
        if len(near) == 1:
            value = value + mesh_permute(value, near[0])
        else:
            one, two, both = (mesh_permute(value, mask) for mask in (near[0], near[1], near[0] ^ near[1]))
            value = (value + one) + (two + both)
    return value


def fold(a, b):
    half = a.shape[1] // 2
    return jnp.where(ids(a.shape, 1) < half, a, b)


def flip(value):
    return turn(value, value.shape[1] // 2, 1)


def halves_of_gram(gram):
    q = gram.shape[0] // 8
    first = [fold(gram[: 2 * q], flip(gram[2 * q : 4 * q])), fold(flip(gram[:q]), gram[q : 2 * q])]
    second = [fold(flip(gram[4 * q : 6 * q]), gram[6 * q :]), fold(flip(gram[2 * q : 3 * q]), gram[3 * q : 4 * q])]
    return (jnp.concatenate(first, axis=0), jnp.concatenate(second, axis=0))


def gram_of_halves(first, second):
    q = first.shape[0] // 3
    return jnp.concatenate(
        [
            fold(first[:q], flip(first[2 * q :])),
            fold(first[q : 2 * q], first[2 * q :]),
            fold(flip(first[:q]), flip(second[2 * q :])),
            fold(flip(first[q : 2 * q]), second[2 * q :]),
            flip(second[: 2 * q]),
            second[: 2 * q],
        ],
        axis=0,
    )


def spread_lane(value, lane):
    return jnp.broadcast_to(value[:, lane : lane + 1], value.shape)


def squares(rows):
    high = rows.astype(jnp.bfloat16).astype(jnp.float32)
    rest = rows - high
    middle = rest.astype(jnp.bfloat16).astype(jnp.float32)
    low = rest - middle
    one = jnp.concatenate([high, high, middle, high, low, middle], axis=0).astype(jnp.bfloat16)
    two = jnp.concatenate([high, middle, high, low, high, middle], axis=0).astype(jnp.bfloat16)
    return lax.dot_general(one, two, (((0,), (0,)), ((), ())), preferred_element_type=jnp.float32)


def factor_kernel(scale, meta, own, other, out_ref):
    order = out_ref.shape[0]
    height = 8
    count = order // height
    shape = (height, order)
    is_first = meta[3] == 0
    mine, theirs = (own[...], other[...])
    gram = gram_of_halves(jnp.where(is_first, mine, theirs), jnp.where(is_first, theirs, mine)) * scale
    blocks = [gram[height * b : height * (b + 1), :] for b in range(count)]
    row_ids, col_ids = (ids(shape, 0), ids(shape, 1))
    previous = None
    for p in range(count):
        base = height * p
        rows = [jnp.broadcast_to(blocks[p][j : j + 1, :], shape) for j in range(height)]
        corner = {(i, j): spread_lane(rows[j], base + i) for j in range(height) for i in range(j, height)}
        if previous is not None:
            for done in previous:
                lanes = [spread_lane(done, base + j) for j in range(height)]
                for j in range(height):
                    rows[j] = rows[j] - lanes[j] * done
                    for i in range(j, height):
                        corner[i, j] = corner[i, j] - lanes[i] * lanes[j]
        panel = jnp.zeros(shape, jnp.float32)
        for s in range(height):
            inverse = lax.rsqrt(corner[s, s])
            rows[s] = rows[s] * inverse
            lanes = {j: corner[j, s] * inverse for j in range(s + 1, height)}
            for j in range(s + 1, height):
                for i in range(j, height):
                    corner[i, j] = corner[i, j] - lanes[i] * lanes[j]
                rows[j] = rows[j] - lanes[j] * rows[s]
            panel = jnp.where(row_ids == s, rows[s], panel)
        panel = jnp.where(col_ids >= base + row_ids, panel, 0.0)
        out_ref[base : base + height, :] = panel
        if p + 2 < count:
            update = squares(panel)
            for q in range(p + 2, count):
                blocks[q] = blocks[q] - update[height * q : height * (q + 1), :]
        previous = rows


def edge_kernel(runs, omega, conductance, wet, static_out, edge_out):
    levels, rows, cols = omega.shape[1:]
    shape = (rows, cols)
    row_ids, col_ids = (ids(shape, 0), ids(shape, 1))
    wet_cells = wet[...].astype(jnp.float32)
    open_x = (col_ids >= runs[0, 0]) & (col_ids < runs[0, 0] + runs[0, 1])
    open_y = (row_ids >= runs[0, 2]) & (row_ids < runs[0, 2] + runs[0, 3])
    keep_x = (row_ids > 0) | open_x
    keep_y = (col_ids > 0) | open_y
    group = cols // EDGE
    chunks = omega.shape[0] // group
    for level in range(levels):
        statics = [
            jnp.where(keep_x, conductance[0, level], 0.0),
            jnp.where(keep_y, conductance[1, level], 0.0),
            conductance[2, level] if level else jnp.zeros(shape, jnp.float32),
            wet_cells,
        ]
        edge = None
        for kind, value in enumerate(statics):
            static_out[kind, level] = value
            edge = add_edge(edge, value, kind)
        edge_out[chunks, level] = edge
        for chunk in range(chunks):
            edge = None
            for place in range(group):
                edge = add_edge(edge, omega[chunk * group + place, level] * wet_cells, place)
            edge_out[chunk, level] = edge


def face_kernel(first, meta, omega, wet, *row_outs):
    levels, rows, cols = omega.shape[1:]
    group = cols // EDGE
    is_first_row = meta[0] == 0
    wet_cells = wet[...].astype(jnp.float32)
    for chunk, out in enumerate(row_outs):
        for level in range(levels):
            for pair in range(group // 2):
                at = (first + chunk) * group + 2 * pair
                start = [omega[at + i, level] * wet_cells for i in range(2)]
                store_pair((out,), (pair, level), start[0], start[1], is_first_row)


def rim_kernel(meta, statics, left, right, out):
    is_first_row = meta[0] == 0
    groups, levels, rows, cols = left.shape
    kinds = statics.shape[0]
    take = left_lanes((rows, cols))
    for g in range(groups):
        for level in range(0, levels, 2):
            pair = [jnp.where(take, left[g, level + i], right[g, level + i]) for i in range(2)]
            store_pair((out,), g * levels // 2 + level // 2, pair[0], pair[1], is_first_row)
    first = groups * levels // 2
    for kind in range(0, kinds, 2):
        for level in range(levels):
            at = first + kind // 2 * levels + level
            store_pair((out,), at, statics[kind, level], statics[kind + 1, level], is_first_row)


def near_rows(is_first_row, a, b, halo):
    low = low_half(halo.shape)
    turned = turn(halo, ITERS, 0)
    result = []
    for own, across, moved in ((a, halo, turned), (b, turned, halo)):
        near = turn(own, ITERS, 0)
        result.append(jnp.where(low, jnp.where(is_first_row, near, across), jnp.where(is_first_row, moved, near)))
    return result


def spread_kind(strip, kind):
    cols = strip.shape[1]
    value = jnp.where(ids(strip.shape, 1) // EDGE == 0, turn(strip, -EDGE * kind, 1), 0.0)
    span = EDGE
    while span < cols:
        value = value + turn(value, span, 1)
        span *= 2
    return value


def store_weights(out, values, after_row, after_col):
    levels = len(values[0])
    for level in range(levels):
        cond_x, cond_y, cond_z, wet = (kind[level] for kind in values)
        below = values[2][level + 1] if level + 1 < levels else jnp.zeros_like(cond_z)
        faces = [cond_x, after_row(level), cond_y, after_col(level), cond_z, below]
        total = faces[0]
        for face in faces[1:]:
            total = total + face
        out[0, level] = wet * (1.0 - total)
        for index, face in enumerate(faces):
            out[index + 1, level] = wet * face


def plane_pass(state, weight, row_before, row_after, rim_at):
    levels = len(state)
    result = []
    for level in range(levels):
        value = state[level]
        rim = rim_at(level)
        before = turn(value, 1, 1) if rim is None else prev_col(value, rim)
        after = turn(value, -1, 1) if rim is None else next_col(value, rim)
        total = weight(0, level) * value
        total = total + weight(1, level) * row_before(value, level)
        total = total + weight(2, level) * row_after(value, level)
        total = total + weight(3, level) * before
        total = total + weight(4, level) * after
        if level > 0:
            total = total + weight(5, level) * state[level - 1]
        if level < levels - 1:
            total = total + weight(6, level) * state[level + 1]
        result.append(total)
    return result


def no_rim(level):
    return None


def pack_levels(values, use_first):
    pairs = []
    for level in range(0, len(values), 2):
        a, b = values[level : level + 2]
        pairs.append(jnp.where(use_first, first_pair(a, b), last_pair(a, b)))
    return pairs


def store_half(keep, send, place, pairs, keeps_low):
    rows = pairs[0].shape[0]
    half = len(pairs) // 2
    for i in range(half):
        at = (place * half + i) * rows
        keep[at : at + rows, :] = jnp.where(keeps_low, pairs[i], pairs[half + i])
        send[at : at + rows, :] = jnp.where(keeps_low, pairs[half + i], pairs[i])


def far_kernel(
    batch, meta, statics, omega, wet, volume, edges, left, right,
    final_out, bound_out, strip_bound_out, keep_out, send_out, weights, strip_weights, cross_scratch
):
    vectors, levels, rows, cols = omega.shape
    kinds = statics.shape[0]
    shape = (rows, cols)
    group = cols // EDGE
    chunks = vectors // group
    is_first_row = meta[0] == 0
    keeps_low = meta[2] == 0
    row_ids = ids(shape, 0)
    take = left_lanes(shape)
    wet_cells = wet[...].astype(jnp.float32)
    root = jnp.sqrt(volume[...])

    def sides(g, level):
        return strips(edges[g, level], jnp.where(take, left[g, level], right[g, level]))

    def roll_before(value, level):
        return turn(value, 1, 0)

    def roll_after(value, level):
        return turn(value, -1, 0)

    def closed_after(value):
        return jnp.where(row_ids == rows - 1, 0.0, turn(value, -1, 0))

    field = [[statics[kind, level] for level in range(levels)] for kind in range(kinds)]
    pairs = [sides(chunks, level) for level in range(levels)]
    crosses = [crossing(*pair) for pair in pairs]
    store_weights(
        weights, field, lambda level: closed_after(field[0][level]),
        lambda level: next_col(field[1][level], rim_of(crosses[level], 1)),
    )
    for s in range(2):
        side = [[spread_kind(pairs[level][s], kind) for level in range(levels)] for kind in range(kinds)]
        store_weights(
            strip_weights.at[s], side, lambda level: closed_after(side[0][level]), lambda level: turn(side[1][level], -1, 1)
        )

    def keep_bound(acc, value, sweep):
        edge = jnp.where(is_first_row, value, turn(value, -1, 0))
        moved = turn(edge, sweep - (ITERS - 1), 0)
        return moved if acc is None else jnp.where(row_ids == sweep, moved, acc)

    for g in range(chunks):
        state = [[sides(g, level)[s] for level in range(levels)] for s in range(2)]
        bounds = [[None] * levels for _ in range(2)]
        for sweep in range(ITERS):
            for level in range(levels):
                cross_scratch[g, sweep, level] = crossing(state[0][level], state[1][level])
                for s in range(2):
                    bounds[s][level] = keep_bound(bounds[s][level], state[s][level], sweep)
            if sweep < ITERS - 1:
                for s in range(2):
                    state[s] = plane_pass(
                        state[s], lambda n, level: strip_weights[s, n, level], roll_before, roll_after, no_rim
                    )
        for s in range(2):
            for level in range(levels):
                strip_bound_out[g, s, level] = bounds[s][level]

    for first in range(0, vectors, batch):
        g = first // group
        fields = [[omega[place, level] * wet_cells for level in range(levels)] for place in range(first, first + batch)]
        bounds = [[None] * levels for _ in range(batch)]
        for sweep in range(ITERS):
            for i in range(batch):
                for level in range(levels):
                    bounds[i][level] = keep_bound(bounds[i][level], fields[i][level], sweep)
                fields[i] = plane_pass(
                    fields[i], lambda n, level: weights[n, level], roll_before, roll_after,
                    lambda level: rim_of(cross_scratch[g, sweep, level], (first + i) % group),
                )
        for i in range(batch):
            for level in range(levels):
                final_out[first + i, level] = fields[i][level]
                bound_out[first + i, level] = bounds[i][level]
            scaled = [value * root for value in fields[i]]
            store_half(keep_out, send_out, first + i, pack_levels(scaled, is_first_row), keeps_low)


def near_weight_kernel(meta, statics, rims, edges, left, right, weights, strip_weights):
    kinds, levels, rows, cols = statics.shape
    shape = (rows, cols)
    is_first_row = meta[0] == 0
    take = left_lanes(shape)
    last = ids(shape, 0) == rows - 1
    g = edges.shape[0] - 1
    groups = edges.shape[0]
    first = groups * levels // 2
    field = [[None] * levels for _ in range(kinds)]
    for kind in range(0, kinds, 2):
        for level in range(levels):
            own = (statics[kind, level], statics[kind + 1, level])
            pair = near_rows(is_first_row, *own, rims[first + kind // 2 * levels + level])
            field[kind][level], field[kind + 1][level] = pair
    rim = [jnp.where(take, left[g, level], right[g, level]) for level in range(levels)]
    near_rim = []
    for level in range(0, levels, 2):
        near_rim += near_rows(is_first_row, rim[level], rim[level + 1], rims[g * levels // 2 + level // 2])
    near_edge = []
    for level in range(levels):
        edge = None
        for kind in range(kinds):
            edge = add_edge(edge, field[kind][level], kind)
        near_edge.append(edge)
    pairs = [strips(near_edge[level], near_rim[level]) for level in range(levels)]
    tile_pairs = [strips(edges[g, level], rim[level]) for level in range(levels)]
    crosses = [crossing(*pair) for pair in pairs]

    def with_next(value, tile_value):
        beyond = jnp.broadcast_to(tile_value[ITERS : ITERS + 1, :], shape)
        return jnp.where(last, beyond, turn(value, -1, 0))

    store_weights(
        weights, field, lambda level: with_next(field[0][level], statics[0, level]),
        lambda level: next_col(field[1][level], rim_of(crosses[level], 1)),
    )
    for s in range(2):
        side = [[spread_kind(pairs[level][s], kind) for level in range(levels)] for kind in range(kinds)]
        tile_side = [spread_kind(tile_pairs[level][s], 0) for level in range(levels)]
        store_weights(
            strip_weights.at[s], side, lambda level: with_next(side[0][level], tile_side[level]),
            lambda level: turn(side[1][level], -1, 1),
        )


def near_kernel(
    batch, base, parts, meta, omega, wet, volume, rims, left, right, weights, strip_weights, bound, strip_bound, final, *rest
):
    halos = rest[:parts]
    field_out, keep_out, send_out, cross_scratch, start = rest[-5:]
    levels, rows, cols = omega.shape[1:]
    group = omega.shape[0] // parts
    shape = (rows, cols)
    is_first_row = meta[0] == 0
    keeps_low = meta[2] == 0
    row_ids = ids(shape, 0)
    take = left_lanes(shape)
    top = (row_ids == 0) & is_first_row
    bottom = (row_ids == rows - 1) & jnp.logical_not(is_first_row)
    is_near = low_half(shape) != is_first_row
    wet_cells = wet[...].astype(jnp.float32)
    root = jnp.sqrt(volume[...])

    def around(bound_at, sweep):
        def kept(level):
            return jnp.broadcast_to(bound_at(level)[sweep : sweep + 1, :], shape)

        return (
            lambda value, level: jnp.where(top, kept(level), turn(value, 1, 0)),
            lambda value, level: jnp.where(bottom, kept(level), turn(value, -1, 0)),
        )

    for part in range(parts):
        near_edge = [None] * levels
        for level in range(levels):
            for pair in range(group // 2):
                at = part * group + 2 * pair
                own = [omega[at + i, level] * wet_cells for i in range(2)]
                two = near_rows(is_first_row, *own, halos[part][pair, level])
                for i in range(2):
                    start[at + i, level] = two[i]
                    near_edge[level] = add_edge(near_edge[level], two[i], 2 * pair + i)
        rim = [jnp.where(take, left[part, level], right[part, level]) for level in range(levels)]
        near_rim = []
        for level in range(0, levels, 2):
            across = rims[(base + part) * levels // 2 + level // 2]
            near_rim += near_rows(is_first_row, rim[level], rim[level + 1], across)
        pairs = [strips(near_edge[level], near_rim[level]) for level in range(levels)]
        state = [[pairs[level][s] for level in range(levels)] for s in range(2)]
        for sweep in range(ITERS):
            for level in range(levels):
                cross_scratch[part, sweep, level] = crossing(state[0][level], state[1][level])
            if sweep < ITERS - 1:
                for s in range(2):
                    state[s] = plane_pass(
                        state[s], lambda n, level: strip_weights[s, n, level],
                        *around(lambda level: strip_bound[part, s, level], sweep), no_rim,
                    )

    for first in range(0, parts * group, batch):
        part = first // group
        fields = [[start[place, level] for level in range(levels)] for place in range(first, first + batch)]
        for sweep in range(ITERS):
            for i in range(batch):
                fields[i] = plane_pass(
                    fields[i], lambda n, level: weights[n, level],
                    *around(lambda level: bound[first + i, level], sweep),
                    lambda level: rim_of(cross_scratch[part, sweep, level], (first + i) % group),
                )
        for i in range(batch):
            scaled = []
            for level in range(levels):
                value = jnp.where(is_near, turn(fields[i][level], ITERS, 0), final[first + i, level])
                field_out[first + i, level] = value
                scaled.append(value * root)
            store_half(keep_out, send_out, first + i, pack_levels(scaled, jnp.logical_not(is_first_row)), keeps_low)


def shifted(value, axis, steps):
    count = lax.axis_size(axis)
    first, last = (max(0, -steps), min(count, count - steps))
    return lax.ppermute(value, axis, [(source, source + steps) for source in range(first, last)])


def beside(value, steps):
    count = lax.axis_size("tiles")
    pairs = [(source, source + steps) for source in range(count)]
    return lax.ppermute(value, "tiles", [(a, b) for a, b in pairs if 0 <= b < count and a // TGY == b // TGY])


def after(values, *done):
    return lax.optimization_barrier((values, done))[0]


def exchange_rows(messages, grid_rows):
    if len(messages) == 1:
        received = swapped(messages[0], "tiles", TGY)
        return (received, received)
    return (shifted(messages[0], "tiles", -TGY), shifted(messages[1], "tiles", TGY))


def f32(*shape):
    return jax.ShapeDtypeStruct(shape, jnp.float32)


def block(shape, *at):
    return pl.BlockSpec(shape, lambda i: at)


def call(kernel, in_specs, out_specs, out_shape, flops=0, scratch=(), aliases=None, limit=VMEM_LIMIT):
    return pl.pallas_call(
        kernel,
        grid=(1,),
        in_specs=in_specs,
        out_specs=out_specs,
        out_shape=out_shape,
        scratch_shapes=scratch,
        input_output_aliases=aliases or {},
        compiler_params=pltpu.CompilerParams(vmem_limit_bytes=limit),
        cost_estimate=pl.CostEstimate(flops=flops, bytes_accessed=1 << 20, transcendentals=0),
    )


def whole(array):
    zeros = (0,) * array.ndim
    return pl.BlockSpec(array.shape, lambda i: zeros)


def factor(meta, mine, theirs, order, scale):
    mine = total_over_chips(mine + swapped(theirs, "tiles", 1))
    smem = pl.BlockSpec(memory_space=pltpu.SMEM)
    return call(
        functools.partial(factor_kernel, scale),
        [smem, whole(mine), whole(mine)],
        whole(f32(order, order)),
        f32(order, order),
    )(meta, mine, swapped(mine, "tiles", 1))


def shards_any(omega, conductance, wet, volume, face_runs):
    vectors, levels, rows, cols = omega.shape
    tiles = lax.axis_size("tiles")
    grid_rows = tiles // TGY
    tile_row = lax.axis_index("tiles") // TGY
    core = lax.axis_index("tiles") % 2
    meta = jnp.stack([tile_row, grid_rows - 1 - tile_row, lax.axis_index("vec"), core]).astype(jnp.int32)
    smem = pl.BlockSpec(memory_space=pltpu.SMEM)
    group = cols // EDGE
    chunks = vectors // group
    directions = 1 if grid_rows == 2 else 2
    kinds = 4
    half = levels // 2

    row_shapes = [f32(group // 2 + (kinds // 2 if c == 0 else 0), levels, rows, cols) for c in range(chunks)]
    row_shapes = [shape for shape in row_shapes for _ in range(directions)]
    packed_shapes = [f32(kinds, levels, rows, cols), f32(chunks + 1, levels, rows, cols)] + row_shapes
    statics, edges, *messages = call(
        functools.partial(pack_kernel, chunks),
        [smem, smem, whole(omega), whole(conductance), whole(wet)],
        [whole(s) for s in packed_shapes],
        packed_shapes,
    )(meta, face_runs, omega, conductance, wet)
    messages = [messages[directions * c : directions * (c + 1)] for c in range(chunks)]
    received = [exchange_rows(messages[0], grid_rows)]
    left = beside(edges, 1)
    right = beside(edges, -1)
    corner_shapes = [f32(chunks + 1, levels // 2, rows, cols)] * directions
    corners = call(
        corner_kernel, [smem, whole(left), whole(right)], [whole(s) for s in corner_shapes], corner_shapes
    )(meta, left, right)
    corners = exchange_rows(corners, grid_rows)
    gates = [(left, right), corners]
    for c in range(1, chunks):
        gate = gates[c - 1] if c <= 2 else received[c - 2]
        received.append(exchange_rows(after(messages[c], *gate), grid_rows))

    def group_specs(c):
        edge = block((1, levels, rows, cols), c, 0, 0, 0)
        corner = block((1, levels // 2, rows, cols), c, 0, 0, 0)
        return [edge, edge, edge, corner, corner]

    around = (edges, left, right, *corners)
    weight_shapes = [f32(7, levels, 2, rows, cols), f32(2, 7, levels, 2, rows, cols)]
    main_weights, strip_weights = call(
        weight_kernel,
        [smem, whole(statics), whole(received[0][0]), whole(received[0][1])] + group_specs(chunks),
        [whole(s) for s in weight_shapes],
        weight_shapes,
    )(meta, statics, *received[0], *around)

    field = None
    kept, sent = ([], [])
    half_shape = f32(group * half * rows, cols)
    for c in range(chunks):
        rims = after(received[c], sent[c - 2]) if c >= 2 else received[c]
        operands = [meta, omega, wet, volume, *rims, *around, main_weights, strip_weights]
        row_block = block((group // 2, levels, rows, cols), 0, 0, 0, 0)
        chunk_block = block((group, levels, rows, cols), c, 0, 0, 0)
        specs = [smem, chunk_block, whole(wet), whole(volume), row_block, row_block] + group_specs(c)
        specs += [whole(main_weights), whole(strip_weights)]
        aliases = {}
        if field is not None:
            aliases = {len(operands): 0}
            operands.append(field)
            specs.append(pl.BlockSpec(memory_space=pl.ANY))
        field, keep, send = call(
            functools.partial(diffuse_kernel, 4),
            specs,
            [chunk_block, whole(half_shape), whole(half_shape)],
            [f32(*omega.shape), half_shape, half_shape],
            flops=4 * 10**9,
            scratch=[pltpu.VMEM((ITERS, levels, 2, rows, cols), jnp.float32), pltpu.VMEM((group, levels, rows, cols), jnp.float32)],
            aliases=aliases,
        )(*operands)
        kept.append(keep)
        sent.append(swapped(send, "vec", 1))

    order = 2 * vectors
    half_gram = f32(3 * order // 8, order)
    mine, theirs = call(
        functools.partial(gram_kernel, chunks, half * rows),
        [smem] + [whole(half_shape)] * (2 * chunks),
        [whole(half_gram)] * 2,
        [half_gram] * 2,
    )(meta, *kept, *sent)
    r_factor = factor(meta, mine, theirs, order, 1.0 / (levels * tiles * rows * cols))
    return (field, r_factor)


def shards_of_two_rows(omega, conductance, wet, volume, face_runs):
    vectors, levels, rows, cols = omega.shape
    tiles = lax.axis_size("tiles")
    tile_row = lax.axis_index("tiles") // TGY
    core = lax.axis_index("tiles") % 2
    meta = jnp.stack([tile_row, 1 - tile_row, lax.axis_index("vec"), core]).astype(jnp.int32)
    smem = pl.BlockSpec(memory_space=pltpu.SMEM)
    group = cols // EDGE
    chunks = vectors // group
    kinds = 4
    half = levels // 4
    plane = (rows, cols)

    def vmem(*lead):
        return pltpu.VMEM(lead + plane, jnp.float32)

    row_shape = f32(group // 2, levels, *plane)
    chunk0 = call(
        functools.partial(face_kernel, 0),
        [smem, block((group, levels, *plane), 0, 0, 0, 0), whole(wet)],
        [whole(row_shape)],
        [row_shape],
        limit=EDGE_LIMIT,
    )(meta, omega, wet)
    edge_shapes = [f32(kinds, levels, *plane), f32(chunks + 1, levels, *plane)]
    statics, edges = call(
        edge_kernel,
        [smem, whole(omega), whole(conductance), whole(wet)],
        [whole(s) for s in edge_shapes],
        edge_shapes,
        limit=EDGE_LIMIT,
    )(after(face_runs, chunk0), omega, conductance, wet)
    left = beside(edges, 1)
    right = beside(edges, -1)
    row_shapes = [row_shape] * (chunks - 1)
    messages = chunk0 + call(
        functools.partial(face_kernel, 1),
        [smem, whole(omega), whole(wet)],
        [whole(s) for s in row_shapes],
        row_shapes,
        flops=10**9,
    )(meta, omega, wet)
    halos = [swapped(messages[0], "tiles", TGY)]
    rim_shape = f32((chunks + 1) * levels // 2 + kinds // 2 * levels, *plane)
    rims = call(rim_kernel, [smem, whole(statics), whole(left), whole(right)], whole(rim_shape), rim_shape)(
        meta, statics, left, right
    )
    rims = swapped(rims, "tiles", TGY)
    gates = [(left, right), (halos[0], rims)]
    for c in range(1, min(chunks, 3)):
        halos.append(swapped(after(messages[c], gates[c - 1]), "tiles", TGY))

    far_shape = f32(vectors * half * rows, cols)
    far_shapes = [f32(*omega.shape), f32(*omega.shape), f32(chunks, 2, levels, *plane), far_shape, far_shape]
    final, bound, strip_bound, far_kept, far_sent = call(
        functools.partial(far_kernel, 4),
        [smem] + [whole(x) for x in (statics, omega, wet, volume, edges, left, right)],
        [whole(s) for s in far_shapes],
        far_shapes,
        flops=8 * 10**9,
        scratch=[vmem(7, levels), vmem(2, 7, levels), vmem(chunks, ITERS, levels)],
    )(meta, statics, omega, wet, volume, edges, left, right)
    far_received = swapped(far_sent, "vec", 1)

    weight_shapes = [f32(7, levels, *plane), f32(2, 7, levels, *plane)]
    weights, strip_weights = call(
        near_weight_kernel,
        [smem] + [whole(x) for x in (statics, rims, edges, left, right)],
        [whole(s) for s in weight_shapes],
        weight_shapes,
    )(meta, statics, rims, edges, left, right)

    field = None
    kept, sent = ([], [])
    steps = [(0, 2)] + [(c, 1) for c in range(2, chunks)]
    for base, parts in steps:
        waits = [(), (far_received,)]
        mine = after(halos[base : base + parts], *(waits[len(sent)] if len(sent) < 2 else ()))
        chunk_block = block((parts * group, levels, *plane), base // parts, 0, 0, 0)
        edge_block = block((parts, levels, *plane), base // parts, 0, 0, 0)
        side_block = block((parts, 2, levels, *plane), base // parts, 0, 0, 0, 0)
        operands = [meta, omega, wet, volume, rims, left, right, weights, strip_weights, bound, strip_bound, final, *mine]
        specs = [smem, chunk_block, whole(wet), whole(volume), whole(rims), edge_block, edge_block]
        specs += [whole(weights), whole(strip_weights), chunk_block, side_block, chunk_block]
        specs += [whole(halo) for halo in mine]
        aliases = {}
        if field is not None:
            aliases = {len(operands): 0}
            operands.append(field)
            specs.append(pl.BlockSpec(memory_space=pl.ANY))
        near_shape = f32(parts * group * half * rows, cols)
        field, keep, send = call(
            functools.partial(near_kernel, 4, base, parts),
            specs,
            [chunk_block, whole(near_shape), whole(near_shape)],
            [f32(*omega.shape), near_shape, near_shape],
            flops=2 * 10**9,
            scratch=[vmem(parts, ITERS, levels), vmem(parts * group, levels)],
            aliases=aliases,
        )(*operands)
        kept.append(keep)
        sent.append(swapped(send, "vec", 1))
        if len(halos) < chunks:
            halos.append(swapped(after(messages[len(halos)], keep), "tiles", TGY))

    order = 2 * vectors
    gram_shape = f32(order, order)
    far_gram = call(
        functools.partial(far_gram_kernel, half * rows), [whole(far_shape)] * 2, whole(gram_shape), gram_shape
    )(far_kept, far_received)
    half_gram = f32(3 * order // 8, order)
    mine, theirs = call(
        functools.partial(near_gram_kernel, half * rows),
        [smem, whole(gram_shape)] + [whole(x) for x in kept + sent],
        [whole(half_gram)] * 2,
        [half_gram] * 2,
    )(meta, far_gram, *kept, *sent)
    r_factor = factor(meta, mine, theirs, order, 1.0 / (levels * tiles * rows * cols))
    return (field, r_factor)


def solution(mesh):
    shards = shards_of_two_rows if mesh.shape["tiles"] == 2 * TGY else shards_any
    in_specs = (
        P("vec", None, "tiles", None),
        P(None, None, "tiles", None),
        P("tiles", None),
        P("tiles", None),
        P("tiles", None),
    )
    out_specs = (P("vec", None, "tiles", None), P())
    return jax.shard_map(shards, mesh=mesh, in_specs=in_specs, out_specs=out_specs, check_vma=False)
```

```python
import functools
import jax
import jax.numpy as jnp
from jax import lax
from jax.experimental import pallas as pl
from jax.experimental.pallas import tpu as pltpu
from jax.sharding import PartitionSpec as P

TGY = 8
ITERS = 4
EDGE = 2 * ITERS
VMEM_LIMIT = 32 * 1024 * 1024
EDGE_LIMIT = 63 * 1024 * 1024 + 256 * 1024
MAIN, SLOT = (0, 1)


def ids(shape, axis):
    return lax.broadcasted_iota(jnp.int32, shape, axis)


def turn(value, steps, axis):
    size = value.shape[axis]
    steps = steps % size
    return value if steps == 0 else pltpu.roll(value, steps, axis)


def low_half(shape):
    return ids(shape, 0) < ITERS


def left_lanes(shape):
    return ids(shape, 1) % EDGE < ITERS


def first_pair(a, b):
    return jnp.where(low_half(a.shape), a, turn(b, ITERS, 0))


def last_pair(a, b):
    return jnp.where(low_half(a.shape), turn(a, ITERS, 0), b)


def slots(below, above):
    low = low_half(below.shape)
    return (
        jnp.where(low, below, turn(above, ITERS, 0)),
        jnp.where(low, turn(below, ITERS, 0), above),
    )


def store_pair(outs, index, a, b, is_first_row):
    if len(outs) == 1:
        outs[0][index] = jnp.where(is_first_row, last_pair(a, b), first_pair(a, b))
    else:
        outs[0][index] = first_pair(a, b)
        outs[1][index] = last_pair(a, b)


def add_edge(acc, value, place):
    lanes = ids(value.shape, 1) // EDGE
    moved = turn(value, EDGE * place + ITERS, 1)
    return moved if acc is None else jnp.where(lanes == place, moved, acc)


def prev_row(part, other):
    return jnp.where(ids(part.shape, 0) == 0, turn(other, 1, 0), turn(part, 1, 0))


def next_row(part, other):
    last = part.shape[0] - 1
    return jnp.where(ids(part.shape, 0) == last, turn(other, -1, 0), turn(part, -1, 0))


def prev_col(part, rim):
    return jnp.where(ids(part.shape, 1) == 0, rim, turn(part, 1, 1))


def next_col(part, rim):
    last = part.shape[1] - 1
    return jnp.where(ids(part.shape, 1) == last, rim, turn(part, -1, 1))


def strips(edges, rims):
    left = left_lanes(edges.shape)
    return (jnp.where(left, rims, edges), jnp.where(left, edges, rims))


def crossing(left_strip, right_strip):
    lanes = ids(left_strip.shape, 1) % EDGE
    return jnp.where(lanes == ITERS - 1, turn(right_strip, -1, 1), turn(left_strip, 1, 1))


def rim_of(cross, place):
    return turn(cross, -(EDGE * place + ITERS), 1)


def pack_kernel(chunks, meta, runs, omega, conductance, wet, static_out, edge_out, *row_outs):
    directions = len(row_outs) // chunks
    levels, rows, cols = omega.shape[1:]
    shape = (rows, cols)
    is_first_row = meta[0] == 0
    row_ids, col_ids = (ids(shape, 0), ids(shape, 1))
    wet_cells = wet[...].astype(jnp.float32)
    open_x = (col_ids >= runs[0, 0]) & (col_ids < runs[0, 0] + runs[0, 1])
    open_y = (row_ids >= runs[0, 2]) & (row_ids < runs[0, 2] + runs[0, 3])
    keep_x = (row_ids > 0) | open_x
    keep_y = (col_ids > 0) | open_y
    statics = []
    for level in range(levels):
        statics.append(
            [
                jnp.where(keep_x, conductance[0, level], 0.0),
                jnp.where(keep_y, conductance[1, level], 0.0),
                conductance[2, level] if level else jnp.zeros(shape, jnp.float32),
                wet_cells,
            ]
        )
    kinds = len(statics[0])
    group = cols // EDGE
    for level in range(levels):
        edge = None
        for kind in range(kinds):
            static_out[kind, level] = statics[level][kind]
            edge = add_edge(edge, statics[level][kind], kind)
        edge_out[chunks, level] = edge
        for kind in range(0, kinds, 2):
            outs = row_outs[:directions]
            store_pair(outs, (group // 2 + kind // 2, level), statics[level][kind], statics[level][kind + 1], is_first_row)
        for chunk in range(chunks):
            outs = row_outs[directions * chunk : directions * (chunk + 1)]
            edge = None
            for pair in range(group // 2):
                start = [omega[chunk * group + 2 * pair + i, level] * wet_cells for i in range(2)]
                edge = add_edge(edge, start[0], 2 * pair)
                edge = add_edge(edge, start[1], 2 * pair + 1)
                store_pair(outs, (pair, level), start[0], start[1], is_first_row)
            edge_out[chunk, level] = edge


def corner_kernel(meta, left, right, *outs):
    is_first_row = meta[0] == 0
    groups, levels, rows, cols = left.shape
    take = left_lanes((rows, cols))
    for g in range(groups):
        for level in range(0, levels, 2):
            pair = [jnp.where(take, left[g, level + i], right[g, level + i]) for i in range(2)]
            store_pair(outs, (g, level // 2), pair[0], pair[1], is_first_row)


def rims_of_group(left, right, corner_below, corner_above):
    levels, rows, cols = left.shape[1:]
    take = left_lanes((rows, cols))
    rims = [[jnp.where(take, left[0, level], right[0, level]), None] for level in range(levels)]
    for level in range(0, levels, 2):
        pair = slots(corner_below[0, level // 2], corner_above[0, level // 2])
        rims[level][SLOT], rims[level + 1][SLOT] = pair
    return rims


def weight_kernel(meta, statics, below, above, edges, left, right, corner_below, corner_above, main_out, strip_out):
    kinds, levels, rows, cols = statics.shape
    shape = (rows, cols)
    low = low_half(shape)
    valid = (low & (meta[1] > 0)) | (jnp.logical_not(low) & (meta[0] > 0))
    first = below.shape[0] - kinds // 2
    rims = rims_of_group(left, right, corner_below, corner_above)
    field = [[[statics[kind, level], None] for level in range(levels)] for kind in range(kinds)]
    for level in range(levels):
        for kind in range(0, kinds, 2):
            pair = slots(below[first + kind // 2, level], above[first + kind // 2, level])
            for i in range(2):
                field[kind + i][level][SLOT] = jnp.where(valid, pair[i], 0.0)
    width = cols // EDGE
    lanes = ids(shape, 1) // EDGE

    def spread(strip, kind):
        value = jnp.where(lanes == 0, turn(strip, -EDGE * kind, 1), 0.0)
        span = 1
        while span < width:
            value = value + turn(value, EDGE * span, 1)
            span *= 2
        return value

    side = [[[[None, None] for _ in range(levels)] for _ in range(kinds)] for _ in range(2)]
    cross = [[None, None] for _ in range(levels)]
    for level in range(levels):
        for part in range(2):
            edge = edges[0, level] if part == MAIN else None
            if part == SLOT:
                for kind in range(kinds):
                    edge = add_edge(edge, field[kind][level][SLOT], kind)
            rim = rims[level][part]
            if part == SLOT:
                rim = jnp.where(valid, rim, 0.0)
            pair = strips(edge, rim)
            cross[level][part] = crossing(pair[0], pair[1])
            for s in range(2):
                for kind in range(kinds):
                    side[s][kind][level][part] = spread(pair[s], kind)

    def emit(out, values, after_of):
        for level in range(levels):
            for part in range(2):
                cond_x, cond_y, cond_z, wet = (values[kind][level][part] for kind in range(kinds))
                faces = [
                    cond_x,
                    next_row(cond_x, values[0][level][1 - part]),
                    cond_y,
                    after_of(cond_y, level, part),
                    cond_z,
                    values[2][level + 1][part] if level + 1 < levels else jnp.zeros(shape, jnp.float32),
                ]
                total = faces[0]
                for face in faces[1:]:
                    total = total + face
                out[0, level, part] = wet * (1.0 - total)
                for index, face in enumerate(faces):
                    out[index + 1, level, part] = wet * face

    emit(main_out, field, lambda cond, level, part: next_col(cond, rim_of(cross[level][part], 1)))
    for s in range(2):
        emit(strip_out.at[s], side[s], lambda cond, level, part: turn(cond, -1, 1))


def one_pass(state, weight, parts, rim_at):
    levels = len(state)
    result = [[None, None] for _ in range(levels)]
    for level in range(levels):
        for part in parts:
            value, other = (state[level][part], state[level][1 - part])
            rim = rim_at(level, part)
            before = turn(value, 1, 1) if rim is None else prev_col(value, rim)
            after = turn(value, -1, 1) if rim is None else next_col(value, rim)
            total = weight(0, level, part) * value
            total = total + weight(1, level, part) * prev_row(value, other)
            total = total + weight(2, level, part) * next_row(value, other)
            total = total + weight(3, level, part) * before
            total = total + weight(4, level, part) * after
            if level > 0:
                total = total + weight(5, level, part) * state[level - 1][part]
            if level < levels - 1:
                total = total + weight(6, level, part) * state[level + 1][part]
            result[level][part] = total
    return result


def diffuse_kernel(
    batch, meta, omega, wet, volume, below, above, edges, left, right, corner_below, corner_above,
    main_weights, strip_weights, *rest
):
    field_out, keep_out, send_out, cross_scratch, slot_scratch = rest[-5:]
    group, levels, rows, cols = omega.shape
    shape = (rows, cols)
    wet_cells = wet[...].astype(jnp.float32)
    root = jnp.sqrt(volume[...])
    half = levels // 2
    keeps_low = meta[2] == 0
    rims = rims_of_group(left, right, corner_below, corner_above)
    slot_edges = [None] * levels
    for level in range(levels):
        for pair in range(group // 2):
            two = slots(below[pair, level], above[pair, level])
            for i in range(2):
                slot_scratch[2 * pair + i, level] = two[i]
                slot_edges[level] = add_edge(slot_edges[level], two[i], 2 * pair + i)
    state = [[[None, None] for _ in range(levels)] for _ in range(2)]
    for level in range(levels):
        for part in range(2):
            edge = edges[0, level] if part == MAIN else slot_edges[level]
            pair = strips(edge, rims[level][part])
            for s in range(2):
                state[s][level][part] = pair[s]
    for sweep in range(ITERS):
        for level in range(levels):
            for part in range(2):
                cross_scratch[sweep, level, part] = crossing(state[0][level][part], state[1][level][part])
        if sweep < ITERS - 1:
            for s in range(2):
                state[s] = one_pass(
                    state[s], lambda n, level, part: strip_weights[s, n, level, part], (MAIN, SLOT), lambda level, part: None
                )

    for first in range(0, group, batch):
        fields = []
        for place in range(first, first + batch):
            fields.append([[omega[place, level] * wet_cells, slot_scratch[place, level]] for level in range(levels)])
        for sweep in range(ITERS):
            parts = (MAIN, SLOT) if sweep < ITERS - 1 else (MAIN,)
            for i in range(batch):
                fields[i] = one_pass(
                    fields[i],
                    lambda n, level, part: main_weights[n, level, part],
                    parts,
                    lambda level, part: rim_of(cross_scratch[sweep, level, part], first + i),
                )
        for i in range(batch):
            scaled = []
            for level in range(levels):
                value = fields[i][level][MAIN]
                field_out[first + i, level] = value
                scaled.append(value * root)
            for level in range(half):
                at = ((first + i) * half + level) * rows
                keep_out[at : at + rows, :] = jnp.where(keeps_low, scaled[level], scaled[half + level])
                send_out[at : at + rows, :] = jnp.where(keeps_low, scaled[half + level], scaled[level])


def gram_of_rows(slices, refs):
    groups = [ref.shape[0] // slices for ref in refs]
    order = sum(groups)
    exact = jnp.zeros((order, order), jnp.float32)
    cross = jnp.zeros((order, order), jnp.float32)
    for at in range(0, slices, 2):
        columns = []
        for i in range(2):
            picked = [ref[pl.ds(at + i, group, slices), :] for ref, group in zip(refs, groups)]
            columns.append(jnp.concatenate(picked, axis=0))
        values = jnp.concatenate(columns, axis=1)
        high = values.astype(jnp.bfloat16)
        rest = (values - high.astype(jnp.float32)).astype(jnp.bfloat16)
        dims = (((1,), (1,)), ((), ()))
        exact = exact + lax.dot_general(high, high, dims, preferred_element_type=jnp.float32)
        cross = cross + lax.dot_general(high, rest, dims, preferred_element_type=jnp.float32)
    return exact + (cross + cross.T)


def store_halves(meta, gram, mine, theirs):
    order = gram.shape[0]
    moved = turn(turn(gram, order // 2, 0), order // 2, 1)
    first, second = halves_of_gram(jnp.where(meta[2] == 0, gram, moved))
    is_first = meta[3] == 0
    mine[...] = jnp.where(is_first, first, second)
    theirs[...] = jnp.where(is_first, second, first)


def gram_kernel(chunks, slices, meta, *refs):
    store_halves(meta, gram_of_rows(slices, refs[:-2]), *refs[-2:])


def far_gram_kernel(slices, kept, received, out):
    out[...] = gram_of_rows(slices, (kept, received))


def near_gram_kernel(slices, meta, far, *refs):
    store_halves(meta, far[...] + gram_of_rows(slices, refs[:-2]), *refs[-2:])


def swapped(value, axis, bit):
    count = lax.axis_size(axis)
    return lax.ppermute(value, axis, [(source, source ^ bit) for source in range(count)])


def mesh_permute(value, mask):
    axes = ("tiles", "vec")
    count = lax.axis_size("tiles") * lax.axis_size("vec")
    return lax.ppermute(value, axes, [(source, source ^ mask) for source in range(count)])


def total_over_chips(value):
    vec = lax.axis_size("vec")
    masks = []
    bit = 1
    while bit < vec:
        masks.append(bit)
        bit *= 2
    bit = 2
    while bit < lax.axis_size("tiles"):
        masks.append(bit * vec)
        bit *= 2
    while masks:
        near, masks = (masks[:2], masks[2:])
        if len(near) == 1:
            value = value + mesh_permute(value, near[0])
        else:
            one, two, both = (mesh_permute(value, mask) for mask in (near[0], near[1], near[0] ^ near[1]))
            value = (value + one) + (two + both)
    return value


def fold(a, b):
    half = a.shape[1] // 2
    return jnp.where(ids(a.shape, 1) < half, a, b)


def flip(value):
    return turn(value, value.shape[1] // 2, 1)


def halves_of_gram(gram):
    q = gram.shape[0] // 8
    first = [fold(gram[: 2 * q], flip(gram[2 * q : 4 * q])), fold(flip(gram[:q]), gram[q : 2 * q])]
    second = [fold(flip(gram[4 * q : 6 * q]), gram[6 * q :]), fold(flip(gram[2 * q : 3 * q]), gram[3 * q : 4 * q])]
    return (jnp.concatenate(first, axis=0), jnp.concatenate(second, axis=0))


def gram_of_halves(first, second):
    q = first.shape[0] // 3
    return jnp.concatenate(
        [
            fold(first[:q], flip(first[2 * q :])),
            fold(first[q : 2 * q], first[2 * q :]),
            fold(flip(first[:q]), flip(second[2 * q :])),
            fold(flip(first[q : 2 * q]), second[2 * q :]),
            flip(second[: 2 * q]),
            second[: 2 * q],
        ],
        axis=0,
    )


def spread_lane(value, lane):
    return jnp.broadcast_to(value[:, lane : lane + 1], value.shape)


def squares(rows):
    high = rows.astype(jnp.bfloat16).astype(jnp.float32)
    rest = rows - high
    middle = rest.astype(jnp.bfloat16).astype(jnp.float32)
    low = rest - middle
    one = jnp.concatenate([high, high, middle, high, low, middle], axis=0).astype(jnp.bfloat16)
    two = jnp.concatenate([high, middle, high, low, high, middle], axis=0).astype(jnp.bfloat16)
    return lax.dot_general(one, two, (((0,), (0,)), ((), ())), preferred_element_type=jnp.float32)


def factor_kernel(scale, meta, own, other, out_ref):
    order = out_ref.shape[0]
    height = 8
    count = order // height
    shape = (height, order)
    is_first = meta[3] == 0
    mine, theirs = (own[...], other[...])
    gram = gram_of_halves(jnp.where(is_first, mine, theirs), jnp.where(is_first, theirs, mine)) * scale
    blocks = [gram[height * b : height * (b + 1), :] for b in range(count)]
    row_ids, col_ids = (ids(shape, 0), ids(shape, 1))
    previous = None
    for p in range(count):
        base = height * p
        rows = [jnp.broadcast_to(blocks[p][j : j + 1, :], shape) for j in range(height)]
        corner = {(i, j): spread_lane(rows[j], base + i) for j in range(height) for i in range(j, height)}
        if previous is not None:
            for done in previous:
                lanes = [spread_lane(done, base + j) for j in range(height)]
                for j in range(height):
                    rows[j] = rows[j] - lanes[j] * done
                    for i in range(j, height):
                        corner[i, j] = corner[i, j] - lanes[i] * lanes[j]
        panel = jnp.zeros(shape, jnp.float32)
        for s in range(height):
            inverse = lax.rsqrt(corner[s, s])
            rows[s] = rows[s] * inverse
            lanes = {j: corner[j, s] * inverse for j in range(s + 1, height)}
            for j in range(s + 1, height):
                for i in range(j, height):
                    corner[i, j] = corner[i, j] - lanes[i] * lanes[j]
                rows[j] = rows[j] - lanes[j] * rows[s]
            panel = jnp.where(row_ids == s, rows[s], panel)
        panel = jnp.where(col_ids >= base + row_ids, panel, 0.0)
        out_ref[base : base + height, :] = panel
        if p + 2 < count:
            update = squares(panel)
            for q in range(p + 2, count):
                blocks[q] = blocks[q] - update[height * q : height * (q + 1), :]
        previous = rows


def edge_kernel(runs, omega, conductance, wet, static_out, edge_out):
    levels, rows, cols = omega.shape[1:]
    shape = (rows, cols)
    row_ids, col_ids = (ids(shape, 0), ids(shape, 1))
    wet_cells = wet[...].astype(jnp.float32)
    open_x = (col_ids >= runs[0, 0]) & (col_ids < runs[0, 0] + runs[0, 1])
    open_y = (row_ids >= runs[0, 2]) & (row_ids < runs[0, 2] + runs[0, 3])
    keep_x = (row_ids > 0) | open_x
    keep_y = (col_ids > 0) | open_y
    group = cols // EDGE
    chunks = omega.shape[0] // group
    for level in range(levels):
        statics = [
            jnp.where(keep_x, conductance[0, level], 0.0),
            jnp.where(keep_y, conductance[1, level], 0.0),
            conductance[2, level] if level else jnp.zeros(shape, jnp.float32),
            wet_cells,
        ]
        edge = None
        for kind, value in enumerate(statics):
            static_out[kind, level] = value
            edge = add_edge(edge, value, kind)
        edge_out[chunks, level] = edge
        for chunk in range(chunks):
            edge = None
            for place in range(group):
                edge = add_edge(edge, omega[chunk * group + place, level] * wet_cells, place)
            edge_out[chunk, level] = edge


def face_kernel(first, meta, omega, wet, *row_outs):
    levels, rows, cols = omega.shape[1:]
    group = cols // EDGE
    is_first_row = meta[0] == 0
    wet_cells = wet[...].astype(jnp.float32)
    for chunk, out in enumerate(row_outs):
        for level in range(levels):
            for pair in range(group // 2):
                at = (first + chunk) * group + 2 * pair
                start = [omega[at + i, level] * wet_cells for i in range(2)]
                store_pair((out,), (pair, level), start[0], start[1], is_first_row)


def rim_kernel(meta, statics, left, right, out):
    is_first_row = meta[0] == 0
    groups, levels, rows, cols = left.shape
    kinds = statics.shape[0]
    take = left_lanes((rows, cols))
    for g in range(groups):
        for level in range(0, levels, 2):
            pair = [jnp.where(take, left[g, level + i], right[g, level + i]) for i in range(2)]
            store_pair((out,), g * levels // 2 + level // 2, pair[0], pair[1], is_first_row)
    first = groups * levels // 2
    for kind in range(0, kinds, 2):
        for level in range(levels):
            at = first + kind // 2 * levels + level
            store_pair((out,), at, statics[kind, level], statics[kind + 1, level], is_first_row)


def near_rows(is_first_row, a, b, halo):
    low = low_half(halo.shape)
    turned = turn(halo, ITERS, 0)
    result = []
    for own, across, moved in ((a, halo, turned), (b, turned, halo)):
        near = turn(own, ITERS, 0)
        result.append(jnp.where(low, jnp.where(is_first_row, near, across), jnp.where(is_first_row, moved, near)))
    return result


def spread_kind(strip, kind):
    cols = strip.shape[1]
    value = jnp.where(ids(strip.shape, 1) // EDGE == 0, turn(strip, -EDGE * kind, 1), 0.0)
    span = EDGE
    while span < cols:
        value = value + turn(value, span, 1)
        span *= 2
    return value


def store_weights(out, values, after_row, after_col):
    levels = len(values[0])
    for level in range(levels):
        cond_x, cond_y, cond_z, wet = (kind[level] for kind in values)
        below = values[2][level + 1] if level + 1 < levels else jnp.zeros_like(cond_z)
        faces = [cond_x, after_row(level), cond_y, after_col(level), cond_z, below]
        total = faces[0]
        for face in faces[1:]:
            total = total + face
        out[0, level] = wet * (1.0 - total)
        for index, face in enumerate(faces):
            out[index + 1, level] = wet * face


def plane_pass(state, weight, row_before, row_after, rim_at):
    levels = len(state)
    result = []
    for level in range(levels):
        value = state[level]
        rim = rim_at(level)
        before = turn(value, 1, 1) if rim is None else prev_col(value, rim)
        after = turn(value, -1, 1) if rim is None else next_col(value, rim)
        total = weight(0, level) * value
        total = total + weight(1, level) * row_before(value, level)
        total = total + weight(2, level) * row_after(value, level)
        total = total + weight(3, level) * before
        total = total + weight(4, level) * after
        if level > 0:
            total = total + weight(5, level) * state[level - 1]
        if level < levels - 1:
            total = total + weight(6, level) * state[level + 1]
        result.append(total)
    return result


def no_rim(level):
    return None


def pack_levels(values, use_first):
    pairs = []
    for level in range(0, len(values), 2):
        a, b = values[level : level + 2]
        pairs.append(jnp.where(use_first, first_pair(a, b), last_pair(a, b)))
    return pairs


def store_half(keep, send, place, pairs, keeps_low):
    rows = pairs[0].shape[0]
    half = len(pairs) // 2
    for i in range(half):
        at = (place * half + i) * rows
        keep[at : at + rows, :] = jnp.where(keeps_low, pairs[i], pairs[half + i])
        send[at : at + rows, :] = jnp.where(keeps_low, pairs[half + i], pairs[i])


def far_kernel(
    batch, meta, statics, omega, wet, volume, edges, left, right,
    final_out, bound_out, strip_bound_out, keep_out, send_out, weights, strip_weights, cross_scratch
):
    vectors, levels, rows, cols = omega.shape
    kinds = statics.shape[0]
    shape = (rows, cols)
    group = cols // EDGE
    chunks = vectors // group
    is_first_row = meta[0] == 0
    keeps_low = meta[2] == 0
    row_ids = ids(shape, 0)
    take = left_lanes(shape)
    wet_cells = wet[...].astype(jnp.float32)
    root = jnp.sqrt(volume[...])

    def sides(g, level):
        return strips(edges[g, level], jnp.where(take, left[g, level], right[g, level]))

    def roll_before(value, level):
        return turn(value, 1, 0)

    def roll_after(value, level):
        return turn(value, -1, 0)

    def closed_after(value):
        return jnp.where(row_ids == rows - 1, 0.0, turn(value, -1, 0))

    field = [[statics[kind, level] for level in range(levels)] for kind in range(kinds)]
    pairs = [sides(chunks, level) for level in range(levels)]
    crosses = [crossing(*pair) for pair in pairs]
    store_weights(
        weights, field, lambda level: closed_after(field[0][level]),
        lambda level: next_col(field[1][level], rim_of(crosses[level], 1)),
    )
    for s in range(2):
        side = [[spread_kind(pairs[level][s], kind) for level in range(levels)] for kind in range(kinds)]
        store_weights(
            strip_weights.at[s], side, lambda level: closed_after(side[0][level]), lambda level: turn(side[1][level], -1, 1)
        )

    def keep_bound(acc, value, sweep):
        edge = jnp.where(is_first_row, value, turn(value, -1, 0))
        moved = turn(edge, sweep - (ITERS - 1), 0)
        return moved if acc is None else jnp.where(row_ids == sweep, moved, acc)

    for g in range(chunks):
        state = [[sides(g, level)[s] for level in range(levels)] for s in range(2)]
        bounds = [[None] * levels for _ in range(2)]
        for sweep in range(ITERS):
            for level in range(levels):
                cross_scratch[g, sweep, level] = crossing(state[0][level], state[1][level])
                for s in range(2):
                    bounds[s][level] = keep_bound(bounds[s][level], state[s][level], sweep)
            if sweep < ITERS - 1:
                for s in range(2):
                    state[s] = plane_pass(
                        state[s], lambda n, level: strip_weights[s, n, level], roll_before, roll_after, no_rim
                    )
        for s in range(2):
            for level in range(levels):
                strip_bound_out[g, s, level] = bounds[s][level]

    for first in range(0, vectors, batch):
        g = first // group
        fields = [[omega[place, level] * wet_cells for level in range(levels)] for place in range(first, first + batch)]
        bounds = [[None] * levels for _ in range(batch)]
        for sweep in range(ITERS):
            for i in range(batch):
                for level in range(levels):
                    bounds[i][level] = keep_bound(bounds[i][level], fields[i][level], sweep)
                fields[i] = plane_pass(
                    fields[i], lambda n, level: weights[n, level], roll_before, roll_after,
                    lambda level: rim_of(cross_scratch[g, sweep, level], (first + i) % group),
                )
        for i in range(batch):
            for level in range(levels):
                final_out[first + i, level] = fields[i][level]
                bound_out[first + i, level] = bounds[i][level]
            scaled = [value * root for value in fields[i]]
            store_half(keep_out, send_out, first + i, pack_levels(scaled, is_first_row), keeps_low)


def near_weight_kernel(meta, statics, rims, edges, left, right, weights, strip_weights):
    kinds, levels, rows, cols = statics.shape
    shape = (rows, cols)
    is_first_row = meta[0] == 0
    take = left_lanes(shape)
    last = ids(shape, 0) == rows - 1
    g = edges.shape[0] - 1
    groups = edges.shape[0]
    first = groups * levels // 2
    field = [[None] * levels for _ in range(kinds)]
    for kind in range(0, kinds, 2):
        for level in range(levels):
            own = (statics[kind, level], statics[kind + 1, level])
            pair = near_rows(is_first_row, *own, rims[first + kind // 2 * levels + level])
            field[kind][level], field[kind + 1][level] = pair
    rim = [jnp.where(take, left[g, level], right[g, level]) for level in range(levels)]
    near_rim = []
    for level in range(0, levels, 2):
        near_rim += near_rows(is_first_row, rim[level], rim[level + 1], rims[g * levels // 2 + level // 2])
    near_edge = []
    for level in range(levels):
        edge = None
        for kind in range(kinds):
            edge = add_edge(edge, field[kind][level], kind)
        near_edge.append(edge)
    pairs = [strips(near_edge[level], near_rim[level]) for level in range(levels)]
    tile_pairs = [strips(edges[g, level], rim[level]) for level in range(levels)]
    crosses = [crossing(*pair) for pair in pairs]

    def with_next(value, tile_value):
        beyond = jnp.broadcast_to(tile_value[ITERS : ITERS + 1, :], shape)
        return jnp.where(last, beyond, turn(value, -1, 0))

    store_weights(
        weights, field, lambda level: with_next(field[0][level], statics[0, level]),
        lambda level: next_col(field[1][level], rim_of(crosses[level], 1)),
    )
    for s in range(2):
        side = [[spread_kind(pairs[level][s], kind) for level in range(levels)] for kind in range(kinds)]
        tile_side = [spread_kind(tile_pairs[level][s], 0) for level in range(levels)]
        store_weights(
            strip_weights.at[s], side, lambda level: with_next(side[0][level], tile_side[level]),
            lambda level: turn(side[1][level], -1, 1),
        )


def near_kernel(
    batch, base, parts, meta, omega, wet, volume, rims, left, right, weights, strip_weights, bound, strip_bound, final, *rest
):
    halos = rest[:parts]
    field_out, keep_out, send_out, cross_scratch, start, done, sems = rest[-7:]
    levels, rows, cols = omega.shape[1:]
    group = cols // EDGE
    offset = base * group
    shape = (rows, cols)
    is_first_row = meta[0] == 0
    keeps_low = meta[2] == 0
    row_ids = ids(shape, 0)
    take = left_lanes(shape)
    top = (row_ids == 0) & is_first_row
    bottom = (row_ids == rows - 1) & jnp.logical_not(is_first_row)
    is_near = low_half(shape) != is_first_row
    wet_cells = wet[...].astype(jnp.float32)
    root = jnp.sqrt(volume[...])

    def around(bound_at, sweep):
        def kept(level):
            return jnp.broadcast_to(bound_at(level)[sweep : sweep + 1, :], shape)

        return (
            lambda value, level: jnp.where(top, kept(level), turn(value, 1, 0)),
            lambda value, level: jnp.where(bottom, kept(level), turn(value, -1, 0)),
        )

    for part in range(parts):
        near_edge = [None] * levels
        for level in range(levels):
            for pair in range(group // 2):
                at = part * group + 2 * pair
                own = [omega[offset + at + i, level] * wet_cells for i in range(2)]
                two = near_rows(is_first_row, *own, halos[part][pair, level])
                for i in range(2):
                    start[at + i, level] = two[i]
                    near_edge[level] = add_edge(near_edge[level], two[i], 2 * pair + i)
        rim = [jnp.where(take, left[base + part, level], right[base + part, level]) for level in range(levels)]
        near_rim = []
        for level in range(0, levels, 2):
            across = rims[(base + part) * levels // 2 + level // 2]
            near_rim += near_rows(is_first_row, rim[level], rim[level + 1], across)
        pairs = [strips(near_edge[level], near_rim[level]) for level in range(levels)]
        state = [[pairs[level][s] for level in range(levels)] for s in range(2)]
        for sweep in range(ITERS):
            for level in range(levels):
                cross_scratch[part, sweep, level] = crossing(state[0][level], state[1][level])
            if sweep < ITERS - 1:
                for s in range(2):
                    state[s] = plane_pass(
                        state[s], lambda n, level: strip_weights[s, n, level],
                        *around(lambda level: strip_bound[base + part, s, level], sweep), no_rim,
                    )

    copies = []
    for first in range(0, parts * group, batch):
        part = first // group
        fields = [[start[place, level] for level in range(levels)] for place in range(first, first + batch)]
        for sweep in range(ITERS):
            for i in range(batch):
                fields[i] = plane_pass(
                    fields[i], lambda n, level: weights[n, level],
                    *around(lambda level: bound[offset + first + i, level], sweep),
                    lambda level: rim_of(cross_scratch[part, sweep, level], (first + i) % group),
                )
        for i in range(batch):
            scaled = []
            for level in range(levels):
                value = jnp.where(is_near, turn(fields[i][level], ITERS, 0), final[offset + first + i, level])
                done[first + i, level] = value
                scaled.append(value * root)
            store_half(keep_out, send_out, first + i, pack_levels(scaled, jnp.logical_not(is_first_row)), keeps_low)
        copies.append(
            pltpu.make_async_copy(
                done.at[pl.ds(first, batch)], field_out.at[pl.ds(offset + first, batch)], sems.at[first // batch]
            )
        )
        copies[-1].start()
    for copy in copies:
        copy.wait()


def shifted(value, axis, steps):
    count = lax.axis_size(axis)
    first, last = (max(0, -steps), min(count, count - steps))
    return lax.ppermute(value, axis, [(source, source + steps) for source in range(first, last)])


def beside(value, steps):
    count = lax.axis_size("tiles")
    pairs = [(source, source + steps) for source in range(count)]
    return lax.ppermute(value, "tiles", [(a, b) for a, b in pairs if 0 <= b < count and a // TGY == b // TGY])


def after(values, *done):
    return lax.optimization_barrier((values, done))[0]


def exchange_rows(messages, grid_rows):
    if len(messages) == 1:
        received = swapped(messages[0], "tiles", TGY)
        return (received, received)
    return (shifted(messages[0], "tiles", -TGY), shifted(messages[1], "tiles", TGY))


def f32(*shape):
    return jax.ShapeDtypeStruct(shape, jnp.float32)


def block(shape, *at):
    return pl.BlockSpec(shape, lambda i: at)


def call(kernel, in_specs, out_specs, out_shape, flops=0, scratch=(), aliases=None, limit=VMEM_LIMIT, grid=(1,)):
    return pl.pallas_call(
        kernel,
        grid=grid,
        in_specs=in_specs,
        out_specs=out_specs,
        out_shape=out_shape,
        scratch_shapes=scratch,
        input_output_aliases=aliases or {},
        compiler_params=pltpu.CompilerParams(vmem_limit_bytes=limit),
        cost_estimate=pl.CostEstimate(flops=flops, bytes_accessed=1 << 20, transcendentals=0),
    )


def resident(count):
    return [pl.BlockSpec(memory_space=pltpu.VMEM)] * count


def whole(array):
    zeros = (0,) * array.ndim
    return pl.BlockSpec(array.shape, lambda i: zeros)


def factor(meta, mine, theirs, order, scale):
    mine = total_over_chips(mine + swapped(theirs, "tiles", 1))
    smem = pl.BlockSpec(memory_space=pltpu.SMEM)
    return call(
        functools.partial(factor_kernel, scale),
        [smem] + resident(2),
        resident(1)[0],
        f32(order, order),
        grid=(),
    )(meta, mine, swapped(mine, "tiles", 1))


def shards_any(omega, conductance, wet, volume, face_runs):
    vectors, levels, rows, cols = omega.shape
    tiles = lax.axis_size("tiles")
    grid_rows = tiles // TGY
    tile_row = lax.axis_index("tiles") // TGY
    core = lax.axis_index("tiles") % 2
    meta = jnp.stack([tile_row, grid_rows - 1 - tile_row, lax.axis_index("vec"), core]).astype(jnp.int32)
    smem = pl.BlockSpec(memory_space=pltpu.SMEM)
    group = cols // EDGE
    chunks = vectors // group
    directions = 1 if grid_rows == 2 else 2
    kinds = 4
    half = levels // 2

    row_shapes = [f32(group // 2 + (kinds // 2 if c == 0 else 0), levels, rows, cols) for c in range(chunks)]
    row_shapes = [shape for shape in row_shapes for _ in range(directions)]
    packed_shapes = [f32(kinds, levels, rows, cols), f32(chunks + 1, levels, rows, cols)] + row_shapes
    statics, edges, *messages = call(
        functools.partial(pack_kernel, chunks),
        [smem, smem, whole(omega), whole(conductance), whole(wet)],
        [whole(s) for s in packed_shapes],
        packed_shapes,
    )(meta, face_runs, omega, conductance, wet)
    messages = [messages[directions * c : directions * (c + 1)] for c in range(chunks)]
    received = [exchange_rows(messages[0], grid_rows)]
    left = beside(edges, 1)
    right = beside(edges, -1)
    corner_shapes = [f32(chunks + 1, levels // 2, rows, cols)] * directions
    corners = call(
        corner_kernel, [smem, whole(left), whole(right)], [whole(s) for s in corner_shapes], corner_shapes
    )(meta, left, right)
    corners = exchange_rows(corners, grid_rows)
    gates = [(left, right), corners]
    for c in range(1, chunks):
        gate = gates[c - 1] if c <= 2 else received[c - 2]
        received.append(exchange_rows(after(messages[c], *gate), grid_rows))

    def group_specs(c):
        edge = block((1, levels, rows, cols), c, 0, 0, 0)
        corner = block((1, levels // 2, rows, cols), c, 0, 0, 0)
        return [edge, edge, edge, corner, corner]

    around = (edges, left, right, *corners)
    weight_shapes = [f32(7, levels, 2, rows, cols), f32(2, 7, levels, 2, rows, cols)]
    main_weights, strip_weights = call(
        weight_kernel,
        [smem, whole(statics), whole(received[0][0]), whole(received[0][1])] + group_specs(chunks),
        [whole(s) for s in weight_shapes],
        weight_shapes,
    )(meta, statics, *received[0], *around)

    field = None
    kept, sent = ([], [])
    half_shape = f32(group * half * rows, cols)
    for c in range(chunks):
        rims = after(received[c], sent[c - 2]) if c >= 2 else received[c]
        operands = [meta, omega, wet, volume, *rims, *around, main_weights, strip_weights]
        row_block = block((group // 2, levels, rows, cols), 0, 0, 0, 0)
        chunk_block = block((group, levels, rows, cols), c, 0, 0, 0)
        specs = [smem, chunk_block, whole(wet), whole(volume), row_block, row_block] + group_specs(c)
        specs += [whole(main_weights), whole(strip_weights)]
        aliases = {}
        if field is not None:
            aliases = {len(operands): 0}
            operands.append(field)
            specs.append(pl.BlockSpec(memory_space=pl.ANY))
        field, keep, send = call(
            functools.partial(diffuse_kernel, 4),
            specs,
            [chunk_block, whole(half_shape), whole(half_shape)],
            [f32(*omega.shape), half_shape, half_shape],
            flops=4 * 10**9,
            scratch=[pltpu.VMEM((ITERS, levels, 2, rows, cols), jnp.float32), pltpu.VMEM((group, levels, rows, cols), jnp.float32)],
            aliases=aliases,
        )(*operands)
        kept.append(keep)
        sent.append(swapped(send, "vec", 1))

    order = 2 * vectors
    half_gram = f32(3 * order // 8, order)
    mine, theirs = call(
        functools.partial(gram_kernel, chunks, half * rows),
        [smem] + [whole(half_shape)] * (2 * chunks),
        [whole(half_gram)] * 2,
        [half_gram] * 2,
    )(meta, *kept, *sent)
    r_factor = factor(meta, mine, theirs, order, 1.0 / (levels * tiles * rows * cols))
    return (field, r_factor)


def shards_of_two_rows(omega, conductance, wet, volume, face_runs):
    vectors, levels, rows, cols = omega.shape
    tiles = lax.axis_size("tiles")
    tile_row = lax.axis_index("tiles") // TGY
    core = lax.axis_index("tiles") % 2
    meta = jnp.stack([tile_row, 1 - tile_row, lax.axis_index("vec"), core]).astype(jnp.int32)
    smem = pl.BlockSpec(memory_space=pltpu.SMEM)
    group = cols // EDGE
    chunks = vectors // group
    kinds = 4
    half = levels // 4
    plane = (rows, cols)

    def vmem(*lead):
        return pltpu.VMEM(lead + plane, jnp.float32)

    row_shape = f32(group // 2, levels, *plane)
    chunk0 = call(
        functools.partial(face_kernel, 0),
        [smem, block((group, levels, *plane), 0, 0, 0, 0), whole(wet)],
        [whole(row_shape)],
        [row_shape],
        limit=EDGE_LIMIT,
    )(meta, omega, wet)
    edge_shapes = [f32(kinds, levels, *plane), f32(chunks + 1, levels, *plane)]
    statics, edges = call(
        edge_kernel,
        [smem, whole(omega), whole(conductance), whole(wet)],
        [whole(s) for s in edge_shapes],
        edge_shapes,
        limit=EDGE_LIMIT,
    )(after(face_runs, chunk0), omega, conductance, wet)
    left = beside(edges, 1)
    right = beside(edges, -1)
    row_shapes = [row_shape] * (chunks - 1)
    messages = chunk0 + call(
        functools.partial(face_kernel, 1),
        [smem] + resident(2),
        resident(len(row_shapes)),
        row_shapes,
        flops=10**9,
        grid=(),
    )(meta, omega, wet)
    halos = [swapped(messages[0], "tiles", TGY)]
    rim_shape = f32((chunks + 1) * levels // 2 + kinds // 2 * levels, *plane)
    rims = call(rim_kernel, [smem] + resident(3), resident(1)[0], rim_shape, grid=())(
        meta, statics, left, right
    )
    rims = swapped(rims, "tiles", TGY)
    gates = [(left, right), (halos[0], rims)]
    for c in range(1, min(chunks, 3)):
        halos.append(swapped(after(messages[c], gates[c - 1]), "tiles", TGY))

    far_shape = f32(vectors * half * rows, cols)
    far_shapes = [f32(*omega.shape), f32(*omega.shape), f32(chunks, 2, levels, *plane), far_shape, far_shape]
    final, bound, strip_bound, far_kept, far_sent = call(
        functools.partial(far_kernel, 4),
        [smem] + resident(7),
        resident(len(far_shapes)),
        far_shapes,
        grid=(),
        flops=8 * 10**9,
        scratch=[vmem(7, levels), vmem(2, 7, levels), vmem(chunks, ITERS, levels)],
    )(meta, statics, omega, wet, volume, edges, left, right)
    far_received = swapped(far_sent, "vec", 1)

    weight_shapes = [f32(7, levels, *plane), f32(2, 7, levels, *plane)]
    weights, strip_weights = call(
        near_weight_kernel,
        [smem] + resident(5),
        resident(2),
        weight_shapes,
        grid=(),
    )(meta, statics, rims, edges, left, right)

    field = None
    kept, sent = ([], [])
    steps = [(0, 2)] + [(c, 1) for c in range(2, chunks)]
    for base, parts in steps:
        waits = [(), (far_received,)]
        mine = after(halos[base : base + parts], *(waits[len(sent)] if len(sent) < 2 else ()))
        operands = [meta, omega, wet, volume, rims, left, right, weights, strip_weights, bound, strip_bound, final, *mine]
        specs = [smem] + resident(len(operands) - 1)
        aliases = {}
        if field is not None:
            aliases = {len(operands): 0}
            operands.append(field)
            specs.append(pl.BlockSpec(memory_space=pl.ANY))
        near_shape = f32(parts * group * half * rows, cols)
        batch = 4
        count = parts * group
        field, keep, send = call(
            functools.partial(near_kernel, batch, base, parts),
            specs,
            [pl.BlockSpec(memory_space=pl.ANY)] + resident(2),
            [f32(*omega.shape), near_shape, near_shape],
            flops=2 * 10**9,
            scratch=[
                vmem(parts, ITERS, levels), vmem(count, levels), vmem(count, levels),
                pltpu.SemaphoreType.DMA((count // batch,)),
            ],
            aliases=aliases,
            grid=(),
        )(*operands)
        kept.append(keep)
        sent.append(swapped(send, "vec", 1))
        if len(halos) < chunks:
            halos.append(swapped(after(messages[len(halos)], keep), "tiles", TGY))

    order = 2 * vectors
    gram_shape = f32(order, order)
    far_gram = call(
        functools.partial(far_gram_kernel, half * rows), resident(2), resident(1)[0], gram_shape, grid=()
    )(far_kept, far_received)
    half_gram = f32(3 * order // 8, order)
    mine, theirs = call(
        functools.partial(near_gram_kernel, half * rows),
        [smem] + resident(1 + len(kept + sent)),
        resident(2),
        [half_gram] * 2,
        grid=(),
    )(meta, far_gram, *kept, *sent)
    r_factor = factor(meta, mine, theirs, order, 1.0 / (levels * tiles * rows * cols))
    return (field, r_factor)


def solution(mesh):
    shards = shards_of_two_rows if mesh.shape["tiles"] == 2 * TGY else shards_any
    in_specs = (
        P("vec", None, "tiles", None),
        P(None, None, "tiles", None),
        P("tiles", None),
        P("tiles", None),
        P("tiles", None),
    )
    out_specs = (P("vec", None, "tiles", None), P())
    return jax.shard_map(shards, mesh=mesh, in_specs=in_specs, out_specs=out_specs, check_vma=False)
```

```python
import functools
import jax
import jax.numpy as jnp
from jax import lax
from jax.experimental import pallas as pl
from jax.experimental.pallas import tpu as pltpu
from jax.sharding import PartitionSpec as P

TGY = 8
ITERS = 4
EDGE = 2 * ITERS
VMEM_LIMIT = 32 * 1024 * 1024
EDGE_LIMIT = 63 * 1024 * 1024 + 256 * 1024
MAIN, SLOT = (0, 1)


def ids(shape, axis):
    return lax.broadcasted_iota(jnp.int32, shape, axis)


def turn(value, steps, axis):
    size = value.shape[axis]
    steps = steps % size
    return value if steps == 0 else pltpu.roll(value, steps, axis)


def low_half(shape):
    return ids(shape, 0) < ITERS


def left_lanes(shape):
    return ids(shape, 1) % EDGE < ITERS


def first_pair(a, b):
    return jnp.where(low_half(a.shape), a, turn(b, ITERS, 0))


def last_pair(a, b):
    return jnp.where(low_half(a.shape), turn(a, ITERS, 0), b)


def slots(below, above):
    low = low_half(below.shape)
    return (
        jnp.where(low, below, turn(above, ITERS, 0)),
        jnp.where(low, turn(below, ITERS, 0), above),
    )


def store_pair(outs, index, a, b, is_first_row):
    if len(outs) == 1:
        outs[0][index] = jnp.where(is_first_row, last_pair(a, b), first_pair(a, b))
    else:
        outs[0][index] = first_pair(a, b)
        outs[1][index] = last_pair(a, b)


def add_edge(acc, value, place):
    lanes = ids(value.shape, 1) // EDGE
    moved = turn(value, EDGE * place + ITERS, 1)
    return moved if acc is None else jnp.where(lanes == place, moved, acc)


def prev_row(part, other):
    return jnp.where(ids(part.shape, 0) == 0, turn(other, 1, 0), turn(part, 1, 0))


def next_row(part, other):
    last = part.shape[0] - 1
    return jnp.where(ids(part.shape, 0) == last, turn(other, -1, 0), turn(part, -1, 0))


def prev_col(part, rim):
    return jnp.where(ids(part.shape, 1) == 0, rim, turn(part, 1, 1))


def next_col(part, rim):
    last = part.shape[1] - 1
    return jnp.where(ids(part.shape, 1) == last, rim, turn(part, -1, 1))


def strips(edges, rims):
    left = left_lanes(edges.shape)
    return (jnp.where(left, rims, edges), jnp.where(left, edges, rims))


def crossing(left_strip, right_strip):
    lanes = ids(left_strip.shape, 1) % EDGE
    return jnp.where(lanes == ITERS - 1, turn(right_strip, -1, 1), turn(left_strip, 1, 1))


def rim_of(cross, place):
    return turn(cross, -(EDGE * place + ITERS), 1)


def pack_kernel(chunks, meta, runs, omega, conductance, wet, static_out, edge_out, *row_outs):
    directions = len(row_outs) // chunks
    levels, rows, cols = omega.shape[1:]
    shape = (rows, cols)
    is_first_row = meta[0] == 0
    row_ids, col_ids = (ids(shape, 0), ids(shape, 1))
    wet_cells = wet[...].astype(jnp.float32)
    open_x = (col_ids >= runs[0, 0]) & (col_ids < runs[0, 0] + runs[0, 1])
    open_y = (row_ids >= runs[0, 2]) & (row_ids < runs[0, 2] + runs[0, 3])
    keep_x = (row_ids > 0) | open_x
    keep_y = (col_ids > 0) | open_y
    statics = []
    for level in range(levels):
        statics.append(
            [
                jnp.where(keep_x, conductance[0, level], 0.0),
                jnp.where(keep_y, conductance[1, level], 0.0),
                conductance[2, level] if level else jnp.zeros(shape, jnp.float32),
                wet_cells,
            ]
        )
    kinds = len(statics[0])
    group = cols // EDGE
    for level in range(levels):
        edge = None
        for kind in range(kinds):
            static_out[kind, level] = statics[level][kind]
            edge = add_edge(edge, statics[level][kind], kind)
        edge_out[chunks, level] = edge
        for kind in range(0, kinds, 2):
            outs = row_outs[:directions]
            store_pair(outs, (group // 2 + kind // 2, level), statics[level][kind], statics[level][kind + 1], is_first_row)
        for chunk in range(chunks):
            outs = row_outs[directions * chunk : directions * (chunk + 1)]
            edge = None
            for pair in range(group // 2):
                start = [omega[chunk * group + 2 * pair + i, level] * wet_cells for i in range(2)]
                edge = add_edge(edge, start[0], 2 * pair)
                edge = add_edge(edge, start[1], 2 * pair + 1)
                store_pair(outs, (pair, level), start[0], start[1], is_first_row)
            edge_out[chunk, level] = edge


def corner_kernel(meta, left, right, *outs):
    is_first_row = meta[0] == 0
    groups, levels, rows, cols = left.shape
    take = left_lanes((rows, cols))
    for g in range(groups):
        for level in range(0, levels, 2):
            pair = [jnp.where(take, left[g, level + i], right[g, level + i]) for i in range(2)]
            store_pair(outs, (g, level // 2), pair[0], pair[1], is_first_row)


def rims_of_group(left, right, corner_below, corner_above):
    levels, rows, cols = left.shape[1:]
    take = left_lanes((rows, cols))
    rims = [[jnp.where(take, left[0, level], right[0, level]), None] for level in range(levels)]
    for level in range(0, levels, 2):
        pair = slots(corner_below[0, level // 2], corner_above[0, level // 2])
        rims[level][SLOT], rims[level + 1][SLOT] = pair
    return rims


def weight_kernel(meta, statics, below, above, edges, left, right, corner_below, corner_above, main_out, strip_out):
    kinds, levels, rows, cols = statics.shape
    shape = (rows, cols)
    low = low_half(shape)
    valid = (low & (meta[1] > 0)) | (jnp.logical_not(low) & (meta[0] > 0))
    first = below.shape[0] - kinds // 2
    rims = rims_of_group(left, right, corner_below, corner_above)
    field = [[[statics[kind, level], None] for level in range(levels)] for kind in range(kinds)]
    for level in range(levels):
        for kind in range(0, kinds, 2):
            pair = slots(below[first + kind // 2, level], above[first + kind // 2, level])
            for i in range(2):
                field[kind + i][level][SLOT] = jnp.where(valid, pair[i], 0.0)
    width = cols // EDGE
    lanes = ids(shape, 1) // EDGE

    def spread(strip, kind):
        value = jnp.where(lanes == 0, turn(strip, -EDGE * kind, 1), 0.0)
        span = 1
        while span < width:
            value = value + turn(value, EDGE * span, 1)
            span *= 2
        return value

    side = [[[[None, None] for _ in range(levels)] for _ in range(kinds)] for _ in range(2)]
    cross = [[None, None] for _ in range(levels)]
    for level in range(levels):
        for part in range(2):
            edge = edges[0, level] if part == MAIN else None
            if part == SLOT:
                for kind in range(kinds):
                    edge = add_edge(edge, field[kind][level][SLOT], kind)
            rim = rims[level][part]
            if part == SLOT:
                rim = jnp.where(valid, rim, 0.0)
            pair = strips(edge, rim)
            cross[level][part] = crossing(pair[0], pair[1])
            for s in range(2):
                for kind in range(kinds):
                    side[s][kind][level][part] = spread(pair[s], kind)

    def emit(out, values, after_of):
        for level in range(levels):
            for part in range(2):
                cond_x, cond_y, cond_z, wet = (values[kind][level][part] for kind in range(kinds))
                faces = [
                    cond_x,
                    next_row(cond_x, values[0][level][1 - part]),
                    cond_y,
                    after_of(cond_y, level, part),
                    cond_z,
                    values[2][level + 1][part] if level + 1 < levels else jnp.zeros(shape, jnp.float32),
                ]
                total = faces[0]
                for face in faces[1:]:
                    total = total + face
                out[0, level, part] = wet * (1.0 - total)
                for index, face in enumerate(faces):
                    out[index + 1, level, part] = wet * face

    emit(main_out, field, lambda cond, level, part: next_col(cond, rim_of(cross[level][part], 1)))
    for s in range(2):
        emit(strip_out.at[s], side[s], lambda cond, level, part: turn(cond, -1, 1))


def one_pass(state, weight, parts, rim_at):
    levels = len(state)
    result = [[None, None] for _ in range(levels)]
    for level in range(levels):
        for part in parts:
            value, other = (state[level][part], state[level][1 - part])
            rim = rim_at(level, part)
            before = turn(value, 1, 1) if rim is None else prev_col(value, rim)
            after = turn(value, -1, 1) if rim is None else next_col(value, rim)
            total = weight(0, level, part) * value
            total = total + weight(1, level, part) * prev_row(value, other)
            total = total + weight(2, level, part) * next_row(value, other)
            total = total + weight(3, level, part) * before
            total = total + weight(4, level, part) * after
            if level > 0:
                total = total + weight(5, level, part) * state[level - 1][part]
            if level < levels - 1:
                total = total + weight(6, level, part) * state[level + 1][part]
            result[level][part] = total
    return result


def diffuse_kernel(
    batch, meta, omega, wet, volume, below, above, edges, left, right, corner_below, corner_above,
    main_weights, strip_weights, *rest
):
    field_out, keep_out, send_out, cross_scratch, slot_scratch = rest[-5:]
    group, levels, rows, cols = omega.shape
    shape = (rows, cols)
    wet_cells = wet[...].astype(jnp.float32)
    root = jnp.sqrt(volume[...])
    half = levels // 2
    keeps_low = meta[2] == 0
    rims = rims_of_group(left, right, corner_below, corner_above)
    slot_edges = [None] * levels
    for level in range(levels):
        for pair in range(group // 2):
            two = slots(below[pair, level], above[pair, level])
            for i in range(2):
                slot_scratch[2 * pair + i, level] = two[i]
                slot_edges[level] = add_edge(slot_edges[level], two[i], 2 * pair + i)
    state = [[[None, None] for _ in range(levels)] for _ in range(2)]
    for level in range(levels):
        for part in range(2):
            edge = edges[0, level] if part == MAIN else slot_edges[level]
            pair = strips(edge, rims[level][part])
            for s in range(2):
                state[s][level][part] = pair[s]
    for sweep in range(ITERS):
        for level in range(levels):
            for part in range(2):
                cross_scratch[sweep, level, part] = crossing(state[0][level][part], state[1][level][part])
        if sweep < ITERS - 1:
            for s in range(2):
                state[s] = one_pass(
                    state[s], lambda n, level, part: strip_weights[s, n, level, part], (MAIN, SLOT), lambda level, part: None
                )

    for first in range(0, group, batch):
        fields = []
        for place in range(first, first + batch):
            fields.append([[omega[place, level] * wet_cells, slot_scratch[place, level]] for level in range(levels)])
        for sweep in range(ITERS):
            parts = (MAIN, SLOT) if sweep < ITERS - 1 else (MAIN,)
            for i in range(batch):
                fields[i] = one_pass(
                    fields[i],
                    lambda n, level, part: main_weights[n, level, part],
                    parts,
                    lambda level, part: rim_of(cross_scratch[sweep, level, part], first + i),
                )
        for i in range(batch):
            scaled = []
            for level in range(levels):
                value = fields[i][level][MAIN]
                field_out[first + i, level] = value
                scaled.append(value * root)
            for level in range(half):
                at = ((first + i) * half + level) * rows
                keep_out[at : at + rows, :] = jnp.where(keeps_low, scaled[level], scaled[half + level])
                send_out[at : at + rows, :] = jnp.where(keeps_low, scaled[half + level], scaled[level])


def gram_of_rows(slices, refs):
    groups = [ref.shape[0] // slices for ref in refs]
    order = sum(groups)
    exact = jnp.zeros((order, order), jnp.float32)
    cross = jnp.zeros((order, order), jnp.float32)
    for at in range(0, slices, 2):
        columns = []
        for i in range(2):
            picked = [ref[pl.ds(at + i, group, slices), :] for ref, group in zip(refs, groups)]
            columns.append(jnp.concatenate(picked, axis=0))
        values = jnp.concatenate(columns, axis=1)
        high = values.astype(jnp.bfloat16)
        rest = (values - high.astype(jnp.float32)).astype(jnp.bfloat16)
        dims = (((1,), (1,)), ((), ()))
        exact = exact + lax.dot_general(high, high, dims, preferred_element_type=jnp.float32)
        cross = cross + lax.dot_general(high, rest, dims, preferred_element_type=jnp.float32)
    return exact + (cross + cross.T)


def store_halves(meta, gram, mine, theirs):
    order = gram.shape[0]
    moved = turn(turn(gram, order // 2, 0), order // 2, 1)
    first, second = halves_of_gram(jnp.where(meta[2] == 0, gram, moved))
    is_first = meta[3] == 0
    mine[...] = jnp.where(is_first, first, second)
    theirs[...] = jnp.where(is_first, second, first)


def gram_kernel(chunks, slices, meta, *refs):
    store_halves(meta, gram_of_rows(slices, refs[:-2]), *refs[-2:])


def far_gram_kernel(slices, kept, received, out):
    out[...] = gram_of_rows(slices, (kept, received))


def near_gram_kernel(slices, meta, far, *refs):
    store_halves(meta, far[...] + gram_of_rows(slices, refs[:-2]), *refs[-2:])


def swapped(value, axis, bit):
    count = lax.axis_size(axis)
    return lax.ppermute(value, axis, [(source, source ^ bit) for source in range(count)])


def mesh_permute(value, mask):
    axes = ("tiles", "vec")
    count = lax.axis_size("tiles") * lax.axis_size("vec")
    return lax.ppermute(value, axes, [(source, source ^ mask) for source in range(count)])


def total_over_chips(value):
    vec = lax.axis_size("vec")
    masks = []
    bit = 1
    while bit < vec:
        masks.append(bit)
        bit *= 2
    bit = 2
    while bit < lax.axis_size("tiles"):
        masks.append(bit * vec)
        bit *= 2
    while masks:
        near, masks = (masks[:2], masks[2:])
        if len(near) == 1:
            value = value + mesh_permute(value, near[0])
        else:
            one, two, both = (mesh_permute(value, mask) for mask in (near[0], near[1], near[0] ^ near[1]))
            value = (value + one) + (two + both)
    return value


def fold(a, b):
    half = a.shape[1] // 2
    return jnp.where(ids(a.shape, 1) < half, a, b)


def flip(value):
    return turn(value, value.shape[1] // 2, 1)


def halves_of_gram(gram):
    q = gram.shape[0] // 8
    first = [fold(gram[: 2 * q], flip(gram[2 * q : 4 * q])), fold(flip(gram[:q]), gram[q : 2 * q])]
    second = [fold(flip(gram[4 * q : 6 * q]), gram[6 * q :]), fold(flip(gram[2 * q : 3 * q]), gram[3 * q : 4 * q])]
    return (jnp.concatenate(first, axis=0), jnp.concatenate(second, axis=0))


def gram_of_halves(first, second):
    q = first.shape[0] // 3
    return jnp.concatenate(
        [
            fold(first[:q], flip(first[2 * q :])),
            fold(first[q : 2 * q], first[2 * q :]),
            fold(flip(first[:q]), flip(second[2 * q :])),
            fold(flip(first[q : 2 * q]), second[2 * q :]),
            flip(second[: 2 * q]),
            second[: 2 * q],
        ],
        axis=0,
    )


def spread_lane(value, lane):
    return jnp.broadcast_to(value[:, lane : lane + 1], value.shape)


def squares(rows):
    high = rows.astype(jnp.bfloat16).astype(jnp.float32)
    rest = rows - high
    middle = rest.astype(jnp.bfloat16).astype(jnp.float32)
    low = rest - middle
    one = jnp.concatenate([high, high, middle, high, low, middle], axis=0).astype(jnp.bfloat16)
    two = jnp.concatenate([high, middle, high, low, high, middle], axis=0).astype(jnp.bfloat16)
    return lax.dot_general(one, two, (((0,), (0,)), ((), ())), preferred_element_type=jnp.float32)


def factor_kernel(scale, meta, own, other, out_ref):
    order = out_ref.shape[0]
    height = 8
    count = order // height
    shape = (height, order)
    is_first = meta[3] == 0
    mine, theirs = (own[...], other[...])
    gram = gram_of_halves(jnp.where(is_first, mine, theirs), jnp.where(is_first, theirs, mine)) * scale
    blocks = [gram[height * b : height * (b + 1), :] for b in range(count)]
    row_ids, col_ids = (ids(shape, 0), ids(shape, 1))
    previous = None
    for p in range(count):
        base = height * p
        rows = [jnp.broadcast_to(blocks[p][j : j + 1, :], shape) for j in range(height)]
        corner = {(i, j): spread_lane(rows[j], base + i) for j in range(height) for i in range(j, height)}
        if previous is not None:
            for done in previous:
                lanes = [spread_lane(done, base + j) for j in range(height)]
                for j in range(height):
                    rows[j] = rows[j] - lanes[j] * done
                    for i in range(j, height):
                        corner[i, j] = corner[i, j] - lanes[i] * lanes[j]
        panel = jnp.zeros(shape, jnp.float32)
        for s in range(height):
            inverse = lax.rsqrt(corner[s, s])
            rows[s] = rows[s] * inverse
            lanes = {j: corner[j, s] * inverse for j in range(s + 1, height)}
            for j in range(s + 1, height):
                for i in range(j, height):
                    corner[i, j] = corner[i, j] - lanes[i] * lanes[j]
                rows[j] = rows[j] - lanes[j] * rows[s]
            panel = jnp.where(row_ids == s, rows[s], panel)
        panel = jnp.where(col_ids >= base + row_ids, panel, 0.0)
        out_ref[base : base + height, :] = panel
        if p + 2 < count:
            update = squares(panel)
            for q in range(p + 2, count):
                blocks[q] = blocks[q] - update[height * q : height * (q + 1), :]
        previous = rows


def edge_kernel(runs, omega, conductance, wet, static_out, edge_out):
    levels, rows, cols = omega.shape[1:]
    shape = (rows, cols)
    row_ids, col_ids = (ids(shape, 0), ids(shape, 1))
    wet_cells = wet[...].astype(jnp.float32)
    open_x = (col_ids >= runs[0, 0]) & (col_ids < runs[0, 0] + runs[0, 1])
    open_y = (row_ids >= runs[0, 2]) & (row_ids < runs[0, 2] + runs[0, 3])
    keep_x = (row_ids > 0) | open_x
    keep_y = (col_ids > 0) | open_y
    group = cols // EDGE
    chunks = omega.shape[0] // group
    for level in range(levels):
        statics = [
            jnp.where(keep_x, conductance[0, level], 0.0),
            jnp.where(keep_y, conductance[1, level], 0.0),
            conductance[2, level] if level else jnp.zeros(shape, jnp.float32),
            wet_cells,
        ]
        edge = None
        for kind, value in enumerate(statics):
            static_out[kind, level] = value
            edge = add_edge(edge, value, kind)
        edge_out[chunks, level] = edge
        for chunk in range(chunks):
            edge = None
            for place in range(group):
                edge = add_edge(edge, omega[chunk * group + place, level] * wet_cells, place)
            edge_out[chunk, level] = edge


def face_kernel(first, meta, omega, wet, *row_outs):
    levels, rows, cols = omega.shape[1:]
    group = cols // EDGE
    is_first_row = meta[0] == 0
    wet_cells = wet[...].astype(jnp.float32)
    for chunk, out in enumerate(row_outs):
        for level in range(levels):
            for pair in range(group // 2):
                at = (first + chunk) * group + 2 * pair
                start = [omega[at + i, level] * wet_cells for i in range(2)]
                store_pair((out,), (pair, level), start[0], start[1], is_first_row)


def rim_kernel(meta, statics, left, right, out):
    is_first_row = meta[0] == 0
    groups, levels, rows, cols = left.shape
    kinds = statics.shape[0]
    take = left_lanes((rows, cols))
    for g in range(groups):
        for level in range(0, levels, 2):
            pair = [jnp.where(take, left[g, level + i], right[g, level + i]) for i in range(2)]
            store_pair((out,), g * levels // 2 + level // 2, pair[0], pair[1], is_first_row)
    first = groups * levels // 2
    for kind in range(0, kinds, 2):
        for level in range(levels):
            at = first + kind // 2 * levels + level
            store_pair((out,), at, statics[kind, level], statics[kind + 1, level], is_first_row)


def near_rows(is_first_row, a, b, halo):
    low = low_half(halo.shape)
    turned = turn(halo, ITERS, 0)
    result = []
    for own, across, moved in ((a, halo, turned), (b, turned, halo)):
        near = turn(own, ITERS, 0)
        result.append(jnp.where(low, jnp.where(is_first_row, near, across), jnp.where(is_first_row, moved, near)))
    return result


def spread_kind(strip, kind):
    cols = strip.shape[1]
    value = jnp.where(ids(strip.shape, 1) // EDGE == 0, turn(strip, -EDGE * kind, 1), 0.0)
    span = EDGE
    while span < cols:
        value = value + turn(value, span, 1)
        span *= 2
    return value


def store_weights(out, values, after_row, after_col):
    levels = len(values[0])
    for level in range(levels):
        cond_x, cond_y, cond_z, wet = (kind[level] for kind in values)
        below = values[2][level + 1] if level + 1 < levels else jnp.zeros_like(cond_z)
        faces = [cond_x, after_row(level), cond_y, after_col(level), cond_z, below]
        total = faces[0]
        for face in faces[1:]:
            total = total + face
        out[0, level] = wet * (1.0 - total)
        for index, face in enumerate(faces):
            out[index + 1, level] = wet * face


def plane_pass(state, weight, row_before, row_after, rim_at):
    levels = len(state)
    result = []
    for level in range(levels):
        value = state[level]
        rim = rim_at(level)
        before = turn(value, 1, 1) if rim is None else prev_col(value, rim)
        after = turn(value, -1, 1) if rim is None else next_col(value, rim)
        total = weight(0, level) * value
        total = total + weight(1, level) * row_before(value, level)
        total = total + weight(2, level) * row_after(value, level)
        total = total + weight(3, level) * before
        total = total + weight(4, level) * after
        if level > 0:
            total = total + weight(5, level) * state[level - 1]
        if level < levels - 1:
            total = total + weight(6, level) * state[level + 1]
        result.append(total)
    return result


def no_rim(level):
    return None


def pack_levels(values, use_first):
    pairs = []
    for level in range(0, len(values), 2):
        a, b = values[level : level + 2]
        pairs.append(jnp.where(use_first, first_pair(a, b), last_pair(a, b)))
    return pairs


def store_half(keep, send, place, pairs, keeps_low):
    rows = pairs[0].shape[0]
    half = len(pairs) // 2
    for i in range(half):
        at = (place * half + i) * rows
        keep[at : at + rows, :] = jnp.where(keeps_low, pairs[i], pairs[half + i])
        send[at : at + rows, :] = jnp.where(keeps_low, pairs[half + i], pairs[i])


def far_kernel(
    batch, meta, statics, omega, wet, volume, edges, left, right,
    final_out, bound_out, strip_bound_out, keep_out, send_out, weights, strip_weights, cross_scratch
):
    vectors, levels, rows, cols = omega.shape
    kinds = statics.shape[0]
    shape = (rows, cols)
    group = cols // EDGE
    chunks = vectors // group
    is_first_row = meta[0] == 0
    keeps_low = meta[2] == 0
    row_ids = ids(shape, 0)
    take = left_lanes(shape)
    wet_cells = wet[...].astype(jnp.float32)
    root = jnp.sqrt(volume[...])

    def sides(g, level):
        return strips(edges[g, level], jnp.where(take, left[g, level], right[g, level]))

    def roll_before(value, level):
        return turn(value, 1, 0)

    def roll_after(value, level):
        return turn(value, -1, 0)

    def closed_after(value):
        return jnp.where(row_ids == rows - 1, 0.0, turn(value, -1, 0))

    field = [[statics[kind, level] for level in range(levels)] for kind in range(kinds)]
    pairs = [sides(chunks, level) for level in range(levels)]
    crosses = [crossing(*pair) for pair in pairs]
    store_weights(
        weights, field, lambda level: closed_after(field[0][level]),
        lambda level: next_col(field[1][level], rim_of(crosses[level], 1)),
    )
    for s in range(2):
        side = [[spread_kind(pairs[level][s], kind) for level in range(levels)] for kind in range(kinds)]
        store_weights(
            strip_weights.at[s], side, lambda level: closed_after(side[0][level]), lambda level: turn(side[1][level], -1, 1)
        )

    def keep_bound(acc, value, sweep):
        edge = jnp.where(is_first_row, value, turn(value, -1, 0))
        moved = turn(edge, sweep - (ITERS - 1), 0)
        return moved if acc is None else jnp.where(row_ids == sweep, moved, acc)

    for g in range(chunks):
        state = [[sides(g, level)[s] for level in range(levels)] for s in range(2)]
        bounds = [[None] * levels for _ in range(2)]
        for sweep in range(ITERS):
            for level in range(levels):
                cross_scratch[g, sweep, level] = crossing(state[0][level], state[1][level])
                for s in range(2):
                    bounds[s][level] = keep_bound(bounds[s][level], state[s][level], sweep)
            if sweep < ITERS - 1:
                for s in range(2):
                    state[s] = plane_pass(
                        state[s], lambda n, level: strip_weights[s, n, level], roll_before, roll_after, no_rim
                    )
        for s in range(2):
            for level in range(levels):
                strip_bound_out[g, s, level] = bounds[s][level]

    for first in range(0, vectors, batch):
        g = first // group
        fields = [[omega[place, level] * wet_cells for level in range(levels)] for place in range(first, first + batch)]
        bounds = [[None] * levels for _ in range(batch)]
        for sweep in range(ITERS):
            for i in range(batch):
                for level in range(levels):
                    bounds[i][level] = keep_bound(bounds[i][level], fields[i][level], sweep)
                fields[i] = plane_pass(
                    fields[i], lambda n, level: weights[n, level], roll_before, roll_after,
                    lambda level: rim_of(cross_scratch[g, sweep, level], (first + i) % group),
                )
        for i in range(batch):
            for level in range(levels):
                final_out[first + i, level] = fields[i][level]
                bound_out[first + i, level] = bounds[i][level]
            scaled = [value * root for value in fields[i]]
            store_half(keep_out, send_out, first + i, pack_levels(scaled, is_first_row), keeps_low)


def near_weight_kernel(meta, statics, rims, edges, left, right, weights, strip_weights):
    kinds, levels, rows, cols = statics.shape
    shape = (rows, cols)
    is_first_row = meta[0] == 0
    take = left_lanes(shape)
    last = ids(shape, 0) == rows - 1
    g = edges.shape[0] - 1
    groups = edges.shape[0]
    first = groups * levels // 2
    field = [[None] * levels for _ in range(kinds)]
    for kind in range(0, kinds, 2):
        for level in range(levels):
            own = (statics[kind, level], statics[kind + 1, level])
            pair = near_rows(is_first_row, *own, rims[first + kind // 2 * levels + level])
            field[kind][level], field[kind + 1][level] = pair
    rim = [jnp.where(take, left[g, level], right[g, level]) for level in range(levels)]
    near_rim = []
    for level in range(0, levels, 2):
        near_rim += near_rows(is_first_row, rim[level], rim[level + 1], rims[g * levels // 2 + level // 2])
    near_edge = []
    for level in range(levels):
        edge = None
        for kind in range(kinds):
            edge = add_edge(edge, field[kind][level], kind)
        near_edge.append(edge)
    pairs = [strips(near_edge[level], near_rim[level]) for level in range(levels)]
    tile_pairs = [strips(edges[g, level], rim[level]) for level in range(levels)]
    crosses = [crossing(*pair) for pair in pairs]

    def with_next(value, tile_value):
        beyond = jnp.broadcast_to(tile_value[ITERS : ITERS + 1, :], shape)
        return jnp.where(last, beyond, turn(value, -1, 0))

    store_weights(
        weights, field, lambda level: with_next(field[0][level], statics[0, level]),
        lambda level: next_col(field[1][level], rim_of(crosses[level], 1)),
    )
    for s in range(2):
        side = [[spread_kind(pairs[level][s], kind) for level in range(levels)] for kind in range(kinds)]
        tile_side = [spread_kind(tile_pairs[level][s], 0) for level in range(levels)]
        store_weights(
            strip_weights.at[s], side, lambda level: with_next(side[0][level], tile_side[level]),
            lambda level: turn(side[1][level], -1, 1),
        )


def near_kernel(
    batch, base, parts, meta, omega, wet, volume, rims, left, right, weights, strip_weights, bound, strip_bound, final, *rest
):
    halos = rest[:parts]
    field_out, keep_out, send_out, cross_scratch, start, done, sems = rest[-7:]
    levels, rows, cols = omega.shape[1:]
    group = cols // EDGE
    offset = base * group
    shape = (rows, cols)
    is_first_row = meta[0] == 0
    keeps_low = meta[2] == 0
    row_ids = ids(shape, 0)
    take = left_lanes(shape)
    top = (row_ids == 0) & is_first_row
    bottom = (row_ids == rows - 1) & jnp.logical_not(is_first_row)
    is_near = low_half(shape) != is_first_row
    wet_cells = wet[...].astype(jnp.float32)
    root = jnp.sqrt(volume[...])

    def around(bound_at, sweep):
        def kept(level):
            return jnp.broadcast_to(bound_at(level)[sweep : sweep + 1, :], shape)

        return (
            lambda value, level: jnp.where(top, kept(level), turn(value, 1, 0)),
            lambda value, level: jnp.where(bottom, kept(level), turn(value, -1, 0)),
        )

    for part in range(parts):
        near_edge = [None] * levels
        for level in range(levels):
            for pair in range(group // 2):
                at = part * group + 2 * pair
                own = [omega[offset + at + i, level] * wet_cells for i in range(2)]
                two = near_rows(is_first_row, *own, halos[part][pair, level])
                for i in range(2):
                    start[at + i, level] = two[i]
                    near_edge[level] = add_edge(near_edge[level], two[i], 2 * pair + i)
        rim = [jnp.where(take, left[base + part, level], right[base + part, level]) for level in range(levels)]
        near_rim = []
        for level in range(0, levels, 2):
            across = rims[(base + part) * levels // 2 + level // 2]
            near_rim += near_rows(is_first_row, rim[level], rim[level + 1], across)
        pairs = [strips(near_edge[level], near_rim[level]) for level in range(levels)]
        state = [[pairs[level][s] for level in range(levels)] for s in range(2)]
        for sweep in range(ITERS):
            for level in range(levels):
                cross_scratch[part, sweep, level] = crossing(state[0][level], state[1][level])
            if sweep < ITERS - 1:
                for s in range(2):
                    state[s] = plane_pass(
                        state[s], lambda n, level: strip_weights[s, n, level],
                        *around(lambda level: strip_bound[base + part, s, level], sweep), no_rim,
                    )

    copies = []
    for first in range(0, parts * group, batch):
        part = first // group
        fields = [[start[place, level] for level in range(levels)] for place in range(first, first + batch)]
        for sweep in range(ITERS):
            for i in range(batch):
                fields[i] = plane_pass(
                    fields[i], lambda n, level: weights[n, level],
                    *around(lambda level: bound[offset + first + i, level], sweep),
                    lambda level: rim_of(cross_scratch[part, sweep, level], (first + i) % group),
                )
        for i in range(batch):
            scaled = []
            for level in range(levels):
                value = jnp.where(is_near, turn(fields[i][level], ITERS, 0), final[offset + first + i, level])
                done[first + i, level] = value
                scaled.append(value * root)
            store_half(keep_out, send_out, first + i, pack_levels(scaled, jnp.logical_not(is_first_row)), keeps_low)
        copies.append(
            pltpu.make_async_copy(
                done.at[pl.ds(first, batch)], field_out.at[pl.ds(offset + first, batch)], sems.at[first // batch]
            )
        )
        copies[-1].start()
    for copy in copies:
        copy.wait()


def shifted(value, axis, steps):
    count = lax.axis_size(axis)
    first, last = (max(0, -steps), min(count, count - steps))
    return lax.ppermute(value, axis, [(source, source + steps) for source in range(first, last)])


def beside(value, steps):
    count = lax.axis_size("tiles")
    pairs = [(source, source + steps) for source in range(count)]
    return lax.ppermute(value, "tiles", [(a, b) for a, b in pairs if 0 <= b < count and a // TGY == b // TGY])


def after(values, *done):
    return lax.optimization_barrier((values, done))[0]


def exchange_rows(messages, grid_rows):
    if len(messages) == 1:
        received = swapped(messages[0], "tiles", TGY)
        return (received, received)
    return (shifted(messages[0], "tiles", -TGY), shifted(messages[1], "tiles", TGY))


def f32(*shape):
    return jax.ShapeDtypeStruct(shape, jnp.float32)


def block(shape, *at):
    return pl.BlockSpec(shape, lambda i: at)


def call(kernel, in_specs, out_specs, out_shape, flops=0, scratch=(), aliases=None, limit=VMEM_LIMIT, grid=(1,)):
    return pl.pallas_call(
        kernel,
        grid=grid,
        in_specs=in_specs,
        out_specs=out_specs,
        out_shape=out_shape,
        scratch_shapes=scratch,
        input_output_aliases=aliases or {},
        compiler_params=pltpu.CompilerParams(vmem_limit_bytes=limit),
        cost_estimate=pl.CostEstimate(flops=flops, bytes_accessed=1 << 20, transcendentals=0),
    )


def resident(count):
    return [pl.BlockSpec(memory_space=pltpu.VMEM)] * count


def whole(array):
    zeros = (0,) * array.ndim
    return pl.BlockSpec(array.shape, lambda i: zeros)


def factor(meta, mine, theirs, order, scale):
    mine = total_over_chips(mine + swapped(theirs, "tiles", 1))
    smem = pl.BlockSpec(memory_space=pltpu.SMEM)
    return call(
        functools.partial(factor_kernel, scale),
        [smem] + resident(2),
        resident(1)[0],
        f32(order, order),
        grid=(),
    )(meta, mine, swapped(mine, "tiles", 1))


def shards_any(omega, conductance, wet, volume, face_runs):
    vectors, levels, rows, cols = omega.shape
    tiles = lax.axis_size("tiles")
    grid_rows = tiles // TGY
    tile_row = lax.axis_index("tiles") // TGY
    core = lax.axis_index("tiles") % 2
    meta = jnp.stack([tile_row, grid_rows - 1 - tile_row, lax.axis_index("vec"), core]).astype(jnp.int32)
    smem = pl.BlockSpec(memory_space=pltpu.SMEM)
    group = cols // EDGE
    chunks = vectors // group
    directions = 1 if grid_rows == 2 else 2
    kinds = 4
    half = levels // 2

    row_shapes = [f32(group // 2 + (kinds // 2 if c == 0 else 0), levels, rows, cols) for c in range(chunks)]
    row_shapes = [shape for shape in row_shapes for _ in range(directions)]
    packed_shapes = [f32(kinds, levels, rows, cols), f32(chunks + 1, levels, rows, cols)] + row_shapes
    statics, edges, *messages = call(
        functools.partial(pack_kernel, chunks),
        [smem, smem, whole(omega), whole(conductance), whole(wet)],
        [whole(s) for s in packed_shapes],
        packed_shapes,
    )(meta, face_runs, omega, conductance, wet)
    messages = [messages[directions * c : directions * (c + 1)] for c in range(chunks)]
    received = [exchange_rows(messages[0], grid_rows)]
    left = beside(edges, 1)
    right = beside(edges, -1)
    corner_shapes = [f32(chunks + 1, levels // 2, rows, cols)] * directions
    corners = call(
        corner_kernel, [smem, whole(left), whole(right)], [whole(s) for s in corner_shapes], corner_shapes
    )(meta, left, right)
    corners = exchange_rows(corners, grid_rows)
    gates = [(left, right), corners]
    for c in range(1, chunks):
        gate = gates[c - 1] if c <= 2 else received[c - 2]
        received.append(exchange_rows(after(messages[c], *gate), grid_rows))

    def group_specs(c):
        edge = block((1, levels, rows, cols), c, 0, 0, 0)
        corner = block((1, levels // 2, rows, cols), c, 0, 0, 0)
        return [edge, edge, edge, corner, corner]

    around = (edges, left, right, *corners)
    weight_shapes = [f32(7, levels, 2, rows, cols), f32(2, 7, levels, 2, rows, cols)]
    main_weights, strip_weights = call(
        weight_kernel,
        [smem, whole(statics), whole(received[0][0]), whole(received[0][1])] + group_specs(chunks),
        [whole(s) for s in weight_shapes],
        weight_shapes,
    )(meta, statics, *received[0], *around)

    field = None
    kept, sent = ([], [])
    half_shape = f32(group * half * rows, cols)
    for c in range(chunks):
        rims = after(received[c], sent[c - 2]) if c >= 2 else received[c]
        operands = [meta, omega, wet, volume, *rims, *around, main_weights, strip_weights]
        row_block = block((group // 2, levels, rows, cols), 0, 0, 0, 0)
        chunk_block = block((group, levels, rows, cols), c, 0, 0, 0)
        specs = [smem, chunk_block, whole(wet), whole(volume), row_block, row_block] + group_specs(c)
        specs += [whole(main_weights), whole(strip_weights)]
        aliases = {}
        if field is not None:
            aliases = {len(operands): 0}
            operands.append(field)
            specs.append(pl.BlockSpec(memory_space=pl.ANY))
        field, keep, send = call(
            functools.partial(diffuse_kernel, 4),
            specs,
            [chunk_block, whole(half_shape), whole(half_shape)],
            [f32(*omega.shape), half_shape, half_shape],
            flops=4 * 10**9,
            scratch=[pltpu.VMEM((ITERS, levels, 2, rows, cols), jnp.float32), pltpu.VMEM((group, levels, rows, cols), jnp.float32)],
            aliases=aliases,
        )(*operands)
        kept.append(keep)
        sent.append(swapped(send, "vec", 1))

    order = 2 * vectors
    half_gram = f32(3 * order // 8, order)
    mine, theirs = call(
        functools.partial(gram_kernel, chunks, half * rows),
        [smem] + [whole(half_shape)] * (2 * chunks),
        [whole(half_gram)] * 2,
        [half_gram] * 2,
    )(meta, *kept, *sent)
    r_factor = factor(meta, mine, theirs, order, 1.0 / (levels * tiles * rows * cols))
    return (field, r_factor)


def shards_of_two_rows(omega, conductance, wet, volume, face_runs):
    vectors, levels, rows, cols = omega.shape
    tiles = lax.axis_size("tiles")
    tile_row = lax.axis_index("tiles") // TGY
    core = lax.axis_index("tiles") % 2
    meta = jnp.stack([tile_row, 1 - tile_row, lax.axis_index("vec"), core]).astype(jnp.int32)
    smem = pl.BlockSpec(memory_space=pltpu.SMEM)
    group = cols // EDGE
    chunks = vectors // group
    kinds = 4
    half = levels // 4
    plane = (rows, cols)

    def vmem(*lead):
        return pltpu.VMEM(lead + plane, jnp.float32)

    row_shape = f32(group // 2, levels, *plane)
    chunk0 = call(
        functools.partial(face_kernel, 0),
        [smem, block((group, levels, *plane), 0, 0, 0, 0), whole(wet)],
        [whole(row_shape)],
        [row_shape],
        limit=EDGE_LIMIT,
    )(meta, omega, wet)
    edge_shapes = [f32(kinds, levels, *plane), f32(chunks + 1, levels, *plane)]
    statics, edges = call(
        edge_kernel,
        [smem, whole(omega), whole(conductance), whole(wet)],
        [whole(s) for s in edge_shapes],
        edge_shapes,
        limit=EDGE_LIMIT,
    )(after(face_runs, chunk0), omega, conductance, wet)
    left = beside(edges, 1)
    right = beside(edges, -1)
    row_shapes = [row_shape] * (chunks - 1)
    messages = chunk0 + call(
        functools.partial(face_kernel, 1),
        [smem] + resident(2),
        resident(len(row_shapes)),
        row_shapes,
        flops=10**9,
        grid=(),
    )(meta, omega, wet)
    halos = [swapped(messages[0], "tiles", TGY)]
    rim_shape = f32((chunks + 1) * levels // 2 + kinds // 2 * levels, *plane)
    rims = call(rim_kernel, [smem] + resident(3), resident(1)[0], rim_shape, grid=())(
        meta, statics, left, right
    )
    rims = swapped(rims, "tiles", TGY)
    gates = [(left, right), (halos[0], rims)]
    for c in range(1, min(chunks, 3)):
        halos.append(swapped(after(messages[c], gates[c - 1]), "tiles", TGY))

    far_shape = f32(vectors * half * rows, cols)
    far_shapes = [f32(*omega.shape), f32(*omega.shape), f32(chunks, 2, levels, *plane), far_shape, far_shape]
    final, bound, strip_bound, far_kept, far_sent = call(
        functools.partial(far_kernel, 8),
        [smem] + resident(7),
        resident(len(far_shapes)),
        far_shapes,
        grid=(),
        flops=8 * 10**9,
        scratch=[vmem(7, levels), vmem(2, 7, levels), vmem(chunks, ITERS, levels)],
    )(meta, statics, omega, wet, volume, edges, left, right)
    far_received = swapped(far_sent, "vec", 1)

    weight_shapes = [f32(7, levels, *plane), f32(2, 7, levels, *plane)]
    weights, strip_weights = call(
        near_weight_kernel,
        [smem] + resident(5),
        resident(2),
        weight_shapes,
        grid=(),
    )(meta, statics, rims, edges, left, right)

    field = None
    kept, sent = ([], [])
    steps = [(0, 2)] + [(c, 1) for c in range(2, chunks)]
    for base, parts in steps:
        waits = [(), (far_received,)]
        mine = after(halos[base : base + parts], *(waits[len(sent)] if len(sent) < 2 else ()))
        operands = [meta, omega, wet, volume, rims, left, right, weights, strip_weights, bound, strip_bound, final, *mine]
        specs = [smem] + resident(len(operands) - 1)
        aliases = {}
        if field is not None:
            aliases = {len(operands): 0}
            operands.append(field)
            specs.append(pl.BlockSpec(memory_space=pl.ANY))
        near_shape = f32(parts * group * half * rows, cols)
        batch = 8
        count = parts * group
        field, keep, send = call(
            functools.partial(near_kernel, batch, base, parts),
            specs,
            [pl.BlockSpec(memory_space=pl.ANY)] + resident(2),
            [f32(*omega.shape), near_shape, near_shape],
            flops=2 * 10**9,
            scratch=[
                vmem(parts, ITERS, levels), vmem(count, levels), vmem(count, levels),
                pltpu.SemaphoreType.DMA((count // batch,)),
            ],
            aliases=aliases,
            grid=(),
        )(*operands)
        kept.append(keep)
        sent.append(swapped(send, "vec", 1))
        if len(halos) < chunks:
            halos.append(swapped(after(messages[len(halos)], keep), "tiles", TGY))

    order = 2 * vectors
    gram_shape = f32(order, order)
    far_gram = call(
        functools.partial(far_gram_kernel, half * rows), resident(2), resident(1)[0], gram_shape, grid=()
    )(far_kept, far_received)
    half_gram = f32(3 * order // 8, order)
    mine, theirs = call(
        functools.partial(near_gram_kernel, half * rows),
        [smem] + resident(1 + len(kept + sent)),
        resident(2),
        [half_gram] * 2,
        grid=(),
    )(meta, far_gram, *kept, *sent)
    r_factor = factor(meta, mine, theirs, order, 1.0 / (levels * tiles * rows * cols))
    return (field, r_factor)


def solution(mesh):
    shards = shards_of_two_rows if mesh.shape["tiles"] == 2 * TGY else shards_any
    in_specs = (
        P("vec", None, "tiles", None),
        P(None, None, "tiles", None),
        P("tiles", None),
        P("tiles", None),
        P("tiles", None),
    )
    out_specs = (P("vec", None, "tiles", None), P())
    return jax.shard_map(shards, mesh=mesh, in_specs=in_specs, out_specs=out_specs, check_vma=False)
```

```python
import functools
import jax
import jax.numpy as jnp
from jax import lax
from jax.experimental import pallas as pl
from jax.experimental.pallas import tpu as pltpu
from jax.sharding import PartitionSpec as P

TGY = 8
ITERS = 4
EDGE = 2 * ITERS
VMEM_LIMIT = 32 * 1024 * 1024
EDGE_LIMIT = 63 * 1024 * 1024 + 256 * 1024
MAIN, SLOT = (0, 1)


def ids(shape, axis):
    return lax.broadcasted_iota(jnp.int32, shape, axis)


def turn(value, steps, axis):
    size = value.shape[axis]
    steps = steps % size
    return value if steps == 0 else pltpu.roll(value, steps, axis)


def low_half(shape):
    return ids(shape, 0) < ITERS


def left_lanes(shape):
    return ids(shape, 1) % EDGE < ITERS


def first_pair(a, b):
    return jnp.where(low_half(a.shape), a, turn(b, ITERS, 0))


def last_pair(a, b):
    return jnp.where(low_half(a.shape), turn(a, ITERS, 0), b)


def slots(below, above):
    low = low_half(below.shape)
    return (
        jnp.where(low, below, turn(above, ITERS, 0)),
        jnp.where(low, turn(below, ITERS, 0), above),
    )


def store_pair(outs, index, a, b, is_first_row):
    if len(outs) == 1:
        outs[0][index] = jnp.where(is_first_row, last_pair(a, b), first_pair(a, b))
    else:
        outs[0][index] = first_pair(a, b)
        outs[1][index] = last_pair(a, b)


def add_edge(acc, value, place):
    lanes = ids(value.shape, 1) // EDGE
    moved = turn(value, EDGE * place + ITERS, 1)
    return moved if acc is None else jnp.where(lanes == place, moved, acc)


def prev_row(part, other):
    return jnp.where(ids(part.shape, 0) == 0, turn(other, 1, 0), turn(part, 1, 0))


def next_row(part, other):
    last = part.shape[0] - 1
    return jnp.where(ids(part.shape, 0) == last, turn(other, -1, 0), turn(part, -1, 0))


def prev_col(part, rim):
    return jnp.where(ids(part.shape, 1) == 0, rim, turn(part, 1, 1))


def next_col(part, rim):
    last = part.shape[1] - 1
    return jnp.where(ids(part.shape, 1) == last, rim, turn(part, -1, 1))


def strips(edges, rims):
    left = left_lanes(edges.shape)
    return (jnp.where(left, rims, edges), jnp.where(left, edges, rims))


def crossing(left_strip, right_strip):
    lanes = ids(left_strip.shape, 1) % EDGE
    return jnp.where(lanes == ITERS - 1, turn(right_strip, -1, 1), turn(left_strip, 1, 1))


def rim_of(cross, place):
    return turn(cross, -(EDGE * place + ITERS), 1)


def pack_kernel(chunks, meta, runs, omega, conductance, wet, static_out, edge_out, *row_outs):
    directions = len(row_outs) // chunks
    levels, rows, cols = omega.shape[1:]
    shape = (rows, cols)
    is_first_row = meta[0] == 0
    row_ids, col_ids = (ids(shape, 0), ids(shape, 1))
    wet_cells = wet[...].astype(jnp.float32)
    open_x = (col_ids >= runs[0, 0]) & (col_ids < runs[0, 0] + runs[0, 1])
    open_y = (row_ids >= runs[0, 2]) & (row_ids < runs[0, 2] + runs[0, 3])
    keep_x = (row_ids > 0) | open_x
    keep_y = (col_ids > 0) | open_y
    statics = []
    for level in range(levels):
        statics.append(
            [
                jnp.where(keep_x, conductance[0, level], 0.0),
                jnp.where(keep_y, conductance[1, level], 0.0),
                conductance[2, level] if level else jnp.zeros(shape, jnp.float32),
                wet_cells,
            ]
        )
    kinds = len(statics[0])
    group = cols // EDGE
    for level in range(levels):
        edge = None
        for kind in range(kinds):
            static_out[kind, level] = statics[level][kind]
            edge = add_edge(edge, statics[level][kind], kind)
        edge_out[chunks, level] = edge
        for kind in range(0, kinds, 2):
            outs = row_outs[:directions]
            store_pair(outs, (group // 2 + kind // 2, level), statics[level][kind], statics[level][kind + 1], is_first_row)
        for chunk in range(chunks):
            outs = row_outs[directions * chunk : directions * (chunk + 1)]
            edge = None
            for pair in range(group // 2):
                start = [omega[chunk * group + 2 * pair + i, level] * wet_cells for i in range(2)]
                edge = add_edge(edge, start[0], 2 * pair)
                edge = add_edge(edge, start[1], 2 * pair + 1)
                store_pair(outs, (pair, level), start[0], start[1], is_first_row)
            edge_out[chunk, level] = edge


def corner_kernel(meta, left, right, *outs):
    is_first_row = meta[0] == 0
    groups, levels, rows, cols = left.shape
    take = left_lanes((rows, cols))
    for g in range(groups):
        for level in range(0, levels, 2):
            pair = [jnp.where(take, left[g, level + i], right[g, level + i]) for i in range(2)]
            store_pair(outs, (g, level // 2), pair[0], pair[1], is_first_row)


def rims_of_group(left, right, corner_below, corner_above):
    levels, rows, cols = left.shape[1:]
    take = left_lanes((rows, cols))
    rims = [[jnp.where(take, left[0, level], right[0, level]), None] for level in range(levels)]
    for level in range(0, levels, 2):
        pair = slots(corner_below[0, level // 2], corner_above[0, level // 2])
        rims[level][SLOT], rims[level + 1][SLOT] = pair
    return rims


def weight_kernel(meta, statics, below, above, edges, left, right, corner_below, corner_above, main_out, strip_out):
    kinds, levels, rows, cols = statics.shape
    shape = (rows, cols)
    low = low_half(shape)
    valid = (low & (meta[1] > 0)) | (jnp.logical_not(low) & (meta[0] > 0))
    first = below.shape[0] - kinds // 2
    rims = rims_of_group(left, right, corner_below, corner_above)
    field = [[[statics[kind, level], None] for level in range(levels)] for kind in range(kinds)]
    for level in range(levels):
        for kind in range(0, kinds, 2):
            pair = slots(below[first + kind // 2, level], above[first + kind // 2, level])
            for i in range(2):
                field[kind + i][level][SLOT] = jnp.where(valid, pair[i], 0.0)
    width = cols // EDGE
    lanes = ids(shape, 1) // EDGE

    def spread(strip, kind):
        value = jnp.where(lanes == 0, turn(strip, -EDGE * kind, 1), 0.0)
        span = 1
        while span < width:
            value = value + turn(value, EDGE * span, 1)
            span *= 2
        return value

    side = [[[[None, None] for _ in range(levels)] for _ in range(kinds)] for _ in range(2)]
    cross = [[None, None] for _ in range(levels)]
    for level in range(levels):
        for part in range(2):
            edge = edges[0, level] if part == MAIN else None
            if part == SLOT:
                for kind in range(kinds):
                    edge = add_edge(edge, field[kind][level][SLOT], kind)
            rim = rims[level][part]
            if part == SLOT:
                rim = jnp.where(valid, rim, 0.0)
            pair = strips(edge, rim)
            cross[level][part] = crossing(pair[0], pair[1])
            for s in range(2):
                for kind in range(kinds):
                    side[s][kind][level][part] = spread(pair[s], kind)

    def emit(out, values, after_of):
        for level in range(levels):
            for part in range(2):
                cond_x, cond_y, cond_z, wet = (values[kind][level][part] for kind in range(kinds))
                faces = [
                    cond_x,
                    next_row(cond_x, values[0][level][1 - part]),
                    cond_y,
                    after_of(cond_y, level, part),
                    cond_z,
                    values[2][level + 1][part] if level + 1 < levels else jnp.zeros(shape, jnp.float32),
                ]
                total = faces[0]
                for face in faces[1:]:
                    total = total + face
                out[0, level, part] = wet * (1.0 - total)
                for index, face in enumerate(faces):
                    out[index + 1, level, part] = wet * face

    emit(main_out, field, lambda cond, level, part: next_col(cond, rim_of(cross[level][part], 1)))
    for s in range(2):
        emit(strip_out.at[s], side[s], lambda cond, level, part: turn(cond, -1, 1))


def one_pass(state, weight, parts, rim_at):
    levels = len(state)
    result = [[None, None] for _ in range(levels)]
    for level in range(levels):
        for part in parts:
            value, other = (state[level][part], state[level][1 - part])
            rim = rim_at(level, part)
            before = turn(value, 1, 1) if rim is None else prev_col(value, rim)
            after = turn(value, -1, 1) if rim is None else next_col(value, rim)
            total = weight(0, level, part) * value
            total = total + weight(1, level, part) * prev_row(value, other)
            total = total + weight(2, level, part) * next_row(value, other)
            total = total + weight(3, level, part) * before
            total = total + weight(4, level, part) * after
            if level > 0:
                total = total + weight(5, level, part) * state[level - 1][part]
            if level < levels - 1:
                total = total + weight(6, level, part) * state[level + 1][part]
            result[level][part] = total
    return result


def diffuse_kernel(
    batch, meta, omega, wet, volume, below, above, edges, left, right, corner_below, corner_above,
    main_weights, strip_weights, *rest
):
    field_out, keep_out, send_out, cross_scratch, slot_scratch = rest[-5:]
    group, levels, rows, cols = omega.shape
    shape = (rows, cols)
    wet_cells = wet[...].astype(jnp.float32)
    root = jnp.sqrt(volume[...])
    half = levels // 2
    keeps_low = meta[2] == 0
    rims = rims_of_group(left, right, corner_below, corner_above)
    slot_edges = [None] * levels
    for level in range(levels):
        for pair in range(group // 2):
            two = slots(below[pair, level], above[pair, level])
            for i in range(2):
                slot_scratch[2 * pair + i, level] = two[i]
                slot_edges[level] = add_edge(slot_edges[level], two[i], 2 * pair + i)
    state = [[[None, None] for _ in range(levels)] for _ in range(2)]
    for level in range(levels):
        for part in range(2):
            edge = edges[0, level] if part == MAIN else slot_edges[level]
            pair = strips(edge, rims[level][part])
            for s in range(2):
                state[s][level][part] = pair[s]
    for sweep in range(ITERS):
        for level in range(levels):
            for part in range(2):
                cross_scratch[sweep, level, part] = crossing(state[0][level][part], state[1][level][part])
        if sweep < ITERS - 1:
            for s in range(2):
                state[s] = one_pass(
                    state[s], lambda n, level, part: strip_weights[s, n, level, part], (MAIN, SLOT), lambda level, part: None
                )

    for first in range(0, group, batch):
        fields = []
        for place in range(first, first + batch):
            fields.append([[omega[place, level] * wet_cells, slot_scratch[place, level]] for level in range(levels)])
        for sweep in range(ITERS):
            parts = (MAIN, SLOT) if sweep < ITERS - 1 else (MAIN,)
            for i in range(batch):
                fields[i] = one_pass(
                    fields[i],
                    lambda n, level, part: main_weights[n, level, part],
                    parts,
                    lambda level, part: rim_of(cross_scratch[sweep, level, part], first + i),
                )
        for i in range(batch):
            scaled = []
            for level in range(levels):
                value = fields[i][level][MAIN]
                field_out[first + i, level] = value
                scaled.append(value * root)
            for level in range(half):
                at = ((first + i) * half + level) * rows
                keep_out[at : at + rows, :] = jnp.where(keeps_low, scaled[level], scaled[half + level])
                send_out[at : at + rows, :] = jnp.where(keeps_low, scaled[half + level], scaled[level])


def gram_of_rows(slices, refs):
    groups = [ref.shape[0] // slices for ref in refs]
    order = sum(groups)
    exact = jnp.zeros((order, order), jnp.float32)
    cross = jnp.zeros((order, order), jnp.float32)
    for at in range(0, slices, 2):
        columns = []
        for i in range(2):
            picked = [ref[pl.ds(at + i, group, slices), :] for ref, group in zip(refs, groups)]
            columns.append(jnp.concatenate(picked, axis=0))
        values = jnp.concatenate(columns, axis=1)
        high = values.astype(jnp.bfloat16)
        rest = (values - high.astype(jnp.float32)).astype(jnp.bfloat16)
        dims = (((1,), (1,)), ((), ()))
        exact = exact + lax.dot_general(high, high, dims, preferred_element_type=jnp.float32)
        cross = cross + lax.dot_general(high, rest, dims, preferred_element_type=jnp.float32)
    return exact + (cross + cross.T)


def store_halves(meta, gram, mine, theirs):
    order = gram.shape[0]
    moved = turn(turn(gram, order // 2, 0), order // 2, 1)
    first, second = halves_of_gram(jnp.where(meta[2] == 0, gram, moved))
    is_first = meta[3] == 0
    mine[...] = jnp.where(is_first, first, second)
    theirs[...] = jnp.where(is_first, second, first)


def gram_kernel(chunks, slices, meta, *refs):
    store_halves(meta, gram_of_rows(slices, refs[:-2]), *refs[-2:])


def far_gram_kernel(slices, kept, received, out):
    out[...] = gram_of_rows(slices, (kept, received))


def near_gram_kernel(slices, meta, far, *refs):
    store_halves(meta, far[...] + gram_of_rows(slices, refs[:-2]), *refs[-2:])


def swapped(value, axis, bit):
    count = lax.axis_size(axis)
    return lax.ppermute(value, axis, [(source, source ^ bit) for source in range(count)])


def mesh_permute(value, mask):
    axes = ("tiles", "vec")
    count = lax.axis_size("tiles") * lax.axis_size("vec")
    return lax.ppermute(value, axes, [(source, source ^ mask) for source in range(count)])


def total_over_chips(value):
    vec = lax.axis_size("vec")
    masks = []
    bit = 1
    while bit < vec:
        masks.append(bit)
        bit *= 2
    bit = 2
    while bit < lax.axis_size("tiles"):
        masks.append(bit * vec)
        bit *= 2
    while masks:
        near, masks = (masks[:2], masks[2:])
        if len(near) == 1:
            value = value + mesh_permute(value, near[0])
        else:
            one, two, both = (mesh_permute(value, mask) for mask in (near[0], near[1], near[0] ^ near[1]))
            value = (value + one) + (two + both)
    return value


def fold(a, b):
    half = a.shape[1] // 2
    return jnp.where(ids(a.shape, 1) < half, a, b)


def flip(value):
    return turn(value, value.shape[1] // 2, 1)


def halves_of_gram(gram):
    q = gram.shape[0] // 8
    first = [fold(gram[: 2 * q], flip(gram[2 * q : 4 * q])), fold(flip(gram[:q]), gram[q : 2 * q])]
    second = [fold(flip(gram[4 * q : 6 * q]), gram[6 * q :]), fold(flip(gram[2 * q : 3 * q]), gram[3 * q : 4 * q])]
    return (jnp.concatenate(first, axis=0), jnp.concatenate(second, axis=0))


def gram_of_halves(first, second):
    q = first.shape[0] // 3
    return jnp.concatenate(
        [
            fold(first[:q], flip(first[2 * q :])),
            fold(first[q : 2 * q], first[2 * q :]),
            fold(flip(first[:q]), flip(second[2 * q :])),
            fold(flip(first[q : 2 * q]), second[2 * q :]),
            flip(second[: 2 * q]),
            second[: 2 * q],
        ],
        axis=0,
    )


def spread_lane(value, lane):
    return jnp.broadcast_to(value[:, lane : lane + 1], value.shape)


def squares(rows):
    high = rows.astype(jnp.bfloat16).astype(jnp.float32)
    rest = rows - high
    middle = rest.astype(jnp.bfloat16).astype(jnp.float32)
    low = rest - middle
    one = jnp.concatenate([high, high, middle, high, low, middle], axis=0).astype(jnp.bfloat16)
    two = jnp.concatenate([high, middle, high, low, high, middle], axis=0).astype(jnp.bfloat16)
    return lax.dot_general(one, two, (((0,), (0,)), ((), ())), preferred_element_type=jnp.float32)


def factor_kernel(scale, meta, own, other, out_ref):
    order = out_ref.shape[0]
    height = 8
    count = order // height
    shape = (height, order)
    is_first = meta[3] == 0
    mine, theirs = (own[...], other[...])
    gram = gram_of_halves(jnp.where(is_first, mine, theirs), jnp.where(is_first, theirs, mine)) * scale
    blocks = [gram[height * b : height * (b + 1), :] for b in range(count)]
    row_ids, col_ids = (ids(shape, 0), ids(shape, 1))
    previous = None
    for p in range(count):
        base = height * p
        rows = [jnp.broadcast_to(blocks[p][j : j + 1, :], shape) for j in range(height)]
        corner = {(i, j): spread_lane(rows[j], base + i) for j in range(height) for i in range(j, height)}
        if previous is not None:
            for done in previous:
                lanes = [spread_lane(done, base + j) for j in range(height)]
                for j in range(height):
                    rows[j] = rows[j] - lanes[j] * done
                    for i in range(j, height):
                        corner[i, j] = corner[i, j] - lanes[i] * lanes[j]
        panel = jnp.zeros(shape, jnp.float32)
        for s in range(height):
            inverse = lax.rsqrt(corner[s, s])
            rows[s] = rows[s] * inverse
            lanes = {j: corner[j, s] * inverse for j in range(s + 1, height)}
            for j in range(s + 1, height):
                for i in range(j, height):
                    corner[i, j] = corner[i, j] - lanes[i] * lanes[j]
                rows[j] = rows[j] - lanes[j] * rows[s]
            panel = jnp.where(row_ids == s, rows[s], panel)
        panel = jnp.where(col_ids >= base + row_ids, panel, 0.0)
        out_ref[base : base + height, :] = panel
        if p + 2 < count:
            update = squares(panel)
            for q in range(p + 2, count):
                blocks[q] = blocks[q] - update[height * q : height * (q + 1), :]
        previous = rows


def edge_kernel(runs, omega, conductance, wet, static_out, edge_out):
    levels, rows, cols = omega.shape[1:]
    shape = (rows, cols)
    row_ids, col_ids = (ids(shape, 0), ids(shape, 1))
    wet_cells = wet[...].astype(jnp.float32)
    open_x = (col_ids >= runs[0, 0]) & (col_ids < runs[0, 0] + runs[0, 1])
    open_y = (row_ids >= runs[0, 2]) & (row_ids < runs[0, 2] + runs[0, 3])
    keep_x = (row_ids > 0) | open_x
    keep_y = (col_ids > 0) | open_y
    group = cols // EDGE
    chunks = omega.shape[0] // group
    for level in range(levels):
        statics = [
            jnp.where(keep_x, conductance[0, level], 0.0),
            jnp.where(keep_y, conductance[1, level], 0.0),
            conductance[2, level] if level else jnp.zeros(shape, jnp.float32),
            wet_cells,
        ]
        edge = None
        for kind, value in enumerate(statics):
            static_out[kind, level] = value
            edge = add_edge(edge, value, kind)
        edge_out[chunks, level] = edge
        for chunk in range(chunks):
            edge = None
            for place in range(group):
                edge = add_edge(edge, omega[chunk * group + place, level] * wet_cells, place)
            edge_out[chunk, level] = edge


def face_kernel(first, meta, omega, wet, *row_outs):
    levels, rows, cols = omega.shape[1:]
    group = cols // EDGE
    is_first_row = meta[0] == 0
    wet_cells = wet[...].astype(jnp.float32)
    for chunk, out in enumerate(row_outs):
        for level in range(levels):
            for pair in range(group // 2):
                at = (first + chunk) * group + 2 * pair
                start = [omega[at + i, level] * wet_cells for i in range(2)]
                store_pair((out,), (pair, level), start[0], start[1], is_first_row)


def rim_kernel(meta, statics, left, right, out):
    is_first_row = meta[0] == 0
    groups, levels, rows, cols = left.shape
    kinds = statics.shape[0]
    take = left_lanes((rows, cols))
    for g in range(groups):
        for level in range(0, levels, 2):
            pair = [jnp.where(take, left[g, level + i], right[g, level + i]) for i in range(2)]
            store_pair((out,), g * levels // 2 + level // 2, pair[0], pair[1], is_first_row)
    first = groups * levels // 2
    for kind in range(0, kinds, 2):
        for level in range(levels):
            at = first + kind // 2 * levels + level
            store_pair((out,), at, statics[kind, level], statics[kind + 1, level], is_first_row)


def near_rows(is_first_row, a, b, halo):
    low = low_half(halo.shape)
    turned = turn(halo, ITERS, 0)
    result = []
    for own, across, moved in ((a, halo, turned), (b, turned, halo)):
        near = turn(own, ITERS, 0)
        result.append(jnp.where(low, jnp.where(is_first_row, near, across), jnp.where(is_first_row, moved, near)))
    return result


def spread_kind(strip, kind):
    cols = strip.shape[1]
    value = jnp.where(ids(strip.shape, 1) // EDGE == 0, turn(strip, -EDGE * kind, 1), 0.0)
    span = EDGE
    while span < cols:
        value = value + turn(value, span, 1)
        span *= 2
    return value


def store_weights(out, values, after_row, after_col):
    levels = len(values[0])
    for level in range(levels):
        cond_x, cond_y, cond_z, wet = (kind[level] for kind in values)
        below = values[2][level + 1] if level + 1 < levels else jnp.zeros_like(cond_z)
        faces = [cond_x, after_row(level), cond_y, after_col(level), cond_z, below]
        total = faces[0]
        for face in faces[1:]:
            total = total + face
        out[0, level] = wet * (1.0 - total)
        for index, face in enumerate(faces):
            out[index + 1, level] = wet * face


def plane_pass(state, weight, row_before, row_after, rim_at):
    levels = len(state)
    result = []
    for level in range(levels):
        value = state[level]
        rim = rim_at(level)
        before = turn(value, 1, 1) if rim is None else prev_col(value, rim)
        after = turn(value, -1, 1) if rim is None else next_col(value, rim)
        total = weight(0, level) * value
        total = total + weight(1, level) * row_before(value, level)
        total = total + weight(2, level) * row_after(value, level)
        total = total + weight(3, level) * before
        total = total + weight(4, level) * after
        if level > 0:
            total = total + weight(5, level) * state[level - 1]
        if level < levels - 1:
            total = total + weight(6, level) * state[level + 1]
        result.append(total)
    return result


def no_rim(level):
    return None


def pack_levels(values, use_first):
    pairs = []
    for level in range(0, len(values), 2):
        a, b = values[level : level + 2]
        pairs.append(jnp.where(use_first, first_pair(a, b), last_pair(a, b)))
    return pairs


def store_half(keep, send, place, pairs, keeps_low):
    rows = pairs[0].shape[0]
    half = len(pairs) // 2
    for i in range(half):
        at = (place * half + i) * rows
        keep[at : at + rows, :] = jnp.where(keeps_low, pairs[i], pairs[half + i])
        send[at : at + rows, :] = jnp.where(keeps_low, pairs[half + i], pairs[i])


def far_kernel(
    batch, meta, statics, omega, wet, volume, edges, left, right,
    final_out, bound_out, strip_bound_out, keep_out, send_out, weights, strip_weights, cross_scratch
):
    vectors, levels, rows, cols = omega.shape
    kinds = statics.shape[0]
    shape = (rows, cols)
    group = cols // EDGE
    chunks = vectors // group
    is_first_row = meta[0] == 0
    keeps_low = meta[2] == 0
    row_ids = ids(shape, 0)
    take = left_lanes(shape)
    wet_cells = wet[...].astype(jnp.float32)
    root = jnp.sqrt(volume[...])

    def sides(g, level):
        return strips(edges[g, level], jnp.where(take, left[g, level], right[g, level]))

    def roll_before(value, level):
        return turn(value, 1, 0)

    def roll_after(value, level):
        return turn(value, -1, 0)

    def closed_after(value):
        return jnp.where(row_ids == rows - 1, 0.0, turn(value, -1, 0))

    field = [[statics[kind, level] for level in range(levels)] for kind in range(kinds)]
    pairs = [sides(chunks, level) for level in range(levels)]
    crosses = [crossing(*pair) for pair in pairs]
    store_weights(
        weights, field, lambda level: closed_after(field[0][level]),
        lambda level: next_col(field[1][level], rim_of(crosses[level], 1)),
    )
    for s in range(2):
        side = [[spread_kind(pairs[level][s], kind) for level in range(levels)] for kind in range(kinds)]
        store_weights(
            strip_weights.at[s], side, lambda level: closed_after(side[0][level]), lambda level: turn(side[1][level], -1, 1)
        )

    def keep_bound(acc, value, sweep):
        edge = jnp.where(is_first_row, value, turn(value, -1, 0))
        moved = turn(edge, sweep - (ITERS - 1), 0)
        return moved if acc is None else jnp.where(row_ids == sweep, moved, acc)

    for g in range(chunks):
        state = [[sides(g, level)[s] for level in range(levels)] for s in range(2)]
        bounds = [[None] * levels for _ in range(2)]
        for sweep in range(ITERS):
            for level in range(levels):
                cross_scratch[g, sweep, level] = crossing(state[0][level], state[1][level])
                for s in range(2):
                    bounds[s][level] = keep_bound(bounds[s][level], state[s][level], sweep)
            if sweep < ITERS - 1:
                for s in range(2):
                    state[s] = plane_pass(
                        state[s], lambda n, level: strip_weights[s, n, level], roll_before, roll_after, no_rim
                    )
        for s in range(2):
            for level in range(levels):
                strip_bound_out[g, s, level] = bounds[s][level]

    for first in range(0, vectors, batch):
        g = first // group
        fields = [[omega[place, level] * wet_cells for level in range(levels)] for place in range(first, first + batch)]
        bounds = [[None] * levels for _ in range(batch)]
        for sweep in range(ITERS):
            for i in range(batch):
                for level in range(levels):
                    bounds[i][level] = keep_bound(bounds[i][level], fields[i][level], sweep)
                fields[i] = plane_pass(
                    fields[i], lambda n, level: weights[n, level], roll_before, roll_after,
                    lambda level: rim_of(cross_scratch[g, sweep, level], (first + i) % group),
                )
        for i in range(batch):
            for level in range(levels):
                final_out[first + i, level] = fields[i][level]
                bound_out[first + i, level] = bounds[i][level]
            scaled = [value * root for value in fields[i]]
            store_half(keep_out, send_out, first + i, pack_levels(scaled, is_first_row), keeps_low)


def near_weight_kernel(meta, statics, rims, edges, left, right, weights, strip_weights):
    kinds, levels, rows, cols = statics.shape
    shape = (rows, cols)
    is_first_row = meta[0] == 0
    take = left_lanes(shape)
    last = ids(shape, 0) == rows - 1
    g = edges.shape[0] - 1
    groups = edges.shape[0]
    first = groups * levels // 2
    field = [[None] * levels for _ in range(kinds)]
    for kind in range(0, kinds, 2):
        for level in range(levels):
            own = (statics[kind, level], statics[kind + 1, level])
            pair = near_rows(is_first_row, *own, rims[first + kind // 2 * levels + level])
            field[kind][level], field[kind + 1][level] = pair
    rim = [jnp.where(take, left[g, level], right[g, level]) for level in range(levels)]
    near_rim = []
    for level in range(0, levels, 2):
        near_rim += near_rows(is_first_row, rim[level], rim[level + 1], rims[g * levels // 2 + level // 2])
    near_edge = []
    for level in range(levels):
        edge = None
        for kind in range(kinds):
            edge = add_edge(edge, field[kind][level], kind)
        near_edge.append(edge)
    pairs = [strips(near_edge[level], near_rim[level]) for level in range(levels)]
    tile_pairs = [strips(edges[g, level], rim[level]) for level in range(levels)]
    crosses = [crossing(*pair) for pair in pairs]

    def with_next(value, tile_value):
        beyond = jnp.broadcast_to(tile_value[ITERS : ITERS + 1, :], shape)
        return jnp.where(last, beyond, turn(value, -1, 0))

    store_weights(
        weights, field, lambda level: with_next(field[0][level], statics[0, level]),
        lambda level: next_col(field[1][level], rim_of(crosses[level], 1)),
    )
    for s in range(2):
        side = [[spread_kind(pairs[level][s], kind) for level in range(levels)] for kind in range(kinds)]
        tile_side = [spread_kind(tile_pairs[level][s], 0) for level in range(levels)]
        store_weights(
            strip_weights.at[s], side, lambda level: with_next(side[0][level], tile_side[level]),
            lambda level: turn(side[1][level], -1, 1),
        )


def near_kernel(
    batch, base, parts, meta, omega, wet, volume, rims, left, right, weights, strip_weights, bound, strip_bound, final, *rest
):
    halos = rest[:parts]
    field_out, keep_out, send_out, cross_scratch, start, done, sems = rest[-7:]
    levels, rows, cols = omega.shape[1:]
    group = cols // EDGE
    offset = base * group
    shape = (rows, cols)
    is_first_row = meta[0] == 0
    keeps_low = meta[2] == 0
    row_ids = ids(shape, 0)
    take = left_lanes(shape)
    top = (row_ids == 0) & is_first_row
    bottom = (row_ids == rows - 1) & jnp.logical_not(is_first_row)
    is_near = low_half(shape) != is_first_row
    wet_cells = wet[...].astype(jnp.float32)
    root = jnp.sqrt(volume[...])

    def around(bound_at, sweep):
        def kept(level):
            return jnp.broadcast_to(bound_at(level)[sweep : sweep + 1, :], shape)

        return (
            lambda value, level: jnp.where(top, kept(level), turn(value, 1, 0)),
            lambda value, level: jnp.where(bottom, kept(level), turn(value, -1, 0)),
        )

    for part in range(parts):
        near_edge = [None] * levels
        for level in range(levels):
            for pair in range(group // 2):
                at = part * group + 2 * pair
                own = [omega[offset + at + i, level] * wet_cells for i in range(2)]
                two = near_rows(is_first_row, *own, halos[part][pair, level])
                for i in range(2):
                    start[at + i, level] = two[i]
                    near_edge[level] = add_edge(near_edge[level], two[i], 2 * pair + i)
        rim = [jnp.where(take, left[base + part, level], right[base + part, level]) for level in range(levels)]
        near_rim = []
        for level in range(0, levels, 2):
            across = rims[(base + part) * levels // 2 + level // 2]
            near_rim += near_rows(is_first_row, rim[level], rim[level + 1], across)
        pairs = [strips(near_edge[level], near_rim[level]) for level in range(levels)]
        state = [[pairs[level][s] for level in range(levels)] for s in range(2)]
        for sweep in range(ITERS):
            for level in range(levels):
                cross_scratch[part, sweep, level] = crossing(state[0][level], state[1][level])
            if sweep < ITERS - 1:
                for s in range(2):
                    state[s] = plane_pass(
                        state[s], lambda n, level: strip_weights[s, n, level],
                        *around(lambda level: strip_bound[base + part, s, level], sweep), no_rim,
                    )

    copies = []
    for first in range(0, parts * group, batch):
        part = first // group
        fields = [[start[place, level] for level in range(levels)] for place in range(first, first + batch)]
        for sweep in range(ITERS):
            for i in range(batch):
                fields[i] = plane_pass(
                    fields[i], lambda n, level: weights[n, level],
                    *around(lambda level: bound[offset + first + i, level], sweep),
                    lambda level: rim_of(cross_scratch[part, sweep, level], (first + i) % group),
                )
        for i in range(batch):
            scaled = []
            for level in range(levels):
                value = jnp.where(is_near, turn(fields[i][level], ITERS, 0), final[offset + first + i, level])
                done[first + i, level] = value
                scaled.append(value * root)
            store_half(keep_out, send_out, first + i, pack_levels(scaled, jnp.logical_not(is_first_row)), keeps_low)
        copies.append(
            pltpu.make_async_copy(
                done.at[pl.ds(first, batch)], field_out.at[pl.ds(offset + first, batch)], sems.at[first // batch]
            )
        )
        copies[-1].start()
    for copy in copies:
        copy.wait()


def shifted(value, axis, steps):
    count = lax.axis_size(axis)
    first, last = (max(0, -steps), min(count, count - steps))
    return lax.ppermute(value, axis, [(source, source + steps) for source in range(first, last)])


def beside(value, steps):
    count = lax.axis_size("tiles")
    pairs = [(source, source + steps) for source in range(count)]
    return lax.ppermute(value, "tiles", [(a, b) for a, b in pairs if 0 <= b < count and a // TGY == b // TGY])


def after(values, *done):
    return lax.optimization_barrier((values, done))[0]


def exchange_rows(messages, grid_rows):
    if len(messages) == 1:
        received = swapped(messages[0], "tiles", TGY)
        return (received, received)
    return (shifted(messages[0], "tiles", -TGY), shifted(messages[1], "tiles", TGY))


def f32(*shape):
    return jax.ShapeDtypeStruct(shape, jnp.float32)


def block(shape, *at):
    return pl.BlockSpec(shape, lambda i: at)


def call(kernel, in_specs, out_specs, out_shape, flops=0, scratch=(), aliases=None, limit=VMEM_LIMIT, grid=(1,)):
    return pl.pallas_call(
        kernel,
        grid=grid,
        in_specs=in_specs,
        out_specs=out_specs,
        out_shape=out_shape,
        scratch_shapes=scratch,
        input_output_aliases=aliases or {},
        compiler_params=pltpu.CompilerParams(vmem_limit_bytes=limit),
        cost_estimate=pl.CostEstimate(flops=flops, bytes_accessed=1 << 20, transcendentals=0),
    )


def resident(count):
    return [pl.BlockSpec(memory_space=pltpu.VMEM)] * count


def whole(array):
    zeros = (0,) * array.ndim
    return pl.BlockSpec(array.shape, lambda i: zeros)


def factor(meta, mine, theirs, order, scale):
    mine = total_over_chips(mine + swapped(theirs, "tiles", 1))
    smem = pl.BlockSpec(memory_space=pltpu.SMEM)
    return call(
        functools.partial(factor_kernel, scale),
        [smem] + resident(2),
        resident(1)[0],
        f32(order, order),
        grid=(),
    )(meta, mine, swapped(mine, "tiles", 1))


def shards_any(omega, conductance, wet, volume, face_runs):
    vectors, levels, rows, cols = omega.shape
    tiles = lax.axis_size("tiles")
    grid_rows = tiles // TGY
    tile_row = lax.axis_index("tiles") // TGY
    core = lax.axis_index("tiles") % 2
    meta = jnp.stack([tile_row, grid_rows - 1 - tile_row, lax.axis_index("vec"), core]).astype(jnp.int32)
    smem = pl.BlockSpec(memory_space=pltpu.SMEM)
    group = cols // EDGE
    chunks = vectors // group
    directions = 1 if grid_rows == 2 else 2
    kinds = 4
    half = levels // 2

    row_shapes = [f32(group // 2 + (kinds // 2 if c == 0 else 0), levels, rows, cols) for c in range(chunks)]
    row_shapes = [shape for shape in row_shapes for _ in range(directions)]
    packed_shapes = [f32(kinds, levels, rows, cols), f32(chunks + 1, levels, rows, cols)] + row_shapes
    statics, edges, *messages = call(
        functools.partial(pack_kernel, chunks),
        [smem, smem, whole(omega), whole(conductance), whole(wet)],
        [whole(s) for s in packed_shapes],
        packed_shapes,
    )(meta, face_runs, omega, conductance, wet)
    messages = [messages[directions * c : directions * (c + 1)] for c in range(chunks)]
    received = [exchange_rows(messages[0], grid_rows)]
    left = beside(edges, 1)
    right = beside(edges, -1)
    corner_shapes = [f32(chunks + 1, levels // 2, rows, cols)] * directions
    corners = call(
        corner_kernel, [smem, whole(left), whole(right)], [whole(s) for s in corner_shapes], corner_shapes
    )(meta, left, right)
    corners = exchange_rows(corners, grid_rows)
    gates = [(left, right), corners]
    for c in range(1, chunks):
        gate = gates[c - 1] if c <= 2 else received[c - 2]
        received.append(exchange_rows(after(messages[c], *gate), grid_rows))

    def group_specs(c):
        edge = block((1, levels, rows, cols), c, 0, 0, 0)
        corner = block((1, levels // 2, rows, cols), c, 0, 0, 0)
        return [edge, edge, edge, corner, corner]

    around = (edges, left, right, *corners)
    weight_shapes = [f32(7, levels, 2, rows, cols), f32(2, 7, levels, 2, rows, cols)]
    main_weights, strip_weights = call(
        weight_kernel,
        [smem, whole(statics), whole(received[0][0]), whole(received[0][1])] + group_specs(chunks),
        [whole(s) for s in weight_shapes],
        weight_shapes,
    )(meta, statics, *received[0], *around)

    field = None
    kept, sent = ([], [])
    half_shape = f32(group * half * rows, cols)
    for c in range(chunks):
        rims = after(received[c], sent[c - 2]) if c >= 2 else received[c]
        operands = [meta, omega, wet, volume, *rims, *around, main_weights, strip_weights]
        row_block = block((group // 2, levels, rows, cols), 0, 0, 0, 0)
        chunk_block = block((group, levels, rows, cols), c, 0, 0, 0)
        specs = [smem, chunk_block, whole(wet), whole(volume), row_block, row_block] + group_specs(c)
        specs += [whole(main_weights), whole(strip_weights)]
        aliases = {}
        if field is not None:
            aliases = {len(operands): 0}
            operands.append(field)
            specs.append(pl.BlockSpec(memory_space=pl.ANY))
        field, keep, send = call(
            functools.partial(diffuse_kernel, 4),
            specs,
            [chunk_block, whole(half_shape), whole(half_shape)],
            [f32(*omega.shape), half_shape, half_shape],
            flops=4 * 10**9,
            scratch=[pltpu.VMEM((ITERS, levels, 2, rows, cols), jnp.float32), pltpu.VMEM((group, levels, rows, cols), jnp.float32)],
            aliases=aliases,
        )(*operands)
        kept.append(keep)
        sent.append(swapped(send, "vec", 1))

    order = 2 * vectors
    half_gram = f32(3 * order // 8, order)
    mine, theirs = call(
        functools.partial(gram_kernel, chunks, half * rows),
        [smem] + [whole(half_shape)] * (2 * chunks),
        [whole(half_gram)] * 2,
        [half_gram] * 2,
    )(meta, *kept, *sent)
    r_factor = factor(meta, mine, theirs, order, 1.0 / (levels * tiles * rows * cols))
    return (field, r_factor)


def shards_of_two_rows(omega, conductance, wet, volume, face_runs):
    vectors, levels, rows, cols = omega.shape
    tiles = lax.axis_size("tiles")
    tile_row = lax.axis_index("tiles") // TGY
    core = lax.axis_index("tiles") % 2
    meta = jnp.stack([tile_row, 1 - tile_row, lax.axis_index("vec"), core]).astype(jnp.int32)
    smem = pl.BlockSpec(memory_space=pltpu.SMEM)
    group = cols // EDGE
    chunks = vectors // group
    kinds = 4
    half = levels // 4
    plane = (rows, cols)

    def vmem(*lead):
        return pltpu.VMEM(lead + plane, jnp.float32)

    row_shape = f32(group // 2, levels, *plane)
    chunk0 = call(
        functools.partial(face_kernel, 0),
        [smem, block((group, levels, *plane), 0, 0, 0, 0), whole(wet)],
        [whole(row_shape)],
        [row_shape],
        limit=EDGE_LIMIT,
    )(meta, omega, wet)
    edge_shapes = [f32(kinds, levels, *plane), f32(chunks + 1, levels, *plane)]
    statics, edges = call(
        edge_kernel,
        [smem, whole(omega), whole(conductance), whole(wet)],
        [whole(s) for s in edge_shapes],
        edge_shapes,
        limit=EDGE_LIMIT,
    )(after(face_runs, chunk0), omega, conductance, wet)
    left = beside(edges, 1)
    right = beside(edges, -1)
    row_shapes = [row_shape] * (chunks - 1)
    messages = chunk0 + call(
        functools.partial(face_kernel, 1),
        [smem] + resident(2),
        resident(len(row_shapes)),
        row_shapes,
        flops=10**9,
        grid=(),
    )(meta, omega, wet)
    halos = [swapped(messages[0], "tiles", TGY)]
    rim_shape = f32((chunks + 1) * levels // 2 + kinds // 2 * levels, *plane)
    rims = call(rim_kernel, [smem] + resident(3), resident(1)[0], rim_shape, grid=())(
        meta, statics, left, right
    )
    rims = swapped(rims, "tiles", TGY)
    gates = [(), (halos[0], rims)]
    for c in range(1, min(chunks, 3)):
        halos.append(swapped(after(messages[c], gates[c - 1]), "tiles", TGY))

    far_shape = f32(vectors * half * rows, cols)
    far_shapes = [f32(*omega.shape), f32(*omega.shape), f32(chunks, 2, levels, *plane), far_shape, far_shape]
    final, bound, strip_bound, far_kept, far_sent = call(
        functools.partial(far_kernel, 8),
        [smem] + resident(7),
        resident(len(far_shapes)),
        far_shapes,
        grid=(),
        flops=8 * 10**9,
        scratch=[vmem(7, levels), vmem(2, 7, levels), vmem(chunks, ITERS, levels)],
    )(meta, statics, omega, wet, volume, edges, left, right)
    far_received = swapped(far_sent, "vec", 1)

    weight_shapes = [f32(7, levels, *plane), f32(2, 7, levels, *plane)]
    weights, strip_weights = call(
        near_weight_kernel,
        [smem] + resident(5),
        resident(2),
        weight_shapes,
        grid=(),
    )(meta, statics, rims, edges, left, right)

    field = None
    kept, sent = ([], [])
    steps = [(0, 2)] + [(c, 1) for c in range(2, chunks)]
    for base, parts in steps:
        waits = [(), (far_received,)]
        mine = after(halos[base : base + parts], *(waits[len(sent)] if len(sent) < 2 else ()))
        operands = [meta, omega, wet, volume, rims, left, right, weights, strip_weights, bound, strip_bound, final, *mine]
        specs = [smem] + resident(len(operands) - 1)
        aliases = {}
        if field is not None:
            aliases = {len(operands): 0}
            operands.append(field)
            specs.append(pl.BlockSpec(memory_space=pl.ANY))
        near_shape = f32(parts * group * half * rows, cols)
        batch = 8
        count = parts * group
        field, keep, send = call(
            functools.partial(near_kernel, batch, base, parts),
            specs,
            [pl.BlockSpec(memory_space=pl.ANY)] + resident(2),
            [f32(*omega.shape), near_shape, near_shape],
            flops=2 * 10**9,
            scratch=[
                vmem(parts, ITERS, levels), vmem(count, levels), vmem(count, levels),
                pltpu.SemaphoreType.DMA((count // batch,)),
            ],
            aliases=aliases,
            grid=(),
        )(*operands)
        kept.append(keep)
        sent.append(swapped(send, "vec", 1))
        if len(halos) < chunks:
            halos.append(swapped(after(messages[len(halos)], keep), "tiles", TGY))

    order = 2 * vectors
    gram_shape = f32(order, order)
    far_gram = call(
        functools.partial(far_gram_kernel, half * rows), resident(2), resident(1)[0], gram_shape, grid=()
    )(far_kept, far_received)
    half_gram = f32(3 * order // 8, order)
    mine, theirs = call(
        functools.partial(near_gram_kernel, half * rows),
        [smem] + resident(1 + len(kept + sent)),
        resident(2),
        [half_gram] * 2,
        grid=(),
    )(meta, far_gram, *kept, *sent)
    r_factor = factor(meta, mine, theirs, order, 1.0 / (levels * tiles * rows * cols))
    return (field, r_factor)


def solution(mesh):
    shards = shards_of_two_rows if mesh.shape["tiles"] == 2 * TGY else shards_any
    in_specs = (
        P("vec", None, "tiles", None),
        P(None, None, "tiles", None),
        P("tiles", None),
        P("tiles", None),
        P("tiles", None),
    )
    out_specs = (P("vec", None, "tiles", None), P())
    return jax.shard_map(shards, mesh=mesh, in_specs=in_specs, out_specs=out_specs, check_vma=False)
```
